32 devices in a mesh: pipe: 2 (over core), dp: 16 (over z, y, x).
Axes of the slice: x: 2, y: 2, z: 4, core: 2. Of those that a mesh axis runs over, the one named last changes fastest.
Arguments:
- tokens: bfloat16 [2, 16, 512, 384], P(None, 'dp'), may hold values from -6 to 6
- prompts: bfloat16 [2, 16, 512, 384], P(None, 'dp'), may hold values from -6 to 6
- cotangent: bfloat16 [2, 16, 512, 384], P(None, 'dp'), may hold values from -6 to 6
- segments: int32 [2, 16, 512], P(None, 'dp'), may hold values from 0 to 7, never falling along the last dimension, each value on 1 to 256 neighbouring positions
- weight_in: float32 [2, 384, 1152], P('pipe', 'dp')
- weight_out: float32 [2, 384, 384], P('pipe', 'dp')
- weight_up: float32 [2, 384, 1536], P('pipe', 'dp')
- weight_down: float32 [2, 1536, 384], P('pipe', 'dp')
- first_in: float32 [2, 384, 1152], P('pipe', 'dp')
- first_out: float32 [2, 384, 384], P('pipe', 'dp')
- first_up: float32 [2, 384, 1536], P('pipe', 'dp')
- first_down: float32 [2, 1536, 384], P('pipe', 'dp')
- second_in: float32 [2, 384, 1152], P('pipe', 'dp'), as said below
- second_out: float32 [2, 384, 384], P('pipe', 'dp'), as said below
- second_up: float32 [2, 384, 1536], P('pipe', 'dp'), as said below
- second_down: float32 [2, 1536, 384], P('pipe', 'dp'), as said below
- gains: float32 [2, 2, 384], P('pipe'), as said below
- gain_first: float32 [2, 2, 384], P('pipe')
- gain_second: float32 [2, 2, 384], P('pipe'), as said below
Outputs:
- section_result: float32 [2, 2, 16, 512, 384], P('pipe', None, 'dp')
- drift_in: float32 [2, 384, 1152], P('pipe', 'dp')
- drift_out: float32 [2, 384, 384], P('pipe', 'dp')
- drift_up: float32 [2, 384, 1536], P('pipe', 'dp')
- drift_down: float32 [2, 1536, 384], P('pipe', 'dp')
- spread_in: float32 [2, 384, 1152], P('pipe', 'dp')
- spread_out: float32 [2, 384, 384], P('pipe', 'dp')
- spread_up: float32 [2, 384, 1536], P('pipe', 'dp')
- spread_down: float32 [2, 1536, 384], P('pipe', 'dp')
- updated_in: float32 [2, 384, 1152], P('pipe', 'dp')
- updated_out: float32 [2, 384, 384], P('pipe', 'dp')
- updated_up: float32 [2, 384, 1536], P('pipe', 'dp')
- updated_down: float32 [2, 1536, 384], P('pipe', 'dp')
- copied_in: bfloat16 [2, 384, 1152], P('pipe', 'dp')
- copied_out: bfloat16 [2, 384, 384], P('pipe', 'dp')
- copied_up: bfloat16 [2, 384, 1536], P('pipe', 'dp')
- copied_down: bfloat16 [2, 1536, 384], P('pipe', 'dp')
- gain_drift: float32 [2, 2, 384], P('pipe')
- gain_spread: float32 [2, 2, 384], P('pipe')
- gain_updated: float32 [2, 2, 384], P('pipe')
- norm_pairs: float32 [2, 6, 2], P('pipe')
The draws below stay inside these ranges and needn't reach their ends.
Inputs may be any that keep to these rules, and one draw needn't show every extreme that they name: `segments`: segment numbers never fall along a sequence; each segment holds 1 to 256 rows. `second_in`: positive. `second_out`: positive. `second_up`: positive. `second_down`: positive. `gain_second`: positive. `gains`: positive.
All inputs are finite; a program needn't handle non-finite values.
Results may differ from the reference program's by a relative error of at most 0.025.
The reference program's roundings to bfloat16 on the way count: a program that leaves them out, or rounds other values in their place, can miss the bound.
Values may be sent and summed in bfloat16 or wider, within the bound.
No kernel may reach another device: no remote copies, remote signals or barrier semaphores. Data moves between devices by JAX's collectives and lax.ppermute only.
A program may use at most 128 MiB of HBM per device.

```python
import math
import jax
import jax.numpy as jnp
import numpy as np
from jax import lax

D = 384
FF = 1536
HEADS = 6
HEAD_DIM = 64
SEQ_LEN = 512
MICRO = 2
STEP = 3
SEQS = 16
TOKENS = 16384


def ramp(count, ratio):
    steps = jnp.arange(count, dtype=jnp.float32) / (count - 1)
    return (1.0 + (ratio - 1.0) * steps) * (2.0 / (1.0 + ratio))


def matrix_draw(key, row_count, col_count, fan_in, ratio):
    normal = jax.random.normal(key, (2, row_count, col_count), jnp.float32)
    return normal * fan_in ** (-0.5) * ramp(row_count, ratio)[None, :, None]


def first_draw(key, row_count, col_count, ratio):
    normal = jax.random.normal(key, (2, row_count, col_count), jnp.float32)
    return normal * TOKENS ** 0.5 * ramp(row_count, ratio)[None, :, None]


def second_draw(key, row_count, col_count, ratio):
    factor = jax.random.uniform(key, (2, row_count, col_count), jnp.float32, 1.0, 4.0)
    return factor * TOKENS / ramp(row_count, ratio)[None, :, None]


def draw_weight_in(key, part):
    key = jax.random.fold_in(key, 11)
    ratio = 3.0
    return matrix_draw(key, D, 3 * D, D, ratio)


def draw_weight_out(key, part):
    key = jax.random.fold_in(key, 12)
    ratio = 3.0
    return matrix_draw(key, D, D, D / 8.0, ratio)


def draw_weight_up(key, part):
    key = jax.random.fold_in(key, 13)
    ratio = 3.0
    return matrix_draw(key, D, FF, D, ratio)


def draw_weight_down(key, part):
    key = jax.random.fold_in(key, 14)
    ratio = 3.0
    return matrix_draw(key, FF, D, FF, ratio)


def draw_first_in(key, part):
    key = jax.random.fold_in(key, 21)
    ratio = 3.0
    return first_draw(key, D, 3 * D, ratio)


def draw_first_out(key, part):
    key = jax.random.fold_in(key, 22)
    ratio = 3.0
    return first_draw(key, D, D, ratio)


def draw_first_up(key, part):
    key = jax.random.fold_in(key, 23)
    ratio = 3.0
    return first_draw(key, D, FF, ratio)


def draw_first_down(key, part):
    key = jax.random.fold_in(key, 24)
    ratio = 3.0
    return first_draw(key, FF, D, ratio)


def draw_second_in(key, part):
    key = jax.random.fold_in(key, 31)
    ratio = 3.0
    return second_draw(key, D, 3 * D, ratio)


def draw_second_out(key, part):
    key = jax.random.fold_in(key, 32)
    ratio = 3.0
    return second_draw(key, D, D, ratio)


def draw_second_up(key, part):
    key = jax.random.fold_in(key, 33)
    ratio = 3.0
    return second_draw(key, D, FF, ratio)


def draw_second_down(key, part):
    key = jax.random.fold_in(key, 34)
    ratio = 3.0
    return second_draw(key, FF, D, ratio)


def draw_gains(key, part):
    key = jax.random.fold_in(key, 41)
    ratio = 3.0
    factor = jax.random.uniform(key, (2, 2, D), jnp.float32, 0.8, 1.2)
    return factor * ramp(D, ratio)[None, None, :]


def draw_gain_first(key, part):
    key = jax.random.fold_in(key, 42)
    return jax.random.normal(key, (2, 2, D), jnp.float32) * TOKENS ** 0.5


def draw_gain_second(key, part):
    key = jax.random.fold_in(key, 43)
    return jax.random.uniform(key, (2, 2, D), jnp.float32, 1.0, 4.0) * TOKENS


def block_scale(rng, dims, pieces, smallest, high):
    loudness, own = 1.0, jax.random.fold_in(rng, 6)
    for dim, shards_of in pieces:
        steps = jnp.exp(jax.random.uniform(jax.random.fold_in(own, dim), (shards_of,), jnp.float32, smallest / len(pieces), high / len(pieces)))
        loudness = loudness * jnp.repeat(steps, dims[dim] // shards_of).reshape([-1 if axis == dim else 1 for axis in range(len(dims))])
    return loudness


def profile(number_of, total, bound, skew):
    portions = [(1 << 20) // math.isqrt(standing ** skew) + 1 for standing in range(2, number_of + 1)]
    spare, given = total - bound - (number_of - 1), [1] * (number_of - 1)
    while spare > 0:
        movable = [i for i in range(number_of - 1) if given[i] < bound]
        whole, budget = sum([portions[i] for i in movable]), spare
        for i in movable:
            more = min(bound - given[i], max(1, budget * portions[i] // whole), spare)
            given[i] = given[i] + more
            spare = spare - more
    return np.array([bound] + given)


def uneven(key, amount, total, reach, slope):
    if amount == 2:
        one = jax.random.randint(key, (), max(1, total - reach), min(reach, total - 1) + 1)
        return jnp.stack([one, total - one])
    sizes = jnp.asarray(profile(amount, total, reach, slope), jnp.int32)
    pairs = (amount - 1) // 2
    source_of, taker = sizes[1:1 + 2 * pairs:2], sizes[2:2 + 2 * pairs:2]
    room = jnp.minimum(source_of - 1, reach - taker)
    shifted = jax.random.randint(jax.random.fold_in(key, 1), (pairs,), 0, 1 << 20) % (room + 1)
    sizes = sizes.at[1:1 + 2 * pairs:2].set(source_of - shifted).at[2:2 + 2 * pairs:2].set(taker + shifted)
    return sizes[jax.random.permutation(jax.random.fold_in(key, 2), amount)]


def gaussian(stream_key, extent, width, bound, pieces=(), held_as=jnp.bfloat16):
    array = width * jax.random.normal(stream_key, extent, jnp.float32)
    if pieces:
        array = array * block_scale(stream_key, extent, pieces, -0.22, 0.18)
    return jnp.clip(array, -bound, bound).astype(held_as)


def setup_inputs(seed: int = 0) -> dict:
    streams_of = jax.random.split(jax.random.key(seed), 20)
    tokens = gaussian(streams_of[0], (MICRO, SEQS, SEQ_LEN, D), 1.0, 6.0, ((1, 16),))
    prompts = gaussian(streams_of[1], (MICRO, SEQS, SEQ_LEN, D), 1.0, 6.0, ((1, 16),))
    cotangent = gaussian(streams_of[2], (MICRO, SEQS, SEQ_LEN, D), 1.0, 6.0, ((1, 16),))
    segments = jax.vmap(lambda own: jnp.searchsorted(jnp.cumsum(uneven(own, max(3, SEQ_LEN // 64), SEQ_LEN, SEQ_LEN // 2, 0)), jnp.arange(SEQ_LEN), side="right"))(jax.random.split(streams_of[3], MICRO * SEQS)).reshape((MICRO, SEQS, SEQ_LEN)).astype(jnp.int32)
    weight_in = draw_weight_in(jax.random.fold_in(streams_of[19], 71), 0)
    weight_out = draw_weight_out(jax.random.fold_in(streams_of[19], 71), 0)
    weight_up = draw_weight_up(jax.random.fold_in(streams_of[19], 71), 0)
    weight_down = draw_weight_down(jax.random.fold_in(streams_of[19], 71), 0)
    first_in = draw_first_in(jax.random.fold_in(streams_of[19], 71), 0)
    first_out = draw_first_out(jax.random.fold_in(streams_of[19], 71), 0)
    first_up = draw_first_up(jax.random.fold_in(streams_of[19], 71), 0)
    first_down = draw_first_down(jax.random.fold_in(streams_of[19], 71), 0)
    second_in = draw_second_in(jax.random.fold_in(streams_of[19], 71), 0)
    second_out = draw_second_out(jax.random.fold_in(streams_of[19], 71), 0)
    second_up = draw_second_up(jax.random.fold_in(streams_of[19], 71), 0)
    second_down = draw_second_down(jax.random.fold_in(streams_of[19], 71), 0)
    gains = draw_gains(jax.random.fold_in(streams_of[19], 71), 0)
    gain_first = draw_gain_first(jax.random.fold_in(streams_of[19], 71), 0)
    gain_second = draw_gain_second(jax.random.fold_in(streams_of[19], 71), 0)
    return {"tokens": tokens, "prompts": prompts, "cotangent": cotangent, "segments": segments, "weight_in": weight_in, "weight_out": weight_out, "weight_up": weight_up, "weight_down": weight_down, "first_in": first_in, "first_out": first_out, "first_up": first_up, "first_down": first_down, "second_in": second_in, "second_out": second_out, "second_up": second_up, "second_down": second_down, "gains": gains, "gain_first": gain_first, "gain_second": gain_second}


@jax.custom_vjp
def low(v):
    return lax.optimization_barrier(v.astype(jnp.bfloat16)).astype(jnp.float32)

@jax.custom_vjp
def low_back(v):
    return v

def low_keep(v):
    return (low(v), None)

def low_pass(kept, grad):
    return (grad,)

def back_keep(v):
    return (v, None)

def back_low(kept, grad):
    return (low(grad),)
low.defvjp(low_keep, low_pass)
low_back.defvjp(back_keep, back_low)
highest = lax.Precision.HIGHEST
rate = 0.3
beta = 0.5
eps_adam = 1e-06
decay = 0.01
eps_norm = 1e-05
neg_large = -1e+30

def layer_norm(inputs, gain):
    average = lax.optimization_barrier(jnp.mean(inputs, axis=-1, keepdims=True))
    centered = inputs - average
    variance = lax.optimization_barrier(jnp.mean(centered * centered, axis=-1, keepdims=True))
    return centered * lax.rsqrt(variance + eps_norm) * gain

def attention(packed, segment_row):
    length = packed.shape[0]
    queries = packed[:, :D].reshape(length, HEADS, HEAD_DIM)
    key_rows = packed[:, D:2 * D].reshape(length, HEADS, HEAD_DIM)
    value_rows = packed[:, 2 * D:].reshape(length, HEADS, HEAD_DIM)
    products = jnp.einsum('qhd,khd->hqk', queries, key_rows, precision=highest)
    scores = low_back(products * HEAD_DIM ** (-0.5))
    position = jnp.arange(length)
    allowed = (segment_row[:, None] == segment_row[None, :]) & (position[None, :] <= position[:, None])
    scores = jnp.where(allowed[None], scores, neg_large)
    largest = lax.optimization_barrier(jnp.max(scores, axis=-1, keepdims=True))
    lifted = jnp.exp(scores - largest)
    chances = lifted / lax.optimization_barrier(jnp.sum(lifted, axis=-1, keepdims=True))
    attended = jnp.einsum('hqk,khd->qhd', low(chances), value_rows, precision=highest)
    return attended.reshape(length, D)

def block(inputs, segment_row, matrix_in, matrix_out, matrix_up, matrix_down, gain_one, gain_two):
    normed = low(layer_norm(inputs, gain_one))
    packed = low_back(low(jnp.dot(normed, matrix_in, precision=highest)))
    attended = low_back(low(jax.checkpoint(attention)(packed, segment_row)))
    branch = low_back(jnp.dot(attended, matrix_out, precision=highest))
    middle = inputs + branch
    normed_two = low(layer_norm(middle, gain_two))
    hidden = low_back(jnp.dot(normed_two, matrix_up, precision=highest))
    active = low(jax.nn.gelu(hidden))
    return middle + low_back(jnp.dot(active, matrix_down, precision=highest))

def two_blocks(token_row, prompt_row, segment_row, masters):
    matrix_in, matrix_out, matrix_up, matrix_down, gain_set = masters
    first_result = block(token_row, segment_row, low(matrix_in[0]), low(matrix_out[0]), low(matrix_up[0]), low(matrix_down[0]), gain_set[0, 0], gain_set[0, 1])
    second_input = low_back(low(first_result)) + prompt_row
    return block(second_input, segment_row, low(matrix_in[1]), low(matrix_out[1]), low(matrix_up[1]), low(matrix_down[1]), gain_set[1, 0], gain_set[1, 1])

def moments(master, grad, first, second):
    drift = beta * first + (1.0 - beta) * grad
    spread = beta * second + (1.0 - beta) * grad * grad
    correction = 1.0 - beta ** STEP
    update = drift / correction / (jnp.sqrt(spread / correction) + eps_adam) + decay * master
    return (drift, spread, update)

def reference(tokens, prompts, cotangent, segments, weight_in, weight_out, weight_up, weight_down, first_in, first_out, first_up, first_down, second_in, second_out, second_up, second_down, gains, gain_first, gain_second):
    count = MICRO * SEQS
    token_rows = tokens.astype(jnp.float32).reshape(count, SEQ_LEN, D)
    prompt_rows = prompts.astype(jnp.float32).reshape(count, SEQ_LEN, D)
    cotangent_rows = cotangent.astype(jnp.float32).reshape(count, SEQ_LEN, D)
    segment_rows = segments.reshape(count, SEQ_LEN)
    masters = (weight_in, weight_out, weight_up, weight_down, gains)

    def one_sequence(carry, item):
        token_row, prompt_row, cotangent_row, segment_row = item

        def forward(token_value, *params):
            return two_blocks(token_value, prompt_row, segment_row, params)
        output, pull = jax.vjp(forward, token_row, *masters)
        grads = pull(cotangent_row)
        summed = tuple((total + grad for total, grad in zip(carry, grads[1:])))
        return (summed, (grads[0], output))
    start = tuple((jnp.zeros(master.shape, jnp.float32) for master in masters))
    summed, (input_grads, outputs) = lax.scan(one_sequence, start, (token_rows, prompt_rows, cotangent_rows, segment_rows))
    section_result = jnp.stack([input_grads.reshape(MICRO, SEQS, SEQ_LEN, D), outputs.reshape(MICRO, SEQS, SEQ_LEN, D)])
    firsts = (first_in, first_out, first_up, first_down)
    seconds = (second_in, second_out, second_up, second_down)
    drifts = []
    spreads = []
    updated = []
    weight_norms = []
    update_norms = []
    for member in range(4):
        drift, spread, update = moments(masters[member], summed[member], firsts[member], seconds[member])
        weight_norm = jnp.sqrt(lax.optimization_barrier(jnp.sum(masters[member] * masters[member], axis=(1, 2))))
        update_norm = jnp.sqrt(lax.optimization_barrier(jnp.sum(update * update, axis=(1, 2))))
        updated.append(masters[member] - rate * (weight_norm / update_norm)[:, None, None] * update)
        drifts.append(drift)
        spreads.append(spread)
        weight_norms.append(weight_norm)
        update_norms.append(update_norm)
    gain_drift, gain_spread, gain_update = moments(gains, summed[4], gain_first, gain_second)
    gain_weight = jnp.sqrt(lax.optimization_barrier(jnp.sum(gains * gains, axis=-1)))
    gain_step = jnp.sqrt(lax.optimization_barrier(jnp.sum(gain_update * gain_update, axis=-1)))
    gain_updated = gains - rate * (gain_weight / gain_step)[:, :, None] * gain_update
    weight_column = jnp.concatenate([jnp.stack(weight_norms, axis=1), gain_weight], axis=1)
    update_column = jnp.concatenate([jnp.stack(update_norms, axis=1), gain_step], axis=1)
    norm_pairs = jnp.stack([weight_column, update_column], axis=-1)
    return (section_result, drifts[0], drifts[1], drifts[2], drifts[3], spreads[0], spreads[1], spreads[2], spreads[3], updated[0], updated[1], updated[2], updated[3], updated[0].astype(jnp.bfloat16), updated[1].astype(jnp.bfloat16), updated[2].astype(jnp.bfloat16), updated[3].astype(jnp.bfloat16), gain_drift, gain_spread, gain_updated, norm_pairs)
```

```python
import jax
import jax.numpy as jnp
from jax import lax
from jax.experimental import pallas as pl
from jax.experimental.pallas import tpu as pltpu
from jax.sharding import PartitionSpec as P

D = 384
FF = 1536
HEADS = 6
HEAD_DIM = 64
STEP = 3
BF = jnp.bfloat16
F32 = jnp.float32

rate = 0.3
beta = 0.5
eps_adam = 1e-06
decay = 0.01
eps_norm = 1e-05
neg_large = -1e30

QB = 128
REACH = 256
ROWS = 64
CHUNK = 256
WIDE = 4 * D
VM = pl.BlockSpec(memory_space=pltpu.VMEM)
SM = pl.BlockSpec(memory_space=pltpu.SMEM)
ANY = pl.BlockSpec(memory_space=pl.ANY)
struct = jax.ShapeDtypeStruct


def dot(a, b, ca=1, cb=0):
    return lax.dot_general(a, b, (((ca,), (cb,)), ((), ())), preferred_element_type=F32)


def bands(length):
    out = []
    off = 0
    for b in range(length // QB):
        ks, ke = max(0, QB * b - REACH), QB * (b + 1)
        out.append((b, ks, ke, off))
        off += ke - ks
    return out, off


def unit_of(x):
    mean = jnp.sum(x, axis=-1, keepdims=True) * (1.0 / D)
    centered = x - mean
    variance = jnp.sum(centered * centered, axis=-1, keepdims=True) * (1.0 / D)
    inverse = lax.rsqrt(variance + eps_norm)
    return centered * inverse, inverse


def norm_into(x_ref, gain, n_ref):
    for r in range(0, x_ref.shape[0], ROWS):
        unit, _ = unit_of(x_ref[r : r + ROWS, :].astype(F32))
        n_ref[r : r + ROWS, :] = (unit * gain).astype(BF)


def norm_back(dn_ref, x_ref, dy_ref, gain, out_ref, low_ref):
    grad = jnp.zeros((1, D), F32)
    for r in range(0, x_ref.shape[0], ROWS):
        unit, inverse = unit_of(x_ref[r : r + ROWS, :].astype(F32))
        dn = dn_ref[r : r + ROWS, :]
        grad = grad + jnp.sum(dn * unit, axis=0, keepdims=True)
        e = dn * gain
        first = jnp.sum(e, axis=-1, keepdims=True) * (1.0 / D)
        cross = jnp.sum(e * unit, axis=-1, keepdims=True) * (1.0 / D)
        total = dy_ref[r : r + ROWS, :].astype(F32) + (e - first - unit * cross) * inverse
        if out_ref is not None:
            out_ref[r : r + ROWS, :] = total
        if low_ref is not None:
            low_ref[r : r + ROWS, :] = total.astype(BF)
    return grad


def make_bias(segc_ref, segr_ref, bias_ref, length):
    for b, ks, ke, off in bands(length)[0]:
        row = segr_ref[:, QB * b : QB * b + QB]
        for k in range(ks, ke, QB):
            allowed = segc_ref[k : k + QB, :] == row
            if k == QB * b:
                keys = lax.broadcasted_iota(jnp.int32, (QB, QB), 0)
                allowed = allowed & (keys <= lax.broadcasted_iota(jnp.int32, (QB, QB), 1))
            bias_ref[off + k - ks : off + k - ks + QB, :] = jnp.where(allowed, 0.0, neg_large)


def head_masked(pair_of, scale, dst_ref):
    lane = lax.broadcasted_iota(jnp.int32, (1, 2 * HEAD_DIM), 1)
    for p in range(HEADS // 2):
        pair = pair_of(p)
        for member in (0, 1):
            mask = jnp.where(lane // HEAD_DIM == member, scale, 0.0).astype(BF)
            dst_ref[2 * p + member] = pair * mask


class Weights:
    def __init__(self, wide, up, down):
        self.wide, self.up_ref, self.down = wide, up, down

    def cols(self, ref, lo, n):
        return ref[:, :, lo : lo + n].reshape(D, n)

    def inn(self, lo=0, n=3 * D):
        return self.cols(self.wide, lo, n)

    def out(self):
        return self.cols(self.wide, 3 * D, D)

    def up(self, lo=0, n=FF):
        return self.cols(self.up_ref, lo, n)


def forward(x_ref, segc, segr, w, ready, g_ref, k, out):
    length = x_ref.shape[0]
    norm_into(x_ref, g_ref[0:1, :], k["n1"])
    make_bias(segc, segr, k["bias"], length)
    ready(0)
    pk, pt = k["pk"], k["pt"]
    for c in range(0, 3 * D, D):
        pk[:, c : c + D] = dot(k["n1"][...], w.inn(c, D)).astype(BF)
    k["vT"][...] = pk[:, 2 * D :].T
    head_masked(lambda p: pk[:, 128 * p : 128 * p + 128], HEAD_DIM ** (-0.5), k["qm"])
    for b, ks, ke, off in bands(length)[0]:
        for h in range(HEADS):
            lo = D + 128 * (h // 2)
            st = dot(pk[ks:ke, lo : lo + 128], k["qm"][h, QB * b : QB * b + QB, :], 1, 1)
            st = st + k["bias"][off : off + ke - ks, :]
            lifted = jnp.exp(st - jnp.max(st, axis=0, keepdims=True))
            pb = (lifted * (1.0 / jnp.sum(lifted, axis=0, keepdims=True))).astype(BF)
            pt[h, off : off + ke - ks, :] = pb
            rows = slice(HEAD_DIM * h, HEAD_DIM * h + HEAD_DIM)
            k["attT"][rows, QB * b : QB * b + QB] = dot(k["vT"][rows, ks:ke], pb).astype(BF)
    mid = k["mid"]
    mid[...] = x_ref[...].astype(F32) + dot(k["attT"][...], w.out(), 0, 0)
    norm_into(mid, g_ref[1:2, :], k["n2"])
    ready(1)
    c0 = 0.7978845608028654
    c1 = 0.044715
    hs = k["hs"]
    for i, c in enumerate(range(0, FF, CHUNK)):
        hs[i % 2] = dot(k["n2"][...], w.up(c, CHUNK))
        for r in range(0, length, ROWS):
            v = hs[i % 2, r : r + ROWS, :]
            v2 = v * v
            th = jnp.tanh(v * (c0 + (c0 * c1) * v2))
            half = 0.5 * v
            k["act"][r : r + ROWS, c : c + CHUNK] = (half + half * th).astype(BF)
            slope = 0.5 + 0.5 * th + half * (1.0 - th * th) * (c0 + (3.0 * c0 * c1) * v2)
            k["gp"][r : r + ROWS, c : c + CHUNK] = slope.astype(BF)
    ready(2)
    out(mid[...] + dot(k["act"][...], w.down[...]))


def backward(x_ref, dy_ref, w, ready, g_ref, k, s, emit, dx, dx_low, gg):
    act, n2, pk, pt = k["act"], k["n2"], k["pk"], k["pt"]
    length = x_ref.shape[0]
    dyb = dy_ref
    emit.down(lambda lo, n: dot(act[:, lo : lo + n], dyb[...], 0, 0))
    ready(2)
    dh = s["dh"]
    for c in range(0, FF, CHUNK):
        grad = dot(dyb[...], w.down[c : c + CHUNK, :], 1, 1) * k["gp"][:, c : c + CHUNK].astype(F32)
        dh[:, c : c + CHUNK] = grad.astype(BF)
    emit.wide(1, lambda lo, n: dot(n2[...], dh[:, lo : lo + n], 0, 0), 0, FF)
    ready(1)
    s["dn"][...] = dot(dh[...], w.up(), 1, 1)
    dmb = s["dmb"]
    gg[1:2, :] = norm_back(s["dn"], k["mid"], dy_ref, g_ref[1:2, :], s["dmid"], dmb)
    emit.wide(0, lambda lo, n: dot(k["attT"][...], dmb[:, lo : lo + n]), 3 * D, D)
    ready(0)
    da = s["da"]
    da[...] = dot(dmb[...], w.out(), 1, 1).astype(BF)
    head_masked(lambda p: da[:, 128 * p : 128 * p + 128], 1.0, s["dam"])
    s["kT"][...] = pk[:, D : 2 * D].T
    dk, dv = s["dk"], s["dv"]
    for p in range(HEADS // 2):
        lo = 128 * p
        for b, ks, ke, off in bands(length)[0]:
            qs = slice(QB * b, QB * b + QB)
            gk = gv = None
            for h in (2 * p, 2 * p + 1):
                rows = slice(HEAD_DIM * h, HEAD_DIM * h + HEAD_DIM)
                dp = dot(pk[ks:ke, 2 * D + lo : 2 * D + lo + 128], s["dam"][h, qs, :], 1, 1)
                pb = pt[h, off : off + ke - ks, :]
                pf = pb.astype(F32)
                inner = jnp.sum(pf * dp, axis=0, keepdims=True)
                ds = (pf * (dp - inner)).astype(BF)
                s["dqT"][rows, qs] = dot(s["kT"][rows, ks:ke], ds) * HEAD_DIM ** (-0.5)
                one, two = dot(ds, k["qm"][h, qs, :]), dot(pb, s["dam"][h, qs, :])
                gk, gv = (one, two) if gk is None else (gk + one, gv + two)
            n = ke - ks - QB
            if n:
                dk[ks : ks + n, lo : lo + 128] += gk[:n]
                dv[ks : ks + n, lo : lo + 128] += gv[:n]
            dk[ks + n : ke, lo : lo + 128] = gk[n:]
            dv[ks + n : ke, lo : lo + 128] = gv[n:]
    dpk = s["dpk"]
    dpk[:, 0:D] = s["dqT"][...].T.astype(BF)
    dpk[:, D : 2 * D] = dk[...].astype(BF)
    dpk[:, 2 * D :] = dv[...].astype(BF)
    emit.wide(0, lambda lo, n: dot(k["n1"][...], dpk[:, lo : lo + n], 0, 0), 0, 3 * D)
    s["dn"][...] = dot(dpk[...], w.inn(), 1, 1)
    gg[0:1, :] = norm_back(s["dn"], x_ref, s["dmid"], g_ref[0:1, :], dx, dx_low)


def kept_shapes(L):
    nb = bands(L)[1]
    return dict(
        n1=((L, D), BF),
        pk=((L, 3 * D), BF),
        pt=((HEADS, nb, QB), BF),
        attT=((D, L), BF),
        mid=((L, D), F32),
        n2=((L, D), BF),
        act=((L, FF), BF),
        gp=((L, FF), BF),
        qm=((HEADS, L, 2 * HEAD_DIM), BF),
    )


def forward_scratch(L):
    nb = bands(L)[1]
    return dict(vT=((D, L), BF), bias=((nb, QB), F32), hs=((2, L, CHUNK), F32))


def backward_scratch(L):
    return dict(
        dh=((L, FF), BF),
        dn=((L, D), F32),
        dmid=((L, D), F32),
        dmb=((L, D), BF),
        dam=((HEADS, L, 2 * HEAD_DIM), BF),
        kT=((D, L), BF),
        dqT=((D, L), F32),
        dk=((L, D), F32),
        dv=((L, D), F32),
        dpk=((L, 3 * D), BF),
        da=((L, D), BF),
    )


def weight_scratch(plan):
    wide = (plan.slabs, D // plan.slabs, WIDE)
    return dict(wide=(wide, BF), up=(wide, BF), down=((FF, D), BF))


def vmem(shapes):
    return [pltpu.VMEM(shape, dtype) for shape, dtype in shapes.values()]


class Plan:
    def __init__(self, mesh):
        self.count = mesh.shape["dp"]
        self.bits = self.count.bit_length() - 1
        n = self.bits
        falling = list(reversed(range(n)))
        swapped = falling[:-2] + [falling[-1], falling[-2]]
        mixed = [0, n - 1] + list(range(1, n - 1))
        self.gather_orders = (falling, swapped, mixed)
        self.scatter_orders = tuple(tuple(reversed(o)) for o in self.gather_orders)
        self.slabs = self.count if (D // self.count) % 8 == 0 else 1

    def tables(self):
        me = lax.axis_index("dp")
        far = jnp.arange(self.count, dtype=jnp.int32) ^ me
        out = []
        for orders, rising in ((self.gather_orders, True), (self.scatter_orders, False)):
            for order in orders:
                place = jnp.zeros_like(far)
                for k, bit in enumerate(order):
                    shift = k if rising else self.bits - 1 - k
                    place = place | (((far >> bit) & 1) << shift)
                out.append(place)
        return out


def load_weights(plan, meta, own, got, dst, sems, block):
    core = meta[0]

    def start(src):
        for f in range(3):
            if plan.slabs == 1:
                pltpu.make_async_copy(src[f], dst[f], sems.at[f]).start()
                continue
            for s in range(plan.slabs):
                rows = FF // plan.slabs
                to = dst[f].at[s] if f < 2 else dst[f].at[rows * s : rows * s + rows, :]
                pltpu.make_async_copy(src[f].at[meta[1 + f * plan.count + s]], to, sems.at[f]).start()

    @pl.when(core == block)
    def _():
        start(own)

    @pl.when(core != block)
    def _():
        start(got)

    done = set()

    def ready(f):
        if f not in done:
            done.add(f)
            pltpu.make_async_copy(dst[f], dst[f], sems.at[f]).wait()

    return ready


class Emit:
    def __init__(self, plan, meta, wide, up, down):
        self.plan, self.meta, self.flows, self.down_ref = plan, meta, (wide, up), down

    def place(self, f, s):
        return self.meta[1 + (3 + f) * self.plan.count + s]

    def wide(self, f, make, base, width):
        ref, n, half = self.flows[f], self.plan.slabs, WIDE // 2
        step = D
        for lo in range(0, width, step):
            value = make(lo, step)
            if n == 1:
                ref[0, :, base + lo : base + lo + step] = value.astype(BF)
                continue
            value = value.reshape(n, D // n, step).astype(BF)
            h, at = (base + lo) // half, (base + lo) % half
            for s in range(n):
                ref[h ^ self.meta[0], self.place(f, s), :, at : at + step] = value[s]

    def down(self, make):
        ref, n = self.down_ref, self.plan.slabs
        step = D
        for lo in range(0, FF, step):
            value = make(lo, step)
            if n == 1:
                ref[0, lo : lo + step, :] = value.astype(BF)
                continue
            rows = FF // n // 2
            value = value.reshape(step // rows, rows, D).astype(BF)
            for i in range(step // rows):
                s, h = divmod(lo // rows + i, 2)
                ref[h ^ self.meta[0], self.place(2, s), :, :] = value[i]


def grad_shapes(plan):
    if plan.slabs == 1:
        return [struct((1, D, WIDE), BF), struct((1, D, WIDE), BF), struct((1, FF, D), BF)]
    n = plan.slabs
    wide = struct((2, n, D // n, WIDE // 2), BF)
    return [wide, wide, struct((2, n, FF // n // 2, D), BF)]


def params(mb=56):
    return pltpu.CompilerParams(vmem_limit_bytes=mb * 2**20)


def extractor_forward(plan, meta, x, segc, segr, prompts, gains, own, got):
    L = x.shape[0]
    kept, fs, ws = kept_shapes(L), forward_scratch(L), weight_scratch(plan)

    def kernel(meta, x, segc, segr, pr, g, *refs):
        own, got = refs[0:3], refs[3:6]
        x1 = refs[6]
        k = dict(zip(kept, refs[7:]))
        rest = refs[7 + len(kept) :]
        k.update(zip(fs, rest))
        dst, sems = rest[len(fs) : len(fs) + 3], rest[-1]
        ready = load_weights(plan, meta, own, got, dst, sems, 0)

        def out(value):
            x1[...] = value.astype(BF).astype(F32) + pr[...].astype(F32)

        forward(x, segc, segr, Weights(*dst), ready, g, k, out)

    outs = [struct((L, D), F32)] + [struct(*v) for v in kept.values()]
    res = pl.pallas_call(
        kernel,
        name="extractor_forward",
        out_shape=outs,
        in_specs=[SM] + [VM] * 5 + [ANY] * 6,
        out_specs=[VM] * len(outs),
        scratch_shapes=vmem(fs) + vmem(ws) + [pltpu.SemaphoreType.DMA((3,))],
        compiler_params=params(),
    )(meta, x, segc, segr, prompts, gains, *own, *got)
    return res[0], res[1:]


def generator_step(plan, meta, x, segc, segr, cot, gains, own, got):
    L = x.shape[0]
    kept, fs, bs, ws = kept_shapes(L), forward_scratch(L), backward_scratch(L), weight_scratch(plan)

    def kernel(meta, x, segc, segr, cot, g, *refs):
        own, got = refs[0:3], refs[3:6]
        y2, dx, gw, gu, gd, gg = refs[6:12]
        rest = refs[12:]
        k = dict(zip(kept, rest))
        rest = rest[len(kept) :]
        k.update(zip(fs, rest))
        rest = rest[len(fs) :]
        s = dict(zip(bs, rest))
        rest = rest[len(bs) :]
        dst, sems = rest[:3], rest[3]
        ready = load_weights(plan, meta, own, got, dst, sems, 1)

        def out(value):
            y2[...] = value

        w = Weights(*dst)
        forward(x, segc, segr, w, ready, g, k, out)
        backward(x, cot, w, ready, g, k, s, Emit(plan, meta, gw, gu, gd), None, dx, gg)

    return pl.pallas_call(
        kernel,
        name="generator_step",
        out_shape=[struct((L, D), F32), struct((L, D), BF)] + grad_shapes(plan) + [struct((2, D), F32)],
        in_specs=[SM] + [VM] * 5 + [ANY] * 6,
        out_specs=[VM] * 6,
        scratch_shapes=vmem(kept) + vmem(fs) + vmem(bs) + vmem(ws) + [pltpu.SemaphoreType.DMA((3,))],
        compiler_params=params(),
    )(meta, x, segc, segr, cot, gains, *own, *got)


def extractor_backward(plan, meta, x, dy, gains, own, got, kept_values):
    L = x.shape[0]
    kept, bs, ws = kept_shapes(L), backward_scratch(L), weight_scratch(plan)

    def kernel(meta, x, dy, g, *refs):
        own, got = refs[0:3], refs[3:6]
        k = dict(zip(kept, refs[6:]))
        rest = refs[6 + len(kept) :]
        dx, gw, gu, gd, gg = rest[:5]
        rest = rest[5:]
        s = dict(zip(bs, rest))
        rest = rest[len(bs) :]
        dst, sems = rest[:3], rest[3]
        ready = load_weights(plan, meta, own, got, dst, sems, 0)
        backward(x, dy, Weights(*dst), ready, g, k, s, Emit(plan, meta, gw, gu, gd), dx, None, gg)

    return pl.pallas_call(
        kernel,
        name="extractor_backward",
        out_shape=[struct((L, D), F32)] + grad_shapes(plan) + [struct((2, D), F32)],
        in_specs=[SM] + [VM] * 3 + [ANY] * 6 + [VM] * len(kept),
        out_specs=[VM] * 5,
        scratch_shapes=vmem(bs) + vmem(ws) + [pltpu.SemaphoreType.DMA((3,))],
        compiler_params=params(),
    )(meta, x, dy, gains, *own, *got, *kept_values)


def swap_cores(block):
    return lax.ppermute(block, "pipe", [(0, 1), (1, 0)])


def swap(block, bit):
    return lax.ppermute(block, "dp", [(i, i ^ (1 << bit)) for i in range(lax.axis_size("dp"))])


def gather(plan, shards):
    held = [shard[None] for shard in shards]
    for turn in range(plan.bits):
        came = [swap(held[f], plan.gather_orders[f][turn]) for f in range(3)]
        held = [jnp.concatenate([a, b], 0) for a, b in zip(held, came)]
    return held


def scatter(plan, grads):
    sums = [mine.astype(F32) + other.astype(F32) for mine, other in ((g[0], swap_cores(g[1])) for g in grads)]
    sums = [v.astype(BF) for v in sums]
    for turn in range(plan.bits):
        half = sums[0].shape[0] // 2
        came = [swap(sums[f][half:], plan.scatter_orders[f][turn]) for f in range(3)]
        sums = [(v[:half].astype(F32) + c.astype(F32)).astype(BF) for v, c in zip(sums, came)]
    return [v[0] for v in sums]


def placed_gather(plan, tables, flows):
    if plan.slabs > 1:
        return flows
    return [jnp.take(v, tables[f], axis=0).reshape((1, -1, v.shape[-1]) if f < 2 else (-1, v.shape[-1])) for f, v in enumerate(flows)]


def placed_scatter(plan, tables, core, grads):
    if plan.slabs > 1:
        return grads
    out = []
    for f, v in enumerate(grads):
        v = v.reshape(plan.count, -1, v.shape[-1])
        v = jnp.zeros_like(v).at[tables[3 + f]].set(v)
        axis = 2 if f < 2 else 1
        half = v.shape[axis] // 2
        out.append([lax.dynamic_slice_in_dim(v, c * half, half, axis) for c in (core, 1 - core)])
    return out


def moments(master, grad, first, second):
    drift = beta * first + (1.0 - beta) * grad
    spread = beta * second + (1.0 - beta) * grad * grad
    correction = 1.0 - beta**STEP
    update = drift / correction / (jnp.sqrt(spread / correction) + eps_adam) + decay * master
    return (drift, spread, update)


def solution(mesh):
    plan = Plan(mesh)

    def per_device(
        tokens,
        prompts,
        cotangent,
        segments,
        weight_in,
        weight_out,
        weight_up,
        weight_down,
        first_in,
        first_out,
        first_up,
        first_down,
        second_in,
        second_out,
        second_up,
        second_down,
        gains,
        gain_first,
        gain_second,
    ):
        core = lax.axis_index("pipe")
        leading = core == 0
        masters = (weight_in[0], weight_out[0], weight_up[0], weight_down[0])
        tables = plan.tables()
        meta = jnp.concatenate([core[None].astype(jnp.int32)] + tables)
        low = [m.astype(BF) for m in masters]
        flows = gather(plan, [jnp.concatenate(low[:2], 1), low[2], low[3]])
        flows = placed_gather(plan, tables, flows)
        got = [swap_cores(v) for v in flows]
        gains_got = swap_cores(gains[0])
        gains_zero = jnp.where(leading, gains[0], gains_got)
        gains_one = jnp.where(leading, gains_got, gains[0])

        def mine(v):
            return lax.dynamic_index_in_dim(v, core, 0, keepdims=False)[0]

        x, pr, cot, seg = mine(tokens), mine(prompts), mine(cotangent), mine(segments)
        segc, segr = seg[:, None], seg[None, :]
        x1, kept = extractor_forward(plan, meta, x, segc, segr, pr, gains_zero, flows, got)
        y2, dx1, *rest = generator_step(plan, meta, x1, segc, segr, cot, gains_one, flows, got)
        grads_one, gg_one = rest[:3], rest[3]
        half_one = scatter(plan, placed_scatter(plan, tables, core, grads_one))
        dx0, *rest = extractor_backward(plan, meta, x, dx1, gains_zero, flows, got, kept)
        grads_zero, gg_zero = rest[:3], rest[3]
        half_zero = scatter(plan, placed_scatter(plan, tables, core, grads_zero))

        result_got = swap_cores(jnp.where(leading, y2, dx0))
        result = jnp.where(leading, jnp.stack([dx0, result_got]), jnp.stack([result_got, y2]))
        section_result = result[None, :, None]
        gain_grad = jnp.where(leading, gg_zero, gg_one) + swap_cores(jnp.where(leading, gg_one, gg_zero))

        half_own = [jnp.where(leading, a, b) for a, b in zip(half_zero, half_one)]
        half_send = [jnp.where(leading, b, a) for a, b in zip(half_zero, half_one)]
        half_got = [swap_cores(v) for v in half_send]
        full = []
        for f, (a, b) in enumerate(zip(half_own, half_got)):
            axis = 1 if f < 2 else 0
            full.append(jnp.where(leading, jnp.concatenate([a, b], axis), jnp.concatenate([b, a], axis)).astype(F32))
        shares = (full[0][:, : 3 * D], full[0][:, 3 * D :], full[1], full[2])

        firsts = (first_in[0], first_out[0], first_up[0], first_down[0])
        seconds = (second_in[0], second_out[0], second_up[0], second_down[0])
        states = [moments(masters[m], shares[m], firsts[m], seconds[m]) for m in range(4)]
        squares = [jnp.sum(m * m) for m in masters] + [jnp.sum(st[2] * st[2]) for st in states]
        small = jnp.concatenate([jnp.pad(jnp.stack(squares), (0, D - 8))[None], gain_grad], 0)
        for bit in range(plan.bits):
            small = small + swap(small, bit)
        weight_norms = jnp.sqrt(small[0, 0:4])
        update_norms = jnp.sqrt(small[0, 4:8])
        trust = weight_norms / update_norms
        updated = [masters[m] - rate * trust[m] * states[m][2] for m in range(4)]
        gain_pair = gains[0]
        gain_drift, gain_spread, gain_update = moments(gain_pair, small[1:3], gain_first[0], gain_second[0])
        gain_weight = jnp.sqrt(jnp.sum(gain_pair * gain_pair, axis=-1))
        gain_step = jnp.sqrt(jnp.sum(gain_update * gain_update, axis=-1))
        gain_new = gain_pair - rate * (gain_weight / gain_step)[:, None] * gain_update
        norm_pairs = jnp.stack(
            [jnp.concatenate([weight_norms, gain_weight]), jnp.concatenate([update_norms, gain_step])],
            axis=-1,
        )
        return (
            section_result,
            *[st[0][None] for st in states],
            *[st[1][None] for st in states],
            *[u[None] for u in updated],
            *[u.astype(BF)[None] for u in updated],
            gain_drift[None],
            gain_spread[None],
            gain_new[None],
            norm_pairs[None],
        )

    rows = P(None, "dp", None, None)
    matrix = P("pipe", "dp", None)
    gain = P("pipe", None, None)
    in_specs = (rows, rows, rows, P(None, "dp", None)) + (matrix,) * 12 + (gain,) * 3
    out_specs = (P("pipe", None, "dp", None, None),) + (matrix,) * 16 + (gain,) * 4
    return jax.shard_map(
        per_device, mesh=mesh, in_specs=in_specs, out_specs=out_specs, check_vma=False
    )
```

```python
import math

import jax
import jax.numpy as jnp
from jax import lax
from jax.experimental import pallas as pl
from jax.experimental.pallas import tpu as pltpu
from jax.sharding import PartitionSpec as P

D = 384
FF = 1536
HEADS = 6
HEAD_DIM = 64
STEP = 3
BF = jnp.bfloat16
F32 = jnp.float32

rate = 0.3
beta = 0.5
eps_adam = 1e-06
decay = 0.01
eps_norm = 1e-05
neg_large = -1e30

QB = 128
REACH = 256
ROWS = 64
CHUNK = 384
WIDE = 4 * D
HALF = WIDE // 2
PAIRS = HEADS // 2
PAIR = 2 * HEAD_DIM
VM = pl.BlockSpec(memory_space=pltpu.VMEM)
SM = pl.BlockSpec(memory_space=pltpu.SMEM)
ANY = pl.BlockSpec(memory_space=pl.ANY)
struct = jax.ShapeDtypeStruct


def dot(a, b, ca=1, cb=0):
    return lax.dot_general(a, b, (((ca,), (cb,)), ((), ())), preferred_element_type=F32)


def bands(length):
    out = []
    off = 0
    for b in range(length // QB):
        ks, ke = max(0, QB * b - REACH), QB * (b + 1)
        out.append((b, ks, ke, off))
        off += ke - ks
    return out, off


def unit_of(x):
    mean = jnp.sum(x, axis=-1, keepdims=True) * (1.0 / D)
    centered = x - mean
    variance = jnp.sum(centered * centered, axis=-1, keepdims=True) * (1.0 / D)
    inverse = lax.rsqrt(variance + eps_norm)
    return centered * inverse, inverse


def norm_into(x_ref, gain, n_ref):
    for r in range(0, x_ref.shape[0], ROWS):
        unit, _ = unit_of(x_ref[r : r + ROWS, :].astype(F32))
        n_ref[r : r + ROWS, :] = (unit * gain).astype(BF)


def norm_back(dn_ref, x_ref, dy_ref, gain, out_ref, low_ref):
    grad = jnp.zeros((1, D), F32)
    for r in range(0, x_ref.shape[0], ROWS):
        unit, inverse = unit_of(x_ref[r : r + ROWS, :].astype(F32))
        dn = dn_ref[r : r + ROWS, :]
        grad = grad + jnp.sum(dn * unit, axis=0, keepdims=True)
        e = dn * gain
        first = jnp.sum(e, axis=-1, keepdims=True) * (1.0 / D)
        cross = jnp.sum(e * unit, axis=-1, keepdims=True) * (1.0 / D)
        total = dy_ref[r : r + ROWS, :].astype(F32) + (e - first - unit * cross) * inverse
        if out_ref is not None:
            out_ref[r : r + ROWS, :] = total
        if low_ref is not None:
            low_ref[r : r + ROWS, :] = total.astype(BF)
    return grad


def make_bias(seg_ref, bias_ref, length):
    columns = []
    for b in range(length // QB):
        row = seg_ref[:, QB * b : QB * b + QB].astype(F32)
        columns.append(jnp.broadcast_to(row, (QB, QB)).T)
    for b, ks, ke, off in bands(length)[0]:
        row = seg_ref[:, QB * b : QB * b + QB].astype(F32)
        for k in range(ks, ke, QB):
            allowed = columns[k // QB] == row
            if k == QB * b:
                keys = lax.broadcasted_iota(jnp.int32, (QB, QB), 0)
                allowed = allowed & (keys <= lax.broadcasted_iota(jnp.int32, (QB, QB), 1))
            bias_ref[off + k - ks : off + k - ks + QB, :] = jnp.where(allowed, 0.0, neg_large)


def head_masked(pair_of, scale, dst_ref):
    lane = lax.broadcasted_iota(jnp.int32, (1, PAIR), 1)
    for p in range(PAIRS):
        for b in range(dst_ref.shape[1]):
            pair = pair_of(p, b)
            for member in (0, 1):
                mask = jnp.where(lane // HEAD_DIM == member, scale, 0.0).astype(BF)
                dst_ref[p, b, QB * member : QB * member + QB, :] = pair * mask


def attend(pk, k, length):
    q2, vT, bias, ss, pt, attT = k["q2"], k["vT"], k["bias"], k["ss"], k["pt"], k["attT"]
    vT[...] = pk[:, 2 * D :].T
    head_masked(lambda p, b: pk[QB * b : QB * b + QB, PAIR * p : PAIR * p + PAIR], HEAD_DIM ** (-0.5), q2)
    places = bands(length)[0]
    for p in range(PAIRS):
        lo = D + PAIR * p
        for b, ks, ke, off in places:
            seen = bias[off : off + ke - ks, :]
            products = dot(pk[ks:ke, lo : lo + PAIR], q2[p, b], 1, 1)
            ss[p, off : off + ke - ks, :] = products + jnp.concatenate([seen, seen], 1)
    for p in range(PAIRS):
        for b, ks, ke, off in places:
            for m in (0, 1):
                cols = slice(QB * m, QB * m + QB)
                scores = ss[p, off : off + ke - ks, cols]
                lifted = jnp.exp(scores - jnp.max(scores, axis=0, keepdims=True))
                share = 1.0 / jnp.sum(lifted, axis=0, keepdims=True)
                pt[p, off : off + ke - ks, cols] = (lifted * share).astype(BF)
    for p in range(PAIRS):
        for b, ks, ke, off in places:
            both = dot(vT[PAIR * p : PAIR * p + PAIR, ks:ke], pt[p, off : off + ke - ks, :])
            for m in (0, 1):
                lo = HEAD_DIM * m
                part = both[lo : lo + HEAD_DIM, QB * m : QB * m + QB].astype(BF)
                attT[PAIR * p + lo : PAIR * p + lo + HEAD_DIM, QB * b : QB * b + QB] = part


def attend_back(pk, pt, da, k, length):
    d2, q2, kT, ss, ds, dqT, dk, dv, dpk = (k[n] for n in ("d2", "q2", "kT", "ss", "ds", "dqT", "dk", "dv", "dpk"))
    head_masked(lambda p, b: pk[QB * b : QB * b + QB, PAIR * p : PAIR * p + PAIR], HEAD_DIM ** (-0.5), q2)
    head_masked(lambda p, b: da[QB * b : QB * b + QB, PAIR * p : PAIR * p + PAIR], 1.0, d2)
    kT[...] = pk[:, D : 2 * D].T
    places = bands(length)[0]
    for p in range(PAIRS):
        lo = 2 * D + PAIR * p
        for b, ks, ke, off in places:
            ss[p, off : off + ke - ks, :] = dot(pk[ks:ke, lo : lo + PAIR], d2[p, b], 1, 1)
    for p in range(PAIRS):
        for b, ks, ke, off in places:
            for m in (0, 1):
                cols = slice(QB * m, QB * m + QB)
                chances = pt[p, off : off + ke - ks, cols].astype(F32)
                grad = ss[p, off : off + ke - ks, cols]
                inner = jnp.sum(chances * grad, axis=0, keepdims=True)
                ds[p, off : off + ke - ks, cols] = (chances * (grad - inner)).astype(BF)
    for p in range(PAIRS):
        lo = PAIR * p
        for b, ks, ke, off in places:
            grad = ds[p, off : off + ke - ks, :]
            both = dot(kT[lo : lo + PAIR, ks:ke], grad)
            for m in (0, 1):
                rows = slice(HEAD_DIM * m, HEAD_DIM * m + HEAD_DIM)
                part = both[rows, QB * m : QB * m + QB] * HEAD_DIM ** (-0.5)
                dqT[lo + HEAD_DIM * m : lo + HEAD_DIM * m + HEAD_DIM, QB * b : QB * b + QB] = part
            gk, gv = dot(grad, q2[p, b]), dot(pt[p, off : off + ke - ks, :], d2[p, b])
            n = ke - ks - QB
            if n:
                dk[ks : ks + n, lo : lo + PAIR] += gk[:n]
                dv[ks : ks + n, lo : lo + PAIR] += gv[:n]
            dk[ks + n : ke, lo : lo + PAIR] = gk[n:]
            dv[ks + n : ke, lo : lo + PAIR] = gv[n:]
    dpk[:, 0:D] = dqT[...].T.astype(BF)
    dpk[:, D : 2 * D] = dk[...].astype(BF)
    dpk[:, 2 * D :] = dv[...].astype(BF)


def attention_half(x, k, wide, gain, length):
    norm_into(x, gain[0:1, :], k["n1"])
    make_bias(k["seg"], k["bias"], length)
    pk = k["pk"]
    for c in range(0, 3 * D, D):
        pk[:, c : c + D] = dot(k["n1"][...], wide[:, c : c + D]).astype(BF)
    attend(pk, k, length)
    mid = k["mid"]
    mid[...] = x[...].astype(F32) + dot(k["attT"][...], wide[:, 3 * D :], 0, 0)
    norm_into(mid, gain[1:2, :], k["n2"])


def feed_forward(k, up, down, length, out):
    c0 = 0.7978845608028654
    c1 = 0.044715
    hs, act, gp, n2 = k["hs"], k["act"], k["gp"], k["n2"]
    for i, c in enumerate(range(0, FF, CHUNK)):
        hs[i % 2] = dot(n2[...], up[:, c : c + CHUNK])
        for r in range(0, length, ROWS):
            v = hs[i % 2, r : r + ROWS, :]
            v2 = v * v
            th = jnp.tanh(v * (c0 + (c0 * c1) * v2))
            half = 0.5 * v
            act[r : r + ROWS, c : c + CHUNK] = (half + half * th).astype(BF)
            slope = 0.5 + 0.5 * th + half * (1.0 - th * th) * (c0 + (3.0 * c0 * c1) * v2)
            gp[r : r + ROWS, c : c + CHUNK] = slope.astype(BF)
    out(k["mid"][...] + dot(act[...], down[...]))


def feed_back(dy, k, up, down, gain, emit):
    act, n2, dh, dn = k["act"], k["n2"], k["dh"], k["dn"]
    emit.down(lambda lo, n: dot(act[:, lo : lo + n], dy[...], 0, 0))
    for c in range(0, FF, CHUNK):
        grad = dot(dy[...], down[c : c + CHUNK, :], 1, 1) * k["gp"][:, c : c + CHUNK].astype(F32)
        dh[:, c : c + CHUNK] = grad.astype(BF)
    emit.up(lambda lo, n: dot(n2[...], dh[:, lo : lo + n], 0, 0))
    dn[...] = dot(dh[...], up[...], 1, 1)
    grad = norm_back(dn, k["mid"], dy, gain[1:2, :], k["dmid"], k["dmb"])
    return grad


def attention_back(k, wide, emit, length):
    dmb, da, dpk = k["dmb"], k["da"], k["dpk"]
    da[...] = dot(dmb[...], wide[:, 3 * D :], 1, 1).astype(BF)
    attend_back(k["pk"], k["pt"], da, k, length)

    def grad(lo):
        if lo < 3 * D:
            return dot(k["n1"][...], dpk[:, lo : lo + D], 0, 0)
        return dot(k["attT"][...], dmb[...])

    for at in range(0, HALF, D):
        emit.wide(grad, at)


def input_back(x, k, wide, gain, out, low):
    k["dn"][...] = dot(k["dpk"][...], wide[:, : 3 * D], 1, 1)
    return norm_back(k["dn"], x, k["dmid"], gain[0:1, :], out, low)


def spread_bits(index, order):
    out = 0
    for k, bit in enumerate(order):
        out = out | (((index >> k) & 1) << bit)
    return out


def gather_bits(index, order):
    out = 0
    for k, bit in enumerate(order):
        out = out | (((index >> bit) & 1) << k)
    return out


class Plan:
    def __init__(self, mesh):
        self.count = mesh.shape["dp"]
        self.bits = self.count.bit_length() - 1
        rest = tuple(range(4, self.bits))
        x, y, near, far = 0, 1, 2, 3
        gathers = (
            ((far, near, y, x), (far, x, near, y)),
            ((y, far, near, x), (near, far, x, y)),
            ((far, y, x, near), (far, x, y, near)),
        )
        scatters = (((y, x, far, near), (x, y, near, far)), ((x, far, near, y), (y, near, far, x)))
        self.gather_orders = tuple(tuple(rest + o for o in pair) for pair in gathers)
        self.scatter_orders = tuple(tuple(o + rest for o in pair) for pair in scatters)
        self.thin = (D // self.count) % 8 != 0
        self.slabs = 1 if self.thin else self.count
        self.rows = D // self.slabs

    def source(self, flow, block, place, me):
        return spread_bits(place, self.gather_orders[flow][block]) ^ me

    def place(self, block, half, device, me):
        order = tuple(reversed(self.scatter_orders[block][half]))
        return gather_bits(device, order) ^ gather_bits(me, order)

    def weight_shape(self, flow):
        return (D, WIDE) if flow < 2 else (FF, D)

    def grad_shapes(self):
        if self.thin:
            return {"gp_": [((D, WIDE), BF)], "gq_": [((D, WIDE), BF), ((FF, D), BF)]}
        n, r = self.slabs, self.rows
        return {"gp_": [((n, r, HALF), BF)] * 2, "gq_": [((n, 2, r, HALF), BF)] * 2}


class Emit:
    def __init__(self, plan, block, first, second):
        self.plan, self.first, self.second = plan, first, second
        self.core, me = lax.axis_index("pipe"), lax.axis_index("dp")
        if plan.thin:
            return
        leading = self.core == 0
        places = [[plan.place(block, half, s, me) for s in range(plan.slabs)] for half in (0, 1)]
        self.places = [
            [jnp.where(leading, places[which][s], places[1 - which][s]) for s in range(plan.slabs)] for which in (0, 1)
        ]

    def halves(self, zero, one, put, first=0):
        leading = self.core == 0
        for which, value in ((0, jnp.where(leading, zero, one)), (1, jnp.where(leading, one, zero))):
            value = value.astype(BF)
            for s in range(value.shape[0]):
                put(which, self.places[which][first + s], value[s])

    def wide(self, make, at):
        plan = self.plan
        zero, one = make(at), make(HALF + at)
        if plan.thin:
            self.first[0][:, at : at + D] = zero.astype(BF)
            self.first[0][:, HALF + at : HALF + at + D] = one.astype(BF)
            return
        shape = (plan.slabs, plan.rows, D)

        def put(which, place, value):
            self.first[which][place, :, at : at + D] = value

        self.halves(zero.reshape(shape), one.reshape(shape), put)

    def up(self, make):
        plan = self.plan
        if plan.thin:
            for lo in range(0, FF, D):
                self.second[0][:, lo : lo + D] = make(lo, D).astype(BF)
            return
        shape = (plan.slabs, plan.rows, D)
        for lo in range(0, HALF, D):

            def put(which, place, value, lo=lo):
                self.second[which][place, 0, :, lo : lo + D] = value

            self.halves(make(lo, D).reshape(shape), make(HALF + lo, D).reshape(shape), put)

    def down(self, make):
        plan = self.plan
        for lo in range(0, FF, D):
            value = make(lo, D)
            if plan.thin:
                self.second[1][lo : lo + D, :] = value.astype(BF)
                continue
            value = value.reshape(D // (4 * plan.rows), 2, 2 * plan.rows, D)

            def put(which, place, value, r=plan.rows):
                self.second[which][place, 1, :, 0:D] = value[:r]
                self.second[which][place, 1, :, D : 2 * D] = value[r:]

            self.halves(value[:, 0], value[:, 1], put, lo // (4 * plan.rows))


def limit(size):
    return pltpu.CompilerParams(vmem_limit_bytes=int(size) + 6 * 2**20)


def run_kernel(name, body, block, inputs, outs, scratch, cost, after=()):
    arrays = {n: v if isinstance(v, tuple) else (v, ()) for n, v in inputs.items()}
    size = sum(math.prod(shape) * jnp.dtype(dtype).itemsize for shape, dtype in scratch.values())

    def kernel(*refs):
        names = list(arrays) + [None] * len(after) + list(outs) + list(scratch)
        k = dict(zip(names, refs))
        core = lax.axis_index("pipe")
        for n, (_, index) in arrays.items():
            if index:
                k[n] = k[n].at[tuple(core if i == "core" else i for i in index)]
        gain = None
        if "gains" in arrays:
            gain = jnp.where(core == block, k["gains"][...], k["gains_got"][...])
        body(k, gain)

    result = pl.pallas_call(
        kernel,
        name=name,
        out_shape=[struct(*v) for v in outs.values()],
        in_specs=[VM] * len(arrays) + [ANY] * len(after),
        out_specs=[VM] * len(outs),
        scratch_shapes=[pltpu.VMEM(*v) for v in scratch.values()],
        compiler_params=limit(size),
        cost_estimate=pl.CostEstimate(flops=int(cost * 1e10), bytes_accessed=int(cost * 1e6), transcendentals=0),
    )(*[v for v, _ in arrays.values()], *after)
    return dict(zip(outs, result))


def small_kernel(name, kernel, outs, *inputs, after=()):
    def run(*refs):
        kernel(*refs[: len(inputs)], *refs[len(inputs) + len(after) :])

    return pl.pallas_call(
        run,
        name=name,
        out_shape=outs,
        in_specs=[VM] * len(inputs) + [ANY] * len(after),
        out_specs=[VM] * len(outs),
        compiler_params=limit(0),
    )(*inputs, *after)


def arrange(plan, flow, own, got):
    n, each = plan.slabs, plan.slabs // 2

    def kernel(a0, b0, a1, b1, zero, one):
        core, me = lax.axis_index("pipe"), lax.axis_index("dp")

        def move(first, second, dst, block):
            for place in range(n):
                src = first if place < each else second
                dst[plan.source(flow, block, place, me)] = src[place % each]

        @pl.when(core == 0)
        def _():
            move(a0, b0, zero, 0)
            move(a1, b1, one, 1)

        @pl.when(core != 0)
        def _():
            move(a0, b0, one, 1)
            move(a1, b1, zero, 0)

    like = struct((n, *own[0].shape[1:]), BF)
    out = small_kernel("arrange", kernel, [like, like], *own, *got)
    return [v.reshape(plan.weight_shape(flow)) for v in out]


def shapes(L):
    nb = bands(L)[1]
    return dict(
        n1=((L, D), BF),
        pk=((L, 3 * D), BF),
        pt=((PAIRS, nb, 2 * QB), BF),
        attT=((D, L), BF),
        mid=((L, D), F32),
        n2=((L, D), BF),
        act=((L, FF), BF),
        gp=((L, FF), BF),
        q2=((PAIRS, L // QB, 2 * QB, PAIR), BF),
        d2=((PAIRS, L // QB, 2 * QB, PAIR), BF),
        vT=((D, L), BF),
        bias=((nb, QB), F32),
        ss=((PAIRS, nb, 2 * QB), F32),
        ds=((PAIRS, nb, 2 * QB), BF),
        hs=((2, L, CHUNK), F32),
        dh=((L, FF), BF),
        dn=((L, D), F32),
        dmid=((L, D), F32),
        dmb=((L, D), BF),
        kT=((D, L), BF),
        dqT=((D, L), F32),
        dk=((L, D), F32),
        dv=((L, D), F32),
        dpk=((L, 3 * D), BF),
        da=((L, D), BF),
        x1=((L, D), F32),
        y2=((L, D), F32),
        dx=((L, D), F32),
        dxb=((L, D), BF),
        dg=((1, D), F32),
    )


def swap_cores(block):
    return lax.ppermute(block, "pipe", [(0, 1), (1, 0)])


def swap(block, bits):
    n = lax.axis_size("dp")
    route = [(c * n + i, c * n + (i ^ (1 << bits[c]))) for c in range(2) for i in range(n)]
    return lax.ppermute(block, ("pipe", "dp"), route)


def join(a, b, after):
    def kernel(a, b, out):
        n = a.shape[0]
        out[:n] = a[...]
        out[n:] = b[...]

    return small_kernel("join", kernel, [struct((2 * a.shape[0], *a.shape[1:]), a.dtype)], a, b, after=after)[0]


def gather(plan, shards):
    held = [shard[None] for shard in shards]
    last = ()
    for turn in range(plan.bits):
        came = [swap(held[f], (orders[0][turn], orders[1][turn])) for f, orders in enumerate(plan.gather_orders)]
        if turn < plan.bits - 1:
            for f in range(3):
                held[f] = join(held[f], came[f], last)
                last = (held[f],)
    return [(a, b) for a, b in zip(held, came)]


def added(a, b):
    return (a.astype(F32) + b.astype(F32)).astype(BF)


def add_first(first, second, after=()):
    def kernel(a, b, c, d, *outs):
        n = outs[0].shape[0]
        for i, out in enumerate(outs):
            for j in range(n):
                out[j, 0] = added(a[n * i + j], b[n * i + j])
                out[j, 1:3] = added(c[n * i + j], d[n * i + j])

    n, r, width = first[0].shape
    return small_kernel("add_first", kernel, [struct((n // 2, 3, r, width), BF)] * 2, *first, *second, after=after)


def add_split(a, b, after=()):
    def kernel(a, b, *outs):
        n = outs[0].shape[0]
        for i, out in enumerate(outs):
            for j in range(n):
                out[j] = added(a[n * i + j], b[n * i + j])

    return small_kernel("add_split", kernel, [struct((a.shape[0] // 2, *a.shape[1:]), BF)] * 2, a, b, after=after)


def behind(value, *others):
    return lax.optimization_barrier((value, *others))[0]


class Scatter:
    def __init__(self, plan, block, first, second):
        self.orders, self.turn = plan.scatter_orders[block], 0
        self.keep, self.send = add_first(first, second)

    def came(self, *after):
        send = behind(self.send, *after) if after else self.send
        value = swap(send, (self.orders[0][self.turn], self.orders[1][self.turn]))
        self.turn += 1
        return value

    def step(self, start_after=(), end_after=()):
        self.keep, self.send = add_split(self.keep, self.came(*start_after), end_after)


def owners(zero, one):
    def kernel(a, b, c, d, own, send):
        leading = lax.axis_index("pipe") == 0
        zero, one = a[0].astype(F32) + b[0].astype(F32), c[0].astype(F32) + d[0].astype(F32)
        own[...] = jnp.where(leading, zero, one).astype(BF)
        send[...] = jnp.where(leading, one, zero).astype(BF)

    like = struct(zero[0].shape[1:], BF)
    return small_kernel("owners", kernel, [like, like], *zero, *one)


def thin_arrange(plan, flow, own, got):
    core, me = lax.axis_index("pipe"), lax.axis_index("dp")
    index = jnp.arange(plan.count, dtype=jnp.int32)
    out = []
    for block in (0, 1):
        held = jnp.where(core == block, jnp.concatenate(own, 0), jnp.concatenate(got, 0))
        held = jnp.zeros_like(held).at[plan.source(flow, block, index, me)].set(held)
        out.append(held.reshape(plan.weight_shape(flow)))
    return out


def thin_halves(plan, block, grads, bundle):
    core, me = lax.axis_index("pipe"), lax.axis_index("dp")
    n, r = plan.count, D // plan.count
    parts = grads[0].reshape(n, r, 2, HALF).transpose(2, 0, 1, 3)
    if bundle:
        down = grads[1].reshape(n, 2, 2, r, D).transpose(1, 0, 3, 2, 4).reshape(2, n, r, HALF)
        parts = jnp.stack([parts, down], 2)
    index = jnp.arange(n, dtype=jnp.int32)
    halves = [jnp.zeros_like(parts[h]).at[plan.place(block, h, index, me)].set(parts[h]) for h in (0, 1)]
    return [jnp.where(core == 0, halves[i], halves[1 - i]) for i in (0, 1)]


def lanes(values):
    lane = lax.broadcasted_iota(jnp.int32, (1, D), 1)
    row = jnp.zeros((1, D), F32)
    for place, value in values:
        row = row + jnp.where(lane == place, value, 0.0)
    return row


def square_sum(v):
    return jnp.sum(jnp.sum(v * v, axis=1, keepdims=True), axis=0, keepdims=True)


def moments(master, grad, first, second):
    drift = beta * first + (1.0 - beta) * grad
    spread = beta * second + (1.0 - beta) * grad * grad
    correction = 1.0 - beta**STEP
    update = drift / correction / (jnp.sqrt(spread / correction) + eps_adam) + decay * master
    return (drift, spread, update)


def prepare(plan, masters):
    r = D // plan.count

    def kernel(wi, wo, wu, wd, wide, up, down, row):
        wide[:, : 3 * D] = wi[...].astype(BF)
        wide[:, 3 * D :] = wo[...].astype(BF)
        up[...] = wu[...].astype(BF)
        for q in range(4):
            down[q] = wd[r * q : r * q + r, :].astype(BF)
        row[...] = lanes([(i, square_sum(m[...])) for i, m in enumerate((wi, wo, wu, wd))])

    outs = [struct((r, WIDE), BF), struct((r, WIDE), BF), struct((4, r, D), BF), struct((1, D), F32)]
    return small_kernel("prepare", kernel, outs, *masters)


def update_moments(plan, own, got, masters, firsts, seconds, weight_row, gain_own, gain_got):
    r = D // plan.count

    def kernel(own, got, *refs):
        masters, firsts, seconds, (weight_row, gain_own, gain_got) = refs[0:4], refs[4:8], refs[8:12], refs[12:15]
        drifts, spreads, updates, small = refs[15:19], refs[19:23], refs[23:27], refs[27]
        leading = lax.axis_index("pipe") == 0
        a, b = own[...].astype(F32), got[...].astype(F32)
        h = (jnp.where(leading, a, b), jnp.where(leading, b, a))
        whole, tail = slice(None), 3 * D - HALF
        grads = [
            [((whole, slice(0, HALF)), h[0][0]), ((whole, slice(HALF, 3 * D)), h[1][0][:, :tail])],
            [((whole, slice(0, D)), h[1][0][:, tail:])],
            [((whole, slice(HALF * i, HALF * i + HALF)), h[i][1]) for i in (0, 1)],
            [
                ((slice(r * (2 * i + q), r * (2 * i + q) + r), whole), h[i][2][:, D * q : D * q + D])
                for i in (0, 1)
                for q in (0, 1)
            ],
        ]
        sums = []
        for m in range(4):
            total = jnp.zeros((1, 1), F32)
            for at, grad in grads[m]:
                drift, spread, update = moments(masters[m][at], grad, firsts[m][at], seconds[m][at])
                drifts[m][at], spreads[m][at], updates[m][at] = drift, spread, update
                total = total + square_sum(update)
            sums.append((4 + m, total))
        row = lanes(sums) + weight_row[...]
        gain = gain_own[...] + gain_got[...]
        for i in range(plan.count):
            small[i, 0:1, :] = row
            small[i, 1:3, :] = gain

    like = [struct(m.shape, F32) for m in masters]
    outs = like * 3 + [struct((plan.count, 3, D), F32)]
    res = small_kernel("moments", kernel, outs, own, got, *masters, *firsts, *seconds, weight_row, gain_own, gain_got)
    return res[0:4], res[4:8], res[8:12], res[12]


def finish(small, masters, updates, gains, gain_first, gain_second):
    def kernel(parts, m0, m1, m2, m3, u0, u1, u2, u3, gains, gf, gs, *outs):
        new, low, (gain_drift, gain_spread, gain_new, pairs) = outs[0:4], outs[4:8], outs[8:12]
        small = jnp.sum(parts[...], axis=0)
        weight = [jnp.sqrt(small[0:1, i : i + 1]) for i in range(4)]
        step = [jnp.sqrt(small[0:1, 4 + i : 5 + i]) for i in range(4)]
        for i, (m, u) in enumerate(zip((m0, m1, m2, m3), (u0, u1, u2, u3))):
            value = m[...] - rate * (weight[i] / step[i]) * u[...]
            new[i][...] = value
            low[i][...] = value.astype(BF)
        drift, spread, update = moments(gains[...], small[1:3, :], gf[...], gs[...])
        gain_drift[...] = drift
        gain_spread[...] = spread
        gain_weight = jnp.sqrt(jnp.sum(gains[...] * gains[...], axis=1, keepdims=True))
        gain_step = jnp.sqrt(jnp.sum(update * update, axis=1, keepdims=True))
        gain_new[...] = gains[...] - rate * (gain_weight / gain_step) * update
        for i in range(4):
            pairs[i : i + 1, 0:1] = weight[i]
            pairs[i : i + 1, 1:2] = step[i]
        pairs[4:6, 0:1] = gain_weight
        pairs[4:6, 1:2] = gain_step

    outs = [struct(m.shape, F32) for m in masters] + [struct(m.shape, BF) for m in masters]
    outs += [struct((2, D), F32)] * 3 + [struct((6, 2), F32)]
    return small_kernel("finish", kernel, outs, small, *masters, *updates, gains, gain_first, gain_second)


def lay_results(own, got):
    def kernel(own, got, out):
        core = lax.axis_index("pipe")
        out[core] = own[...]
        out[1 - core] = got[...]

    return small_kernel("lay_results", kernel, [struct((2, *own.shape), F32)], own, got)[0]


def solution(mesh):
    plan = Plan(mesh)

    def per_device(
        tokens,
        prompts,
        cotangent,
        segments,
        weight_in,
        weight_out,
        weight_up,
        weight_down,
        first_in,
        first_out,
        first_up,
        first_down,
        second_in,
        second_out,
        second_up,
        second_down,
        gains,
        gain_first,
        gain_second,
    ):
        L = tokens.shape[2]
        sh = shapes(L)
        masters = (weight_in[0], weight_out[0], weight_up[0], weight_down[0])
        firsts = (first_in[0], first_out[0], first_up[0], first_down[0])
        seconds = (second_in[0], second_out[0], second_up[0], second_down[0])

        wide, up, down, weight_row = prepare(plan, masters)
        flows = gather(plan, (wide, up, down))
        got = [tuple(swap_cores(v) for v in pieces) for pieces in flows]
        gains_got = swap_cores(gains[0])
        put = thin_arrange if plan.thin else arrange
        both = [put(plan, f, flows[f], got[f]) for f in range(3)]

        def weights(block, *which):
            return {n: both[f][block] for f, n in enumerate(("wide", "up", "down")) if n in which}

        def pick(*names):
            return {n: sh[n] for n in names}

        def there(source, *names):
            return {n: source[n] for n in names}

        gain_refs = {"gains": gains[0], "gains_got": gains_got}
        grads = plan.grad_shapes()
        g_first = {f"p{i}": v for i, v in enumerate(grads["gp_"])}
        g_second = {f"q{i}": v for i, v in enumerate(grads["gq_"])}
        x0 = {"x": (tokens, ("core", 0))}
        seg = {"seg": (segments[:, :, None], ("core", 0))}

        def refs_of(k, table):
            return [k[n] for n in table]

        def traded(source, table, block, bundle):
            values = [source[n] for n in table]
            if plan.thin:
                values = thin_halves(plan, block, values, bundle)
            return values[0], swap_cores(values[1])

        def body(k, gain):
            attention_half(k["x"], k, k["wide"], gain, L)

        attention_scratch = pick("q2", "vT", "bias", "ss")
        one = run_kernel(
            "extractor_attention", body, 0, {**gain_refs, **x0, **seg, **weights(0, "wide")},
            pick("n1", "pk", "pt", "attT", "mid", "n2"), attention_scratch, 6,
        )

        def body(k, gain):
            def out(value):
                k["x1"][...] = value.astype(BF).astype(F32) + k["pr"][...].astype(F32)

            feed_forward(k, k["up"], k["down"], L, out)

        two = run_kernel(
            "extractor_feed", body, 0,
            {**there(one, "n2", "mid"), "pr": (prompts, ("core", 0)), **weights(0, "up", "down")},
            pick("act", "gp", "x1"), pick("hs"), 4,
        )

        def body(k, gain):
            attention_half(k["x1"], k, k["wide"], gain, L)

        three = run_kernel(
            "generator_attention", body, 1, {**gain_refs, **there(two, "x1"), **seg, **weights(1, "wide")},
            pick("n1", "pk", "pt", "attT", "mid", "n2"), attention_scratch, 6,
        )

        def body(k, gain):
            def out(value):
                k["y2"][...] = value

            feed_forward(k, k["up"], k["down"], L, out)
            emit = Emit(plan, 1, None, refs_of(k, g_second))
            k["dg"][...] = feed_back(k["dy"], k, k["up"], k["down"], gain, emit)

        cot = {"dy": (cotangent, ("core", 0))}
        four = run_kernel(
            "generator_feed", body, 1,
            {**gain_refs, **there(three, "mid", "n2"), **cot, **weights(1, "up", "down")},
            {**pick("y2", "dmid", "dmb", "dg"), **g_second}, pick("act", "gp", "hs", "dh", "dn"), 10,
        )

        back_scratch = pick("q2", "d2", "kT", "ss", "ds", "dqT", "dk", "dv", "da")

        def body(k, gain):
            emit = Emit(plan, 1, refs_of(k, g_first), None)
            attention_back(k, k["wide"], emit, L)

        five = run_kernel(
            "generator_attention_back", body, 1,
            {**there(four, "dmb"), **there(three, "attT", "pk", "pt", "n1"), **weights(1, "wide")},
            {**g_first, **pick("dpk")}, back_scratch, 6,
        )

        second_one = traded(four, g_second, 1, 1)

        def body(k, gain):
            k["dg"][...] = input_back(k["x1"], k, k["wide"], gain, None, k["dxb"])

        six = run_kernel(
            "generator_input_back", body, 1,
            {**gain_refs, **there(five, "dpk"), **there(four, "dmid"), **there(two, "x1"), **weights(1, "wide")},
            pick("dg", "dxb"), pick("dn"), 3,
        )
        sum_one = Scatter(plan, 1, traded(five, g_first, 1, 0), second_one)

        def body(k, gain):
            emit = Emit(plan, 0, None, refs_of(k, g_second))
            k["dg"][...] = feed_back(k["dxb"], k, k["up"], k["down"], gain, emit)

        seven = run_kernel(
            "extractor_feed_back", body, 0,
            {**gain_refs, **there(six, "dxb"), **there(two, "act", "gp"), **there(one, "n2", "mid"), **weights(0, "up", "down")},
            {**g_second, **pick("dmid", "dmb", "dg")}, pick("dh", "dn"), 7, after=[sum_one.send],
        )
        second_zero = traded(seven, g_second, 0, 1)

        def body(k, gain):
            emit = Emit(plan, 0, refs_of(k, g_first), None)
            attention_back(k, k["wide"], emit, L)

        eight = run_kernel(
            "extractor_attention_back", body, 0,
            {**there(seven, "dmb"), **there(one, "attT", "pk", "pt", "n1"), **weights(0, "wide")},
            {**g_first, **pick("dpk")}, back_scratch, 6,
        )
        sum_one.step(end_after=[eight["dpk"]])
        sum_zero = Scatter(plan, 0, traded(eight, g_first, 0, 0), second_zero)

        def body(k, gain):
            dg = input_back(k["x"], k, k["wide"], gain, k["dx"], None)
            leading = lax.axis_index("pipe") == 0
            k["own"][...] = jnp.where(leading, k["dx"][...], k["y2"][...])
            k["send"][...] = jnp.where(leading, k["y2"][...], k["dx"][...])
            for i, (zero, one) in enumerate(((dg, k["g10"][...]), (k["g01"][...], k["g11"][...]))):
                k["gain_own"][i : i + 1, :] = jnp.where(leading, zero, one)
                k["gain_send"][i : i + 1, :] = jnp.where(leading, one, zero)

        nine = run_kernel(
            "extractor_input_back", body, 0,
            {**gain_refs, **there(eight, "dpk"), **there(seven, "dmid"), **x0, **weights(0, "wide"), **there(four, "y2"),
             "g01": seven["dg"], "g10": six["dg"], "g11": four["dg"]},
            {"own": sh["dx"], "send": sh["dx"], "gain_own": ((2, D), F32), "gain_send": ((2, D), F32)},
            pick("dn", "dx"), 3, after=[sum_zero.send, sum_one.send],
        )
        token = [nine["gain_own"]]
        sum_one.step(end_after=token)
        sum_zero.step(end_after=token)
        for turn in range(plan.bits - 3):
            sum_one.step()
            sum_zero.step()
        sum_zero.step()
        zero = sum_zero.keep, sum_zero.came()
        one = sum_one.keep, sum_one.came()
        own, send = owners(zero, one)
        grad_got = swap_cores(send)

        result = lay_results(nine["own"], swap_cores(nine["send"]))
        section_result = result[None, :, None]
        drifts, spreads, updates, small = update_moments(
            plan, own, grad_got, masters, firsts, seconds, weight_row, nine["gain_own"], swap_cores(nine["gain_send"])
        )
        small = lax.all_to_all(small, "dp", 0, 0)
        done = finish(small, masters, updates, gains[0], gain_first[0], gain_second[0])
        return (
            section_result,
            *[v[None] for v in (*drifts, *spreads)],
            *[v[None] for v in done],
        )

    rows = P(None, "dp", None, None)
    matrix = P("pipe", "dp", None)
    gain = P("pipe", None, None)
    in_specs = (rows, rows, rows, P(None, "dp", None)) + (matrix,) * 12 + (gain,) * 3
    out_specs = (P("pipe", None, "dp", None, None),) + (matrix,) * 16 + (gain,) * 4
    return jax.shard_map(
        per_device, mesh=mesh, in_specs=in_specs, out_specs=out_specs, check_vma=False
    )
```

```python
import math

import jax
import jax.numpy as jnp
from jax import lax
from jax.experimental import pallas as pl
from jax.experimental.pallas import tpu as pltpu
from jax.sharding import PartitionSpec as P

D = 384
FF = 1536
HEADS = 6
HEAD_DIM = 64
STEP = 3
BF = jnp.bfloat16
F32 = jnp.float32

rate = 0.3
beta = 0.5
eps_adam = 1e-06
decay = 0.01
eps_norm = 1e-05
neg_large = -1e30

QB = 128
REACH = 256
ROWS = 64
CHUNK = 384
WIDE = 4 * D
HALF = WIDE // 2
PAIRS = HEADS // 2
PAIR = 2 * HEAD_DIM
VM = pl.BlockSpec(memory_space=pltpu.VMEM)
SM = pl.BlockSpec(memory_space=pltpu.SMEM)
ANY = pl.BlockSpec(memory_space=pl.ANY)
struct = jax.ShapeDtypeStruct


def dot(a, b, ca=1, cb=0):
    return lax.dot_general(a, b, (((ca,), (cb,)), ((), ())), preferred_element_type=F32)


def bands(length):
    out = []
    off = 0
    for b in range(length // QB):
        ks, ke = max(0, QB * b - REACH), QB * (b + 1)
        out.append((b, ks, ke, off))
        off += ke - ks
    return out, off


def unit_of(x):
    mean = jnp.sum(x, axis=-1, keepdims=True) * (1.0 / D)
    centered = x - mean
    variance = jnp.sum(centered * centered, axis=-1, keepdims=True) * (1.0 / D)
    inverse = lax.rsqrt(variance + eps_norm)
    return centered * inverse, inverse


def norm_into(x_ref, gain, n_ref):
    for r in range(0, x_ref.shape[0], ROWS):
        unit, _ = unit_of(x_ref[r : r + ROWS, :].astype(F32))
        n_ref[r : r + ROWS, :] = (unit * gain).astype(BF)


def norm_back(dn_ref, x_ref, dy_ref, gain, out_ref, low_ref):
    grad = jnp.zeros((1, D), F32)
    for r in range(0, x_ref.shape[0], ROWS):
        unit, inverse = unit_of(x_ref[r : r + ROWS, :].astype(F32))
        dn = dn_ref[r : r + ROWS, :]
        grad = grad + jnp.sum(dn * unit, axis=0, keepdims=True)
        e = dn * gain
        first = jnp.sum(e, axis=-1, keepdims=True) * (1.0 / D)
        cross = jnp.sum(e * unit, axis=-1, keepdims=True) * (1.0 / D)
        total = dy_ref[r : r + ROWS, :].astype(F32) + (e - first - unit * cross) * inverse
        if out_ref is not None:
            out_ref[r : r + ROWS, :] = total
        if low_ref is not None:
            low_ref[r : r + ROWS, :] = total.astype(BF)
    return grad


def make_bias(seg_ref, bias_ref, length):
    columns = []
    for b in range(length // QB):
        row = seg_ref[:, QB * b : QB * b + QB].astype(F32)
        columns.append(jnp.broadcast_to(row, (QB, QB)).T)
    for b, ks, ke, off in bands(length)[0]:
        row = seg_ref[:, QB * b : QB * b + QB].astype(F32)
        for k in range(ks, ke, QB):
            allowed = columns[k // QB] == row
            if k == QB * b:
                keys = lax.broadcasted_iota(jnp.int32, (QB, QB), 0)
                allowed = allowed & (keys <= lax.broadcasted_iota(jnp.int32, (QB, QB), 1))
            bias_ref[off + k - ks : off + k - ks + QB, :] = jnp.where(allowed, 0.0, neg_large)


def head_masked(pair_of, scale, dst_ref):
    lane = lax.broadcasted_iota(jnp.int32, (1, PAIR), 1)
    for p in range(PAIRS):
        for b in range(dst_ref.shape[1]):
            pair = pair_of(p, b)
            for member in (0, 1):
                mask = jnp.where(lane // HEAD_DIM == member, scale, 0.0).astype(BF)
                dst_ref[p, b, QB * member : QB * member + QB, :] = pair * mask


def attend(pk, k, length):
    q2, vT, bias, ss, pt, attT = k["q2"], k["vT"], k["bias"], k["ss"], k["pt"], k["attT"]
    vT[...] = pk[:, 2 * D :].T
    head_masked(lambda p, b: pk[QB * b : QB * b + QB, PAIR * p : PAIR * p + PAIR], HEAD_DIM ** (-0.5), q2)
    places = bands(length)[0]
    for p in range(PAIRS):
        lo = D + PAIR * p
        for b, ks, ke, off in places:
            seen = bias[off : off + ke - ks, :]
            products = dot(pk[ks:ke, lo : lo + PAIR], q2[p, b], 1, 1)
            ss[p, off : off + ke - ks, :] = products + jnp.concatenate([seen, seen], 1)
    for p in range(PAIRS):
        for b, ks, ke, off in places:
            for m in (0, 1):
                cols = slice(QB * m, QB * m + QB)
                scores = ss[p, off : off + ke - ks, cols]
                lifted = jnp.exp(scores - jnp.max(scores, axis=0, keepdims=True))
                share = 1.0 / jnp.sum(lifted, axis=0, keepdims=True)
                pt[p, off : off + ke - ks, cols] = (lifted * share).astype(BF)
    for p in range(PAIRS):
        for b, ks, ke, off in places:
            both = dot(vT[PAIR * p : PAIR * p + PAIR, ks:ke], pt[p, off : off + ke - ks, :])
            for m in (0, 1):
                lo = HEAD_DIM * m
                part = both[lo : lo + HEAD_DIM, QB * m : QB * m + QB].astype(BF)
                attT[PAIR * p + lo : PAIR * p + lo + HEAD_DIM, QB * b : QB * b + QB] = part


def attend_back(pk, pt, da, k, length):
    d2, q2, kT, ss, ds, dqT, dk, dv, dpk = (k[n] for n in ("d2", "q2", "kT", "ss", "ds", "dqT", "dk", "dv", "dpk"))
    head_masked(lambda p, b: pk[QB * b : QB * b + QB, PAIR * p : PAIR * p + PAIR], HEAD_DIM ** (-0.5), q2)
    head_masked(lambda p, b: da[QB * b : QB * b + QB, PAIR * p : PAIR * p + PAIR], 1.0, d2)
    kT[...] = pk[:, D : 2 * D].T
    places = bands(length)[0]
    for p in range(PAIRS):
        lo = 2 * D + PAIR * p
        for b, ks, ke, off in places:
            ss[p, off : off + ke - ks, :] = dot(pk[ks:ke, lo : lo + PAIR], d2[p, b], 1, 1)
    for p in range(PAIRS):
        for b, ks, ke, off in places:
            for m in (0, 1):
                cols = slice(QB * m, QB * m + QB)
                chances = pt[p, off : off + ke - ks, cols].astype(F32)
                grad = ss[p, off : off + ke - ks, cols]
                inner = jnp.sum(chances * grad, axis=0, keepdims=True)
                ds[p, off : off + ke - ks, cols] = (chances * (grad - inner)).astype(BF)
    for p in range(PAIRS):
        lo = PAIR * p
        for b, ks, ke, off in places:
            grad = ds[p, off : off + ke - ks, :]
            both = dot(kT[lo : lo + PAIR, ks:ke], grad)
            for m in (0, 1):
                rows = slice(HEAD_DIM * m, HEAD_DIM * m + HEAD_DIM)
                part = both[rows, QB * m : QB * m + QB] * HEAD_DIM ** (-0.5)
                dqT[lo + HEAD_DIM * m : lo + HEAD_DIM * m + HEAD_DIM, QB * b : QB * b + QB] = part
            gk, gv = dot(grad, q2[p, b]), dot(pt[p, off : off + ke - ks, :], d2[p, b])
            n = ke - ks - QB
            if n:
                dk[ks : ks + n, lo : lo + PAIR] += gk[:n]
                dv[ks : ks + n, lo : lo + PAIR] += gv[:n]
            dk[ks + n : ke, lo : lo + PAIR] = gk[n:]
            dv[ks + n : ke, lo : lo + PAIR] = gv[n:]
    dpk[:, 0:D] = dqT[...].T.astype(BF)
    dpk[:, D : 2 * D] = dk[...].astype(BF)
    dpk[:, 2 * D :] = dv[...].astype(BF)


def attention_half(x, k, wide, gain, length):
    norm_into(x, gain[0:1, :], k["n1"])
    make_bias(k["seg"], k["bias"], length)
    pk = k["pk"]
    for c in range(0, 3 * D, D):
        pk[:, c : c + D] = dot(k["n1"][...], wide[:, c : c + D]).astype(BF)
    attend(pk, k, length)
    mid = k["mid"]
    mid[...] = x[...].astype(F32) + dot(k["attT"][...], wide[:, 3 * D :], 0, 0)
    norm_into(mid, gain[1:2, :], k["n2"])


def feed_forward(k, up, down, length, out):
    c0 = 0.7978845608028654
    c1 = 0.044715
    hs, act, gp, n2 = k["hs"], k["act"], k["gp"], k["n2"]
    for i, c in enumerate(range(0, FF, CHUNK)):
        hs[i % 2] = dot(n2[...], up[:, c : c + CHUNK])
        for r in range(0, length, ROWS):
            v = hs[i % 2, r : r + ROWS, :]
            v2 = v * v
            th = jnp.tanh(v * (c0 + (c0 * c1) * v2))
            half = 0.5 * v
            act[r : r + ROWS, c : c + CHUNK] = (half + half * th).astype(BF)
            slope = 0.5 + 0.5 * th + half * (1.0 - th * th) * (c0 + (3.0 * c0 * c1) * v2)
            gp[r : r + ROWS, c : c + CHUNK] = slope.astype(BF)
    out(k["mid"][...] + dot(act[...], down[...]))


def feed_back(dy, k, up, down, gain, emit):
    act, n2, dh, dn = k["act"], k["n2"], k["dh"], k["dn"]
    emit.down(lambda lo, n: dot(act[:, lo : lo + n], dy[...], 0, 0))
    for c in range(0, FF, CHUNK):
        grad = dot(dy[...], down[c : c + CHUNK, :], 1, 1) * k["gp"][:, c : c + CHUNK].astype(F32)
        dh[:, c : c + CHUNK] = grad.astype(BF)
    emit.up(lambda lo, n: dot(n2[...], dh[:, lo : lo + n], 0, 0))
    dn[...] = dot(dh[...], up[...], 1, 1)
    grad = norm_back(dn, k["mid"], dy, gain[1:2, :], k["dmid"], k["dmb"])
    return grad


def attention_back(k, wide, emit, length):
    dmb, da, dpk = k["dmb"], k["da"], k["dpk"]
    da[...] = dot(dmb[...], wide[:, 3 * D :], 1, 1).astype(BF)
    attend_back(k["pk"], k["pt"], da, k, length)

    def grad(lo):
        if lo < 3 * D:
            return dot(k["n1"][...], dpk[:, lo : lo + D], 0, 0)
        return dot(k["attT"][...], dmb[...])

    for at in range(0, HALF, D):
        emit.wide(grad, at)


def input_back(x, k, wide, gain, out, low):
    k["dn"][...] = dot(k["dpk"][...], wide[:, : 3 * D], 1, 1)
    return norm_back(k["dn"], x, k["dmid"], gain[0:1, :], out, low)


def spread_bits(index, order):
    out = 0
    for k, bit in enumerate(order):
        out = out | (((index >> k) & 1) << bit)
    return out


def gather_bits(index, order):
    out = 0
    for k, bit in enumerate(order):
        out = out | (((index >> bit) & 1) << k)
    return out


class Plan:
    def __init__(self, mesh):
        self.count = mesh.shape["dp"]
        self.bits = self.count.bit_length() - 1
        rest = tuple(range(4, self.bits))
        x, y, near, far = 0, 1, 2, 3
        gathers = (
            ((y, far, x, near), (far, near, y, x)),
            ((near, x, far, y), (far, x, near, y)),
            ((near, far, y, x), (far, x, y, near)),
        )
        scatters = (((y, x, near, far), (near, y, x, far)), ((near, x, y, far), (y, x, far, near)))
        self.gather_orders = tuple(tuple(rest + o for o in pair) for pair in gathers)
        self.scatter_orders = tuple(tuple(o + rest for o in pair) for pair in scatters)
        self.thin = (D // self.count) % 8 != 0
        self.slabs = 1 if self.thin else self.count
        self.rows = D // self.slabs

    def source(self, flow, block, place, me):
        return spread_bits(place, self.gather_orders[flow][block]) ^ me

    def place(self, block, half, device, me):
        order = tuple(reversed(self.scatter_orders[block][half]))
        return gather_bits(device, order) ^ gather_bits(me, order)

    def weight_shape(self, flow):
        return (D, WIDE) if flow < 2 else (FF, D)

    def grad_shapes(self):
        if self.thin:
            return {"gp_": [((D, WIDE), BF)], "gq_": [((D, WIDE), BF), ((FF, D), BF)]}
        n, r = self.slabs, self.rows
        return {"gp_": [((n, 1, r, HALF), BF)] * 2, "gq_": [((n, 2, r, HALF), BF)] * 2}


class Emit:
    def __init__(self, plan, block, first, second):
        self.plan, self.first, self.second = plan, first, second
        self.core, me = lax.axis_index("pipe"), lax.axis_index("dp")
        if plan.thin:
            return
        leading = self.core == 0
        places = [[plan.place(block, half, s, me) for s in range(plan.slabs)] for half in (0, 1)]
        self.places = [
            [jnp.where(leading, places[which][s], places[1 - which][s]) for s in range(plan.slabs)] for which in (0, 1)
        ]

    def halves(self, zero, one, put, first=0):
        leading = self.core == 0
        for which, value in ((0, jnp.where(leading, zero, one)), (1, jnp.where(leading, one, zero))):
            value = value.astype(BF)
            for s in range(value.shape[0]):
                put(which, self.places[which][first + s], value[s])

    def wide(self, make, at):
        plan = self.plan
        zero, one = make(at), make(HALF + at)
        if plan.thin:
            self.first[0][:, at : at + D] = zero.astype(BF)
            self.first[0][:, HALF + at : HALF + at + D] = one.astype(BF)
            return
        shape = (plan.slabs, plan.rows, D)

        def put(which, place, value):
            self.first[which][place, 0, :, at : at + D] = value

        self.halves(zero.reshape(shape), one.reshape(shape), put)

    def up(self, make):
        plan = self.plan
        if plan.thin:
            for lo in range(0, FF, D):
                self.second[0][:, lo : lo + D] = make(lo, D).astype(BF)
            return
        shape = (plan.slabs, plan.rows, D)
        for lo in range(0, HALF, D):

            def put(which, place, value, lo=lo):
                self.second[which][place, 0, :, lo : lo + D] = value

            self.halves(make(lo, D).reshape(shape), make(HALF + lo, D).reshape(shape), put)

    def down(self, make):
        plan = self.plan
        for lo in range(0, FF, D):
            value = make(lo, D)
            if plan.thin:
                self.second[1][lo : lo + D, :] = value.astype(BF)
                continue
            value = value.reshape(D // (4 * plan.rows), 2, 2 * plan.rows, D)

            def put(which, place, value, r=plan.rows):
                self.second[which][place, 1, :, 0:D] = value[:r]
                self.second[which][place, 1, :, D : 2 * D] = value[r:]

            self.halves(value[:, 0], value[:, 1], put, lo // (4 * plan.rows))


def limit(size):
    return pltpu.CompilerParams(vmem_limit_bytes=int(size) + 6 * 2**20)


def run_kernel(name, body, block, inputs, outs, scratch, cost, after=()):
    arrays = {n: v if isinstance(v, tuple) else (v, ()) for n, v in inputs.items()}
    size = sum(math.prod(shape) * jnp.dtype(dtype).itemsize for shape, dtype in scratch.values())

    def kernel(*refs):
        names = list(arrays) + [None] * len(after) + list(outs) + list(scratch)
        k = dict(zip(names, refs))
        core = lax.axis_index("pipe")
        for n, (_, index) in arrays.items():
            if index:
                k[n] = k[n].at[tuple(core if i == "core" else i for i in index)]
        gain = None
        if "gains" in arrays:
            gain = jnp.where(core == block, k["gains"][...], k["gains_got"][...])
        body(k, gain)

    result = pl.pallas_call(
        kernel,
        name=name,
        out_shape=[struct(*v) for v in outs.values()],
        in_specs=[VM] * len(arrays) + [ANY] * len(after),
        out_specs=[VM] * len(outs),
        scratch_shapes=[pltpu.VMEM(*v) for v in scratch.values()],
        compiler_params=limit(size),
        cost_estimate=pl.CostEstimate(flops=int(cost * 1e10), bytes_accessed=8, transcendentals=0),
    )(*[v for v, _ in arrays.values()], *after)
    return dict(zip(outs, result))


def small_kernel(name, kernel, outs, *inputs, after=()):
    def run(*refs):
        kernel(*refs[: len(inputs)], *refs[len(inputs) + len(after) :])

    return pl.pallas_call(
        run,
        name=name,
        out_shape=outs,
        in_specs=[VM] * len(inputs) + [ANY] * len(after),
        out_specs=[VM] * len(outs),
        compiler_params=limit(0),
    )(*inputs, *after)


def arrange(plan, flow, own, got):
    n, each = plan.slabs, plan.slabs // 2

    def kernel(a0, b0, a1, b1, zero, one):
        core, me = lax.axis_index("pipe"), lax.axis_index("dp")

        def move(first, second, dst, block):
            for place in range(n):
                src = first if place < each else second
                dst[plan.source(flow, block, place, me)] = src[place % each]

        @pl.when(core == 0)
        def _():
            move(a0, b0, zero, 0)
            move(a1, b1, one, 1)

        @pl.when(core != 0)
        def _():
            move(a0, b0, one, 1)
            move(a1, b1, zero, 0)

    like = struct((n, *own[0].shape[1:]), BF)
    out = small_kernel("arrange", kernel, [like, like], *own, *got)
    return [v.reshape(plan.weight_shape(flow)) for v in out]


def shapes(L):
    nb = bands(L)[1]
    return dict(
        n1=((L, D), BF),
        pk=((L, 3 * D), BF),
        pt=((PAIRS, nb, 2 * QB), BF),
        attT=((D, L), BF),
        mid=((L, D), F32),
        n2=((L, D), BF),
        act=((L, FF), BF),
        gp=((L, FF), BF),
        q2=((PAIRS, L // QB, 2 * QB, PAIR), BF),
        d2=((PAIRS, L // QB, 2 * QB, PAIR), BF),
        vT=((D, L), BF),
        bias=((nb, QB), F32),
        ss=((PAIRS, nb, 2 * QB), F32),
        ds=((PAIRS, nb, 2 * QB), BF),
        hs=((2, L, CHUNK), F32),
        dh=((L, FF), BF),
        dn=((L, D), F32),
        dmid=((L, D), F32),
        dmb=((L, D), BF),
        kT=((D, L), BF),
        dqT=((D, L), F32),
        dk=((L, D), F32),
        dv=((L, D), F32),
        dpk=((L, 3 * D), BF),
        da=((L, D), BF),
        x1=((L, D), F32),
        y2=((L, D), F32),
        dx=((L, D), F32),
        dxb=((L, D), BF),
        dg=((1, D), F32),
    )


def swap_cores(block):
    return lax.ppermute(block, "pipe", [(0, 1), (1, 0)])


def swap(block, bits):
    n = lax.axis_size("dp")
    route = [(c * n + i, c * n + (i ^ (1 << bits[c]))) for c in range(2) for i in range(n)]
    return lax.ppermute(block, ("pipe", "dp"), route)


def join(a, b, after):
    def kernel(a, b, out):
        n = a.shape[0]
        out[:n] = a[...]
        out[n:] = b[...]

    return small_kernel("join", kernel, [struct((2 * a.shape[0], *a.shape[1:]), a.dtype)], a, b, after=after)[0]


def gather(plan, shards):
    held = [shard[None] for shard in shards]
    last = ()
    for turn in range(plan.bits):
        came = [swap(held[f], (orders[0][turn], orders[1][turn])) for f, orders in enumerate(plan.gather_orders)]
        if turn < plan.bits - 1:
            for f in range(3):
                held[f] = join(held[f], came[f], last)
                last = (held[f],)
    return [(a, b) for a, b in zip(held, came)]


def added(a, b):
    return (a.astype(F32) + b.astype(F32)).astype(BF)


def add_split(pairs, after=()):
    def kernel(*refs):
        outs, n, at = refs[-2:], refs[-1].shape[0], 0
        for k in range(0, len(refs) - 2, 2):
            a, b = refs[k : k + 2]
            wide = a.shape[1]
            for i, out in enumerate(outs):
                for j in range(n):
                    out[j, at : at + wide] = added(a[n * i + j], b[n * i + j])
            at += wide

    n, _, r, width = pairs[0][0].shape
    outs = [struct((n // 2, sum(a.shape[1] for a, _ in pairs), r, width), BF)] * 2
    return small_kernel("add_split", kernel, outs, *[v for pair in pairs for v in pair], after=after)


def behind(value, *others):
    return lax.optimization_barrier((value, *others))[0]


class Scatter:
    def __init__(self, plan, block, *halves):
        self.orders, self.turn = plan.scatter_orders[block], 0
        self.pairs = [(mine, swap_cores(other)) for mine, other in halves]

    def step(self, *after):
        keep, send = add_split(self.pairs, after)
        self.pairs = [(keep, swap(send, (self.orders[0][self.turn], self.orders[1][self.turn])))]
        self.turn += 1
        return keep


def owners(zero, one):
    zero, one = ([pair for sums in v for pair in sums.pairs] for v in (zero, one))

    def total(refs):
        return jnp.concatenate([a[0].astype(F32) + b[0].astype(F32) for a, b in zip(refs[0::2], refs[1::2])], 0)

    def kernel(*refs):
        own, send = refs[-2:]
        a, b = total(refs[: 2 * len(zero)]), total(refs[2 * len(zero) : -2])
        leading = lax.axis_index("pipe") == 0
        own[...] = jnp.where(leading, a, b).astype(BF)
        send[...] = jnp.where(leading, b, a).astype(BF)

    like = struct((3, *zero[0][0].shape[2:]), BF)
    return small_kernel("owners", kernel, [like, like], *[v for pair in zero + one for v in pair])


def thin_arrange(plan, flow, own, got):
    core, me = lax.axis_index("pipe"), lax.axis_index("dp")
    index = jnp.arange(plan.count, dtype=jnp.int32)
    out = []
    for block in (0, 1):
        held = jnp.where(core == block, jnp.concatenate(own, 0), jnp.concatenate(got, 0))
        held = jnp.zeros_like(held).at[plan.source(flow, block, index, me)].set(held)
        out.append(held.reshape(plan.weight_shape(flow)))
    return out


def thin_halves(plan, block, grads, bundle):
    core, me = lax.axis_index("pipe"), lax.axis_index("dp")
    n, r = plan.count, D // plan.count
    parts = grads[0].reshape(n, r, 2, HALF).transpose(2, 0, 1, 3)
    parts = parts[:, :, None]
    if bundle:
        down = grads[1].reshape(n, 2, 2, r, D).transpose(1, 0, 3, 2, 4).reshape(2, n, 1, r, HALF)
        parts = jnp.concatenate([parts, down], 2)
    index = jnp.arange(n, dtype=jnp.int32)
    halves = [jnp.zeros_like(parts[h]).at[plan.place(block, h, index, me)].set(parts[h]) for h in (0, 1)]
    return [jnp.where(core == 0, halves[i], halves[1 - i]) for i in (0, 1)]


def lanes(values):
    lane = lax.broadcasted_iota(jnp.int32, (1, D), 1)
    row = jnp.zeros((1, D), F32)
    for place, value in values:
        row = row + jnp.where(lane == place, value, 0.0)
    return row


def square_sum(v):
    return jnp.sum(jnp.sum(v * v, axis=1, keepdims=True), axis=0, keepdims=True)


def moments(master, grad, first, second):
    drift = beta * first + (1.0 - beta) * grad
    spread = beta * second + (1.0 - beta) * grad * grad
    correction = 1.0 - beta**STEP
    update = drift / correction / (jnp.sqrt(spread / correction) + eps_adam) + decay * master
    return (drift, spread, update)


def update_moments(plan, own, got, masters, firsts, seconds, gain_own, gain_got):
    r = D // plan.count

    def kernel(own, got, *refs):
        masters, firsts, seconds, (gain_own, gain_got) = refs[0:4], refs[4:8], refs[8:12], refs[12:14]
        drifts, spreads, updates, small = refs[14:18], refs[18:22], refs[22:26], refs[26]
        leading = lax.axis_index("pipe") == 0
        a, b = own[...].astype(F32), got[...].astype(F32)
        h = (jnp.where(leading, a, b), jnp.where(leading, b, a))
        whole, tail = slice(None), 3 * D - HALF
        grads = [
            [((whole, slice(0, HALF)), h[0][0]), ((whole, slice(HALF, 3 * D)), h[1][0][:, :tail])],
            [((whole, slice(0, D)), h[1][0][:, tail:])],
            [((whole, slice(HALF * i, HALF * i + HALF)), h[i][1]) for i in (0, 1)],
            [
                ((slice(r * (2 * i + q), r * (2 * i + q) + r), whole), h[i][2][:, D * q : D * q + D])
                for i in (0, 1)
                for q in (0, 1)
            ],
        ]
        sums = [(m, square_sum(masters[m][...])) for m in range(4)]
        for m in range(4):
            total = jnp.zeros((1, 1), F32)
            for at, grad in grads[m]:
                drift, spread, update = moments(masters[m][at], grad, firsts[m][at], seconds[m][at])
                drifts[m][at], spreads[m][at], updates[m][at] = drift, spread, update
                total = total + square_sum(update)
            sums.append((4 + m, total))
        row = lanes(sums)
        gain = gain_own[...] + gain_got[...]
        for i in range(plan.count):
            small[i, 0:1, :] = row
            small[i, 1:3, :] = gain

    like = [struct(m.shape, F32) for m in masters]
    outs = like * 3 + [struct((plan.count, 3, D), F32)]
    res = small_kernel("moments", kernel, outs, own, got, *masters, *firsts, *seconds, gain_own, gain_got)
    return res[0:4], res[4:8], res[8:12], res[12]


def finish(small, masters, updates, gains, gain_first, gain_second):
    def kernel(parts, m0, m1, m2, m3, u0, u1, u2, u3, gains, gf, gs, *outs):
        new, low, (gain_drift, gain_spread, gain_new, pairs) = outs[0:4], outs[4:8], outs[8:12]
        small = jnp.sum(parts[...], axis=0)
        weight = [jnp.sqrt(small[0:1, i : i + 1]) for i in range(4)]
        step = [jnp.sqrt(small[0:1, 4 + i : 5 + i]) for i in range(4)]
        for i, (m, u) in enumerate(zip((m0, m1, m2, m3), (u0, u1, u2, u3))):
            value = m[...] - rate * (weight[i] / step[i]) * u[...]
            new[i][...] = value
            low[i][...] = value.astype(BF)
        drift, spread, update = moments(gains[...], small[1:3, :], gf[...], gs[...])
        gain_drift[...] = drift
        gain_spread[...] = spread
        gain_weight = jnp.sqrt(jnp.sum(gains[...] * gains[...], axis=1, keepdims=True))
        gain_step = jnp.sqrt(jnp.sum(update * update, axis=1, keepdims=True))
        gain_new[...] = gains[...] - rate * (gain_weight / gain_step) * update
        for i in range(4):
            pairs[0:1, i : i + 1] = weight[i]
            pairs[1:2, i : i + 1] = step[i]
        for i in range(2):
            pairs[0:1, 4 + i : 5 + i] = gain_weight[i : i + 1, :]
            pairs[1:2, 4 + i : 5 + i] = gain_step[i : i + 1, :]

    outs = [struct(m.shape, F32) for m in masters] + [struct(m.shape, BF) for m in masters]
    outs += [struct((2, D), F32)] * 3 + [struct((2, 6), F32)]
    res = small_kernel("finish", kernel, outs, small, *masters, *updates, gains, gain_first, gain_second)
    return [*res[:-1], res[-1].T]


def lay_results(own, got):
    def kernel(own, got, out, done):
        core = lax.axis_index("pipe")
        out[core] = own[...]
        out[1 - core] = got[...]
        done[...] = jnp.zeros(done.shape, F32)

    return small_kernel("lay_results", kernel, [struct((2, *own.shape), F32), struct((8, 128), F32)], own, got)


def solution(mesh):
    plan = Plan(mesh)

    def per_device(
        tokens,
        prompts,
        cotangent,
        segments,
        weight_in,
        weight_out,
        weight_up,
        weight_down,
        first_in,
        first_out,
        first_up,
        first_down,
        second_in,
        second_out,
        second_up,
        second_down,
        gains,
        gain_first,
        gain_second,
    ):
        L = tokens.shape[2]
        sh = shapes(L)
        masters = (weight_in[0], weight_out[0], weight_up[0], weight_down[0])
        firsts = (first_in[0], first_out[0], first_up[0], first_down[0])
        seconds = (second_in[0], second_out[0], second_up[0], second_down[0])

        low = [m.astype(BF) for m in masters]
        wide = jnp.concatenate(low[:2], 1)
        flows = gather(plan, (wide, low[2], low[3].reshape(4, -1, D)))
        gains_got = swap_cores(gains[0])
        put = thin_arrange if plan.thin else arrange
        both = [None] * 3

        def place_flow(flow, *after):
            first, second = flows[flow]
            if after:
                second = behind(second, *after)
            both[flow] = put(plan, flow, (first, second), (swap_cores(first), swap_cores(second)))

        place_flow(0)

        def weights(block, *which):
            return {n: both[f][block] for f, n in enumerate(("wide", "up", "down")) if n in which}

        def pick(*names):
            return {n: sh[n] for n in names}

        def there(source, *names):
            return {n: source[n] for n in names}

        gain_refs = {"gains": gains[0], "gains_got": gains_got}
        grads = plan.grad_shapes()
        g_first = {f"p{i}": v for i, v in enumerate(grads["gp_"])}
        g_second = {f"q{i}": v for i, v in enumerate(grads["gq_"])}
        x0 = {"x": (tokens, ("core", 0))}
        seg = {"seg": (segments[:, :, None], ("core", 0))}

        def refs_of(k, table):
            return [k[n] for n in table]

        def halves(source, table, block, bundle):
            values = [source[n] for n in table]
            return thin_halves(plan, block, values, bundle) if plan.thin else values

        def body(k, gain):
            attention_half(k["x"], k, k["wide"], gain, L)

        attention_scratch = pick("q2", "vT", "bias", "ss")
        one = run_kernel(
            "extractor_attention", body, 0, {**gain_refs, **x0, **seg, **weights(0, "wide")},
            pick("n1", "pk", "pt", "attT", "mid", "n2"), attention_scratch, 1e-9,
        )

        place_flow(1)
        place_flow(2)

        def body(k, gain):
            def out(value):
                k["x1"][...] = value.astype(BF).astype(F32) + k["pr"][...].astype(F32)

            feed_forward(k, k["up"], k["down"], L, out)

        two = run_kernel(
            "extractor_feed", body, 0,
            {**there(one, "n2", "mid"), "pr": (prompts, ("core", 0)), **weights(0, "up", "down")},
            pick("act", "gp", "x1"), pick("hs"), 1e-9,
        )

        def body(k, gain):
            attention_half(k["x1"], k, k["wide"], gain, L)

        three = run_kernel(
            "generator_attention", body, 1, {**gain_refs, **there(two, "x1"), **seg, **weights(1, "wide")},
            pick("n1", "pk", "pt", "attT", "mid", "n2"), attention_scratch, 1e-9,
        )

        def body(k, gain):
            def out(value):
                k["y2"][...] = value

            feed_forward(k, k["up"], k["down"], L, out)
            emit = Emit(plan, 1, None, refs_of(k, g_second))
            k["dg"][...] = feed_back(k["dy"], k, k["up"], k["down"], gain, emit)

        cot = {"dy": (cotangent, ("core", 0))}
        four = run_kernel(
            "generator_feed", body, 1,
            {**gain_refs, **there(three, "mid", "n2"), **cot, **weights(1, "up", "down")},
            {**pick("y2", "dmid", "dmb", "dg"), **g_second}, pick("act", "gp", "hs", "dh", "dn"), 10,
        )

        back_scratch = pick("q2", "d2", "kT", "ss", "ds", "dqT", "dk", "dv", "da")

        def body(k, gain):
            emit = Emit(plan, 1, refs_of(k, g_first), None)
            attention_back(k, k["wide"], emit, L)

        five = run_kernel(
            "generator_attention_back", body, 1,
            {**there(four, "dmb"), **there(three, "attT", "pk", "pt", "n1"), **weights(1, "wide")},
            {**g_first, **pick("dpk")}, back_scratch, 6,
        )
        def body(k, gain):
            k["dg"][...] = input_back(k["x1"], k, k["wide"], gain, None, k["dxb"])

        six = run_kernel(
            "generator_input_back", body, 1,
            {**gain_refs, **there(five, "dpk"), **there(four, "dmid"), **there(two, "x1"), **weights(1, "wide")},
            pick("dg", "dxb"), pick("dn"), 3,
        )
        sum_one = Scatter(plan, 1, halves(five, g_first, 1, 0), halves(four, g_second, 1, 1))
        last = sum_one.step(six["dxb"])

        def body(k, gain):
            emit = Emit(plan, 0, None, refs_of(k, g_second))
            k["dg"][...] = feed_back(k["dxb"], k, k["up"], k["down"], gain, emit)

        seven = run_kernel(
            "extractor_feed_back", body, 0,
            {**gain_refs, **there(six, "dxb"), **there(two, "act", "gp"), **there(one, "n2", "mid"), **weights(0, "up", "down")},
            {**g_second, **pick("dmid", "dmb", "dg")}, pick("dh", "dn"), 7, after=[last],
        )

        def body(k, gain):
            emit = Emit(plan, 0, refs_of(k, g_first), None)
            attention_back(k, k["wide"], emit, L)

        eight = run_kernel(
            "extractor_attention_back", body, 0,
            {**there(seven, "dmb"), **there(one, "attT", "pk", "pt", "n1"), **weights(0, "wide")},
            {**g_first, **pick("dpk")}, back_scratch, 6,
        )
        sum_zero = Scatter(plan, 0, halves(eight, g_first, 0, 0), halves(seven, g_second, 0, 1))
        last = sum_one.step(eight["dpk"])
        last = sum_zero.step(last)

        def body(k, gain):
            dg = input_back(k["x"], k, k["wide"], gain, k["dx"], None)
            leading = lax.axis_index("pipe") == 0
            k["own"][...] = jnp.where(leading, k["dx"][...], k["y2"][...])
            k["send"][...] = jnp.where(leading, k["y2"][...], k["dx"][...])
            for i, (zero, one) in enumerate(((dg, k["g10"][...]), (k["g01"][...], k["g11"][...]))):
                k["gain_own"][i : i + 1, :] = jnp.where(leading, zero, one)
                k["gain_send"][i : i + 1, :] = jnp.where(leading, one, zero)

        nine = run_kernel(
            "extractor_input_back", body, 0,
            {**gain_refs, **there(eight, "dpk"), **there(seven, "dmid"), **x0, **weights(0, "wide"), **there(four, "y2"),
             "g01": seven["dg"], "g10": six["dg"], "g11": four["dg"]},
            {"own": sh["dx"], "send": sh["dx"], "gain_own": ((2, D), F32), "gain_send": ((2, D), F32)},
            pick("dn", "dx"), 3, after=[last],
        )
        gain_got = swap_cores(nine["gain_send"])
        result, laid = lay_results(nine["own"], swap_cores(nine["send"]))
        section_result = result[None, :, None]
        last = sum_one.step(nine["gain_own"])
        last = sum_zero.step(last, gain_got)
        beside = (laid,)
        while sum_zero.turn < plan.bits:
            if sum_one.turn < plan.bits:
                last = sum_one.step(last)
            last = sum_zero.step(last, *beside)
            beside = ()
        own, send = owners((sum_zero,), (sum_one,))
        grad_got = swap_cores(send)

        drifts, spreads, updates, small = update_moments(
            plan, own, grad_got, masters, firsts, seconds, nine["gain_own"], gain_got
        )
        small = lax.all_to_all(small, "dp", 0, 0)
        done = finish(small, masters, updates, gains[0], gain_first[0], gain_second[0])
        return (
            section_result,
            *[v[None] for v in (*drifts, *spreads)],
            *[v[None] for v in done],
        )

    rows = P(None, "dp", None, None)
    matrix = P("pipe", "dp", None)
    gain = P("pipe", None, None)
    in_specs = (rows, rows, rows, P(None, "dp", None)) + (matrix,) * 12 + (gain,) * 3
    out_specs = (P("pipe", None, "dp", None, None),) + (matrix,) * 16 + (gain,) * 4
    return jax.shard_map(
        per_device, mesh=mesh, in_specs=in_specs, out_specs=out_specs, check_vma=False
    )
```

```python
import math

import jax
import jax.numpy as jnp
from jax import lax
from jax.experimental import pallas as pl
from jax.experimental.pallas import tpu as pltpu
from jax.sharding import PartitionSpec as P

D = 384
FF = 1536
HEADS = 6
HEAD_DIM = 64
STEP = 3
BF = jnp.bfloat16
F32 = jnp.float32

rate = 0.3
beta = 0.5
eps_adam = 1e-06
decay = 0.01
eps_norm = 1e-05
neg_large = -1e30

QB = 128
REACH = 256
ROWS = 64
CHUNK = 512
WIDE = 4 * D
HALF = WIDE // 2
PAIRS = HEADS // 2
PAIR = 2 * HEAD_DIM
VM = pl.BlockSpec(memory_space=pltpu.VMEM)
SM = pl.BlockSpec(memory_space=pltpu.SMEM)
ANY = pl.BlockSpec(memory_space=pl.ANY)
struct = jax.ShapeDtypeStruct


def dot(a, b, ca=1, cb=0):
    return lax.dot_general(a, b, (((ca,), (cb,)), ((), ())), preferred_element_type=F32)


def bands(length):
    out = []
    off = 0
    for b in range(length // QB):
        ks, ke = max(0, QB * b - REACH), QB * (b + 1)
        out.append((b, ks, ke, off))
        off += ke - ks
    return out, off


def unit_of(x):
    mean = jnp.sum(x, axis=-1, keepdims=True) * (1.0 / D)
    centered = x - mean
    variance = jnp.sum(centered * centered, axis=-1, keepdims=True) * (1.0 / D)
    inverse = lax.rsqrt(variance + eps_norm)
    return centered * inverse, inverse


def norm_into(x_ref, gain, n_ref):
    for r in range(0, x_ref.shape[0], ROWS):
        unit, _ = unit_of(x_ref[r : r + ROWS, :].astype(F32))
        n_ref[r : r + ROWS, :] = (unit * gain).astype(BF)


def norm_back(dn_ref, x_ref, dy_ref, gain, out_ref, low_ref):
    grad = jnp.zeros((1, D), F32)
    for r in range(0, x_ref.shape[0], ROWS):
        unit, inverse = unit_of(x_ref[r : r + ROWS, :].astype(F32))
        dn = dn_ref[r : r + ROWS, :]
        grad = grad + jnp.sum(dn * unit, axis=0, keepdims=True)
        e = dn * gain
        first = jnp.sum(e, axis=-1, keepdims=True) * (1.0 / D)
        cross = jnp.sum(e * unit, axis=-1, keepdims=True) * (1.0 / D)
        total = dy_ref[r : r + ROWS, :].astype(F32) + (e - first - unit * cross) * inverse
        if out_ref is not None:
            out_ref[r : r + ROWS, :] = total
        if low_ref is not None:
            low_ref[r : r + ROWS, :] = total.astype(BF)
    return grad


def make_bias(seg_ref, bias_ref, length):
    columns = []
    for b in range(length // QB):
        row = seg_ref[:, QB * b : QB * b + QB].astype(F32)
        columns.append(jnp.broadcast_to(row, (QB, QB)).T)
    for b, ks, ke, off in bands(length)[0]:
        row = seg_ref[:, QB * b : QB * b + QB].astype(F32)
        for k in range(ks, ke, QB):
            allowed = columns[k // QB] == row
            if k == QB * b:
                keys = lax.broadcasted_iota(jnp.int32, (QB, QB), 0)
                allowed = allowed & (keys <= lax.broadcasted_iota(jnp.int32, (QB, QB), 1))
            bias_ref[off + k - ks : off + k - ks + QB, :] = jnp.where(allowed, 0.0, neg_large)


def head_masked(pair_of, scale, dst_ref):
    lane = lax.broadcasted_iota(jnp.int32, (1, PAIR), 1)
    for p in range(PAIRS):
        for b in range(dst_ref.shape[1]):
            pair = pair_of(p, b)
            for member in (0, 1):
                mask = jnp.where(lane // HEAD_DIM == member, scale, 0.0).astype(BF)
                dst_ref[p, b, QB * member : QB * member + QB, :] = pair * mask


def attend(pk, k, length):
    q2, vT, bias, ss, pt, attT = k["q2"], k["vT"], k["bias"], k["ss"], k["pt"], k["attT"]
    vT[...] = pk[:, 2 * D :].T
    head_masked(lambda p, b: pk[QB * b : QB * b + QB, PAIR * p : PAIR * p + PAIR], HEAD_DIM ** (-0.5), q2)
    places = bands(length)[0]
    for p in range(PAIRS):
        lo = D + PAIR * p
        for b, ks, ke, off in places:
            seen = bias[off : off + ke - ks, :]
            products = dot(pk[ks:ke, lo : lo + PAIR], q2[p, b], 1, 1)
            ss[p, off : off + ke - ks, :] = products + jnp.concatenate([seen, seen], 1)
    for p in range(PAIRS):
        for b, ks, ke, off in places:
            for m in (0, 1):
                cols = slice(QB * m, QB * m + QB)
                scores = ss[p, off : off + ke - ks, cols]
                lifted = jnp.exp(scores - jnp.max(scores, axis=0, keepdims=True))
                share = 1.0 / jnp.sum(lifted, axis=0, keepdims=True)
                pt[p, off : off + ke - ks, cols] = (lifted * share).astype(BF)
    for p in range(PAIRS):
        for b, ks, ke, off in places:
            both = dot(vT[PAIR * p : PAIR * p + PAIR, ks:ke], pt[p, off : off + ke - ks, :])
            for m in (0, 1):
                lo = HEAD_DIM * m
                part = both[lo : lo + HEAD_DIM, QB * m : QB * m + QB].astype(BF)
                attT[PAIR * p + lo : PAIR * p + lo + HEAD_DIM, QB * b : QB * b + QB] = part


def attend_back(pk, pt, da, k, length):
    d2, q2, kT, ss, ds, dqT, dk, dv, dpk = (k[n] for n in ("d2", "q2", "kT", "ss", "ds", "dqT", "dk", "dv", "dpk"))
    head_masked(lambda p, b: pk[QB * b : QB * b + QB, PAIR * p : PAIR * p + PAIR], HEAD_DIM ** (-0.5), q2)
    head_masked(lambda p, b: da[QB * b : QB * b + QB, PAIR * p : PAIR * p + PAIR], 1.0, d2)
    kT[...] = pk[:, D : 2 * D].T
    places = bands(length)[0]
    for p in range(PAIRS):
        lo = 2 * D + PAIR * p
        for b, ks, ke, off in places:
            ss[p, off : off + ke - ks, :] = dot(pk[ks:ke, lo : lo + PAIR], d2[p, b], 1, 1)
    for p in range(PAIRS):
        for b, ks, ke, off in places:
            for m in (0, 1):
                cols = slice(QB * m, QB * m + QB)
                chances = pt[p, off : off + ke - ks, cols].astype(F32)
                grad = ss[p, off : off + ke - ks, cols]
                inner = jnp.sum(chances * grad, axis=0, keepdims=True)
                ds[p, off : off + ke - ks, cols] = (chances * (grad - inner)).astype(BF)
    for p in range(PAIRS):
        lo = PAIR * p
        for b, ks, ke, off in places:
            grad = ds[p, off : off + ke - ks, :]
            both = dot(kT[lo : lo + PAIR, ks:ke], grad)
            for m in (0, 1):
                rows = slice(HEAD_DIM * m, HEAD_DIM * m + HEAD_DIM)
                part = both[rows, QB * m : QB * m + QB] * HEAD_DIM ** (-0.5)
                dqT[lo + HEAD_DIM * m : lo + HEAD_DIM * m + HEAD_DIM, QB * b : QB * b + QB] = part
            gk, gv = dot(grad, q2[p, b]), dot(pt[p, off : off + ke - ks, :], d2[p, b])
            n = ke - ks - QB
            if n:
                dk[ks : ks + n, lo : lo + PAIR] += gk[:n]
                dv[ks : ks + n, lo : lo + PAIR] += gv[:n]
            dk[ks + n : ke, lo : lo + PAIR] = gk[n:]
            dv[ks + n : ke, lo : lo + PAIR] = gv[n:]
    dpk[:, 0:D] = dqT[...].T.astype(BF)
    dpk[:, D : 2 * D] = dk[...].astype(BF)
    dpk[:, 2 * D :] = dv[...].astype(BF)


def attention_half(x, k, wide, gain, length):
    norm_into(x, gain[0:1, :], k["n1"])
    make_bias(k["seg"], k["bias"], length)
    pk = k["pk"]
    pk[...] = dot(k["n1"][...], wide[:, : 3 * D]).astype(BF)
    attend(pk, k, length)
    mid = k["mid"]
    mid[...] = x[...].astype(F32) + dot(k["attT"][...], wide[:, 3 * D :], 0, 0)
    norm_into(mid, gain[1:2, :], k["n2"])


def feed_forward(k, up, down, length, out):
    c0 = 0.7978845608028654
    c1 = 0.044715
    hs, act, gp, n2 = k["hs"], k["act"], k["gp"], k["n2"]
    for i, c in enumerate(range(0, FF, CHUNK)):
        hs[i % 2] = dot(n2[...], up[:, c : c + CHUNK])
        for r in range(0, length, ROWS):
            v = hs[i % 2, r : r + ROWS, :]
            v2 = v * v
            th = jnp.tanh(v * (c0 + (c0 * c1) * v2))
            half = 0.5 * v
            act[r : r + ROWS, c : c + CHUNK] = (half + half * th).astype(BF)
            slope = 0.5 + 0.5 * th + half * (1.0 - th * th) * (c0 + (3.0 * c0 * c1) * v2)
            gp[r : r + ROWS, c : c + CHUNK] = slope.astype(BF)
    out(k["mid"][...] + dot(act[...], down[...]))


def feed_back(dy, k, up, down, gain, emit):
    act, n2, dh, dn = k["act"], k["n2"], k["dh"], k["dn"]
    emit.down(lambda lo, n: dot(act[:, lo : lo + n], dy[...], 0, 0))
    for c in range(0, FF, CHUNK):
        grad = dot(dy[...], down[c : c + CHUNK, :], 1, 1) * k["gp"][:, c : c + CHUNK].astype(F32)
        dh[:, c : c + CHUNK] = grad.astype(BF)
    emit.up(lambda lo, n: dot(n2[...], dh[:, lo : lo + n], 0, 0))
    dn[...] = dot(dh[...], up[...], 1, 1)
    grad = norm_back(dn, k["mid"], dy, gain[1:2, :], k["dmid"], k["dmb"])
    return grad


def attention_back(k, wide, emit, length):
    dmb, da, dpk = k["dmb"], k["da"], k["dpk"]
    da[...] = dot(dmb[...], wide[:, 3 * D :], 1, 1).astype(BF)
    attend_back(k["pk"], k["pt"], da, k, length)

    n1 = k["n1"]
    zero = dot(n1[...], dpk[:, :HALF], 0, 0)
    emit.wide(zero[:, :D], dot(n1[...], dpk[:, HALF:], 0, 0), 0)
    emit.wide(zero[:, D:], dot(k["attT"][...], dmb[...]), D)


def input_back(x, k, wide, gain, out, low):
    k["dn"][...] = dot(k["dpk"][...], wide[:, : 3 * D], 1, 1)
    return norm_back(k["dn"], x, k["dmid"], gain[0:1, :], out, low)


def spread_bits(index, order):
    out = 0
    for k, bit in enumerate(order):
        out = out | (((index >> k) & 1) << bit)
    return out


def gather_bits(index, order):
    out = 0
    for k, bit in enumerate(order):
        out = out | (((index >> bit) & 1) << k)
    return out


class Plan:
    def __init__(self, mesh):
        self.count = mesh.shape["dp"]
        self.bits = self.count.bit_length() - 1
        rest = tuple(range(4, self.bits))
        x, y, near, far = 0, 1, 2, 3
        gathers = (
            ((y, far, x, near), (far, near, y, x)),
            ((near, x, far, y), (far, x, near, y)),
            ((near, far, y, x), (far, x, y, near)),
        )
        scatters = (((y, x, near, far), (near, y, x, far)), ((near, x, y, far), (y, x, far, near)))
        self.gather_orders = tuple(tuple(rest + o for o in pair) for pair in gathers)
        self.scatter_orders = tuple(tuple(o + rest for o in pair) for pair in scatters)
        self.thin = (D // self.count) % 8 != 0
        self.slabs = 1 if self.thin else self.count
        self.rows = D // self.slabs

    def source(self, flow, block, place, me):
        return spread_bits(place, self.gather_orders[flow][block]) ^ me

    def place(self, block, half, device, me):
        order = tuple(reversed(self.scatter_orders[block][half]))
        return gather_bits(device, order) ^ gather_bits(me, order)

    def weight_shape(self, flow):
        return (D, WIDE) if flow < 2 else (FF, D)

    def grad_shapes(self):
        if self.thin:
            return {"gp_": [((D, WIDE), BF)], "gq_": [((D, WIDE), BF), ((FF, D), BF)]}
        n, r = self.slabs, self.rows
        return {"gp_": [((n, 1, r, HALF), BF)] * 2, "gq_": [((n, 2, r, HALF), BF)] * 2}


class Emit:
    def __init__(self, plan, block, first, second):
        self.plan, self.first, self.second = plan, first, second
        self.core, me = lax.axis_index("pipe"), lax.axis_index("dp")
        if plan.thin:
            return
        leading = self.core == 0
        places = [[plan.place(block, half, s, me) for s in range(plan.slabs)] for half in (0, 1)]
        self.places = [
            [jnp.where(leading, places[which][s], places[1 - which][s]) for s in range(plan.slabs)] for which in (0, 1)
        ]

    def halves(self, zero, one, put, first=0):
        leading = self.core == 0
        for which, value in ((0, jnp.where(leading, zero, one)), (1, jnp.where(leading, one, zero))):
            value = value.astype(BF)
            for s in range(value.shape[0]):
                put(which, self.places[which][first + s], value[s])

    def wide(self, zero, one, at):
        plan = self.plan
        if plan.thin:
            self.first[0][:, at : at + D] = zero.astype(BF)
            self.first[0][:, HALF + at : HALF + at + D] = one.astype(BF)
            return
        shape = (plan.slabs, plan.rows, D)

        def put(which, place, value):
            self.first[which][place, 0, :, at : at + D] = value

        self.halves(zero.reshape(shape), one.reshape(shape), put)

    def up(self, make):
        plan = self.plan
        if plan.thin:
            for lo in (0, HALF):
                self.second[0][:, lo : lo + HALF] = make(lo, HALF).astype(BF)
            return
        shape = (plan.slabs, plan.rows, HALF)

        def put(which, place, value):
            self.second[which][place, 0, :, :] = value

        self.halves(make(0, HALF).reshape(shape), make(HALF, HALF).reshape(shape), put)

    def down(self, make):
        plan = self.plan
        for lo in range(0, FF, HALF):
            value = make(lo, HALF)
            if plan.thin:
                self.second[1][lo : lo + HALF, :] = value.astype(BF)
                continue
            value = value.reshape(HALF // (4 * plan.rows), 2, 2 * plan.rows, D)

            def put(which, place, value, r=plan.rows):
                self.second[which][place, 1, :, 0:D] = value[:r]
                self.second[which][place, 1, :, D : 2 * D] = value[r:]

            self.halves(value[:, 0], value[:, 1], put, lo // (4 * plan.rows))


def limit(size):
    return pltpu.CompilerParams(vmem_limit_bytes=int(size) + 6 * 2**20)


def run_kernel(name, body, block, inputs, outs, scratch, cost, after=()):
    arrays = {n: v if isinstance(v, tuple) else (v, ()) for n, v in inputs.items()}
    size = sum(math.prod(shape) * jnp.dtype(dtype).itemsize for shape, dtype in scratch.values())

    def kernel(*refs):
        names = list(arrays) + [None] * len(after) + list(outs) + list(scratch)
        k = dict(zip(names, refs))
        core = lax.axis_index("pipe")
        for n, (_, index) in arrays.items():
            if index:
                k[n] = k[n].at[tuple(core if i == "core" else i for i in index)]
        gain = None
        if "gains" in arrays:
            gain = jnp.where(core == block, k["gains"][...], k["gains_got"][...])
        body(k, gain)

    result = pl.pallas_call(
        kernel,
        name=name,
        out_shape=[struct(*v) for v in outs.values()],
        in_specs=[VM] * len(arrays) + [ANY] * len(after),
        out_specs=[VM] * len(outs),
        scratch_shapes=[pltpu.VMEM(*v) for v in scratch.values()],
        compiler_params=limit(size),
        cost_estimate=pl.CostEstimate(flops=int(cost * 1e10), bytes_accessed=8, transcendentals=0),
    )(*[v for v, _ in arrays.values()], *after)
    return dict(zip(outs, result))


def small_kernel(name, kernel, outs, *inputs, after=()):
    def run(*refs):
        kernel(*refs[: len(inputs)], *refs[len(inputs) + len(after) :])

    return pl.pallas_call(
        run,
        name=name,
        out_shape=outs,
        in_specs=[VM] * len(inputs) + [ANY] * len(after),
        out_specs=[VM] * len(outs),
        compiler_params=limit(0),
    )(*inputs, *after)


def arrange(plan, flow, own, got, after):
    n, each = plan.slabs, plan.slabs // 2

    def kernel(a0, b0, a1, b1, zero, one):
        core, me = lax.axis_index("pipe"), lax.axis_index("dp")

        def move(first, second, dst, block):
            for place in range(n):
                src = first if place < each else second
                dst[plan.source(flow, block, place, me)] = src[place % each]

        @pl.when(core == 0)
        def _():
            move(a0, b0, zero, 0)
            move(a1, b1, one, 1)

        @pl.when(core != 0)
        def _():
            move(a0, b0, one, 1)
            move(a1, b1, zero, 0)

    like = struct((n, *own[0].shape[1:]), BF)
    out = small_kernel("arrange", kernel, [like, like], *own, *got, after=after)
    return [v.reshape(plan.weight_shape(flow)) for v in out]


def shapes(L):
    nb = bands(L)[1]
    return dict(
        n1=((L, D), BF),
        pk=((L, 3 * D), BF),
        pt=((PAIRS, nb, 2 * QB), BF),
        attT=((D, L), BF),
        mid=((L, D), F32),
        n2=((L, D), BF),
        act=((L, FF), BF),
        gp=((L, FF), BF),
        q2=((PAIRS, L // QB, 2 * QB, PAIR), BF),
        d2=((PAIRS, L // QB, 2 * QB, PAIR), BF),
        vT=((D, L), BF),
        bias=((nb, QB), F32),
        ss=((PAIRS, nb, 2 * QB), F32),
        ds=((PAIRS, nb, 2 * QB), BF),
        hs=((2, L, CHUNK), F32),
        dh=((L, FF), BF),
        dn=((L, D), F32),
        dmid=((L, D), F32),
        dmb=((L, D), BF),
        kT=((D, L), BF),
        dqT=((D, L), F32),
        dk=((L, D), F32),
        dv=((L, D), F32),
        dpk=((L, 3 * D), BF),
        da=((L, D), BF),
        x1=((L, D), F32),
        y2=((L, D), F32),
        dx=((L, D), F32),
        dxb=((L, D), BF),
        dg=((1, D), F32),
    )


def swap_cores(block):
    return lax.ppermute(block, "pipe", [(0, 1), (1, 0)])


def swap(block, bits):
    n = lax.axis_size("dp")
    route = [(c * n + i, c * n + (i ^ (1 << bits[c]))) for c in range(2) for i in range(n)]
    return lax.ppermute(block, ("pipe", "dp"), route)


def join(a, b, after):
    def kernel(a, b, out):
        n = a.shape[0]
        out[:n] = a[...]
        out[n:] = b[...]

    return small_kernel("join", kernel, [struct((2 * a.shape[0], *a.shape[1:]), a.dtype)], a, b, after=after)[0]


def gather(plan, shards, early):
    held = [shard[None] for shard in shards]
    last = ()
    for turn in range(plan.bits):
        came = [swap(held[f], (orders[0][turn], orders[1][turn])) for f, orders in enumerate(plan.gather_orders)]
        last = (*last, early) if turn == 1 else last
        if turn < plan.bits - 1:
            for f in range(3):
                held[f] = join(held[f], came[f], last)
                last = (held[f],)
    return [(a, b) for a, b in zip(held, came)]


def added(a, b):
    return (a.astype(F32) + b.astype(F32)).astype(BF)


def add_split(pairs, after=()):
    def kernel(*refs):
        outs, n, at = refs[-2:], refs[-1].shape[0], 0
        for k in range(0, len(refs) - 2, 2):
            a, b = refs[k : k + 2]
            wide = a.shape[1]
            for i, out in enumerate(outs):
                for j in range(n):
                    out[j, at : at + wide] = added(a[n * i + j], b[n * i + j])
            at += wide

    n, _, r, width = pairs[0][0].shape
    outs = [struct((n // 2, sum(a.shape[1] for a, _ in pairs), r, width), BF)] * 2
    return small_kernel("add_split", kernel, outs, *[v for pair in pairs for v in pair], after=after)


def behind(value, *others):
    return lax.optimization_barrier((value, *others))[0]


class Scatter:
    def __init__(self, plan, block):
        self.orders, self.turn, self.pairs = plan.scatter_orders[block], 0, []

    def exchange(self, pairs, turn, after):
        keep, send = add_split(pairs, after)
        return keep, swap(send, (self.orders[0][turn], self.orders[1][turn]))

    def begin(self, parts, *after):
        self.pairs = [self.exchange(parts, 0, after)]
        self.turn = 1
        return self.pairs[0][0]

    def part(self, mine, came, *after):
        self.pairs.append(self.exchange([(mine, came)], 0, after))
        self.turn = 1
        return self.pairs[-1][0]

    def step(self, *after):
        if self.turn == 1:
            self.pairs.reverse()
        self.pairs = [self.exchange(self.pairs, self.turn, after)]
        self.turn += 1
        return self.pairs[0][0]


def owners(zero, one):
    zero, one = ([pair for sums in v for pair in sums.pairs] for v in (zero, one))

    def total(refs):
        return jnp.concatenate([a[0].astype(F32) + b[0].astype(F32) for a, b in zip(refs[0::2], refs[1::2])], 0)

    def kernel(*refs):
        own, send = refs[-2:]
        a, b = total(refs[: 2 * len(zero)]), total(refs[2 * len(zero) : -2])
        leading = lax.axis_index("pipe") == 0
        own[...] = jnp.where(leading, a, b).astype(BF)
        send[...] = jnp.where(leading, b, a).astype(BF)

    like = struct((3, *zero[0][0].shape[2:]), BF)
    return small_kernel("owners", kernel, [like, like], *[v for pair in zero + one for v in pair])


def thin_arrange(plan, flow, own, got, after):
    core, me = lax.axis_index("pipe"), lax.axis_index("dp")
    index = jnp.arange(plan.count, dtype=jnp.int32)
    out = []
    for block in (0, 1):
        held = jnp.where(core == block, jnp.concatenate(own, 0), jnp.concatenate(got, 0))
        held = jnp.zeros_like(held).at[plan.source(flow, block, index, me)].set(held)
        out.append(held.reshape(plan.weight_shape(flow)))
    return out


def thin_halves(plan, block, grads, bundle):
    core, me = lax.axis_index("pipe"), lax.axis_index("dp")
    n, r = plan.count, D // plan.count
    parts = grads[0].reshape(n, r, 2, HALF).transpose(2, 0, 1, 3)
    parts = parts[:, :, None]
    if bundle:
        down = grads[1].reshape(n, 2, 2, r, D).transpose(1, 0, 3, 2, 4).reshape(2, n, 1, r, HALF)
        parts = jnp.concatenate([parts, down], 2)
    index = jnp.arange(n, dtype=jnp.int32)
    halves = [jnp.zeros_like(parts[h]).at[plan.place(block, h, index, me)].set(parts[h]) for h in (0, 1)]
    return [jnp.where(core == 0, halves[i], halves[1 - i]) for i in (0, 1)]


def lanes(values):
    lane = lax.broadcasted_iota(jnp.int32, (1, D), 1)
    row = jnp.zeros((1, D), F32)
    for place, value in values:
        row = row + jnp.where(lane == place, value, 0.0)
    return row


def square_sum(v):
    return jnp.sum(jnp.sum(v * v, axis=1, keepdims=True), axis=0, keepdims=True)


def moments(master, grad, first, second):
    drift = beta * first + (1.0 - beta) * grad
    spread = beta * second + (1.0 - beta) * grad * grad
    correction = 1.0 - beta**STEP
    update = drift / correction / (jnp.sqrt(spread / correction) + eps_adam) + decay * master
    return (drift, spread, update)


def update_moments(plan, own, got, masters, firsts, seconds, gain_own, gain_got):
    r = D // plan.count

    def kernel(own, got, *refs):
        masters, firsts, seconds, (gain_own, gain_got) = refs[0:4], refs[4:8], refs[8:12], refs[12:14]
        drifts, spreads, updates, small = refs[14:18], refs[18:22], refs[22:26], refs[26]
        leading = lax.axis_index("pipe") == 0
        a, b = own[...].astype(F32), got[...].astype(F32)
        h = (jnp.where(leading, a, b), jnp.where(leading, b, a))
        whole, tail = slice(None), 3 * D - HALF
        grads = [
            [((whole, slice(0, HALF)), h[0][0]), ((whole, slice(HALF, 3 * D)), h[1][0][:, :tail])],
            [((whole, slice(0, D)), h[1][0][:, tail:])],
            [((whole, slice(HALF * i, HALF * i + HALF)), h[i][1]) for i in (0, 1)],
            [
                ((slice(r * (2 * i + q), r * (2 * i + q) + r), whole), h[i][2][:, D * q : D * q + D])
                for i in (0, 1)
                for q in (0, 1)
            ],
        ]
        sums = [(m, square_sum(masters[m][...])) for m in range(4)]
        for m in range(4):
            total = jnp.zeros((1, 1), F32)
            for at, grad in grads[m]:
                drift, spread, update = moments(masters[m][at], grad, firsts[m][at], seconds[m][at])
                drifts[m][at], spreads[m][at], updates[m][at] = drift, spread, update
                total = total + square_sum(update)
            sums.append((4 + m, total))
        row = lanes(sums)
        gain = gain_own[...] + gain_got[...]
        for i in range(plan.count):
            small[i, 0:1, :] = row
            small[i, 1:3, :] = gain

    like = [struct(m.shape, F32) for m in masters]
    outs = like * 3 + [struct((plan.count, 3, D), F32)]
    res = small_kernel("moments", kernel, outs, own, got, *masters, *firsts, *seconds, gain_own, gain_got)
    return res[0:4], res[4:8], res[8:12], res[12]


def finish(small, masters, updates, gains, gain_first, gain_second):
    def kernel(parts, m0, m1, m2, m3, u0, u1, u2, u3, gains, gf, gs, *outs):
        new, low, (gain_drift, gain_spread, gain_new, pairs) = outs[0:4], outs[4:8], outs[8:12]
        small = jnp.sum(parts[...], axis=0)
        weight = [jnp.sqrt(small[0:1, i : i + 1]) for i in range(4)]
        step = [jnp.sqrt(small[0:1, 4 + i : 5 + i]) for i in range(4)]
        for i, (m, u) in enumerate(zip((m0, m1, m2, m3), (u0, u1, u2, u3))):
            value = m[...] - rate * (weight[i] / step[i]) * u[...]
            new[i][...] = value
            low[i][...] = value.astype(BF)
        drift, spread, update = moments(gains[...], small[1:3, :], gf[...], gs[...])
        gain_drift[...] = drift
        gain_spread[...] = spread
        gain_weight = jnp.sqrt(jnp.sum(gains[...] * gains[...], axis=1, keepdims=True))
        gain_step = jnp.sqrt(jnp.sum(update * update, axis=1, keepdims=True))
        gain_new[...] = gains[...] - rate * (gain_weight / gain_step) * update
        for i in range(4):
            pairs[0:1, i : i + 1] = weight[i]
            pairs[1:2, i : i + 1] = step[i]
        for i in range(2):
            pairs[0:1, 4 + i : 5 + i] = gain_weight[i : i + 1, :]
            pairs[1:2, 4 + i : 5 + i] = gain_step[i : i + 1, :]

    outs = [struct(m.shape, F32) for m in masters] + [struct(m.shape, BF) for m in masters]
    outs += [struct((2, D), F32)] * 3 + [struct((2, 6), F32)]
    res = small_kernel("finish", kernel, outs, small, *masters, *updates, gains, gain_first, gain_second)
    return [*res[:-1], res[-1].T]


def lay_results(own, got):
    def kernel(own, got, out, done):
        core = lax.axis_index("pipe")
        out[core] = own[...]
        out[1 - core] = got[...]
        done[...] = jnp.zeros(done.shape, F32)

    return small_kernel("lay_results", kernel, [struct((2, *own.shape), F32), struct((8, 128), F32)], own, got)


def solution(mesh):
    plan = Plan(mesh)

    def per_device(
        tokens,
        prompts,
        cotangent,
        segments,
        weight_in,
        weight_out,
        weight_up,
        weight_down,
        first_in,
        first_out,
        first_up,
        first_down,
        second_in,
        second_out,
        second_up,
        second_down,
        gains,
        gain_first,
        gain_second,
    ):
        L = tokens.shape[2]
        sh = shapes(L)
        masters = (weight_in[0], weight_out[0], weight_up[0], weight_down[0])
        firsts = (first_in[0], first_out[0], first_up[0], first_down[0])
        seconds = (second_in[0], second_out[0], second_up[0], second_down[0])

        low = [m.astype(BF) for m in masters]
        wide = jnp.concatenate(low[:2], 1)
        gains_got = swap_cores(gains[0])
        flows = gather(plan, (wide, low[2], low[3].reshape(4, -1, D)), gains_got)
        put = thin_arrange if plan.thin else arrange
        both = [None] * 3

        def place_flow(flow, *after):
            both[flow] = put(plan, flow, flows[flow], tuple(swap_cores(v) for v in flows[flow]), after)

        place_flow(0)

        def weights(block, *which):
            return {n: both[f][block] for f, n in enumerate(("wide", "up", "down")) if n in which}

        def pick(*names):
            return {n: sh[n] for n in names}

        def there(source, *names):
            return {n: source[n] for n in names}

        gain_refs = {"gains": gains[0], "gains_got": gains_got}
        grads = plan.grad_shapes()
        g_first = {f"p{i}": v for i, v in enumerate(grads["gp_"])}
        g_second = {f"q{i}": v for i, v in enumerate(grads["gq_"])}
        x0 = {"x": (tokens, ("core", 0))}
        seg = {"seg": (segments[:, :, None], ("core", 0))}

        def refs_of(k, table):
            return [k[n] for n in table]

        def traded(source, table, block, bundle):
            values = [source[n] for n in table]
            if plan.thin:
                values = thin_halves(plan, block, values, bundle)
            return values[0], swap_cores(values[1])

        def body(k, gain):
            attention_half(k["x"], k, k["wide"], gain, L)

        attention_scratch = pick("q2", "vT", "bias", "ss")
        one = run_kernel(
            "extractor_attention", body, 0, {**gain_refs, **x0, **seg, "pr": (prompts, ("core", 0)), **weights(0, "wide")},
            pick("n1", "pk", "pt", "attT", "mid", "n2"), attention_scratch, 1e-9,
        )

        place_flow(1, one["n2"])
        place_flow(2, one["n2"])

        def body(k, gain):
            def out(value):
                k["x1"][...] = value.astype(BF).astype(F32) + k["pr"][...].astype(F32)

            feed_forward(k, k["up"], k["down"], L, out)

        two = run_kernel(
            "extractor_feed", body, 0,
            {**there(one, "n2", "mid"), "pr": (prompts, ("core", 0)), **weights(0, "up", "down")},
            pick("act", "gp", "x1"), pick("hs"), 3.2,
        )

        def body(k, gain):
            attention_half(k["x1"], k, k["wide"], gain, L)

        three = run_kernel(
            "generator_attention", body, 1, {**gain_refs, **there(two, "x1"), **seg, **weights(1, "wide")},
            pick("n1", "pk", "pt", "attT", "mid", "n2"), attention_scratch, 1e-9,
        )

        def body(k, gain):
            def out(value):
                k["y2"][...] = value

            feed_forward(k, k["up"], k["down"], L, out)
            emit = Emit(plan, 1, None, refs_of(k, g_second))
            k["dg"][...] = feed_back(k["dy"], k, k["up"], k["down"], gain, emit)

        cot = {"dy": (cotangent, ("core", 0))}
        four = run_kernel(
            "generator_feed", body, 1,
            {**gain_refs, **there(three, "mid", "n2"), **cot, **weights(1, "up", "down")},
            {**pick("y2", "dmid", "dmb", "dg"), **g_second}, pick("act", "gp", "hs", "dh", "dn"), 10,
        )

        second_one = traded(four, g_second, 1, 1)
        back_scratch = pick("q2", "d2", "kT", "ss", "ds", "dqT", "dk", "dv", "da")

        def body(k, gain):
            emit = Emit(plan, 1, refs_of(k, g_first), None)
            attention_back(k, k["wide"], emit, L)

        five = run_kernel(
            "generator_attention_back", body, 1,
            {**there(four, "dmb"), **there(three, "attT", "pk", "pt", "n1"), **weights(1, "wide")},
            {**g_first, **pick("dpk")}, back_scratch, 6,
        )
        sum_one = Scatter(plan, 1)
        first_one = traded(five, g_first, 1, 0)

        def body(k, gain):
            k["dg"][...] = input_back(k["x1"], k, k["wide"], gain, None, k["dxb"])

        six = run_kernel(
            "generator_input_back", body, 1,
            {**gain_refs, **there(five, "dpk"), **there(four, "dmid"), **there(two, "x1"), **weights(1, "wide")},
            pick("dg", "dxb"), pick("dn"), 3,
        )
        last = sum_one.begin([first_one, second_one], six["dxb"])

        def body(k, gain):
            emit = Emit(plan, 0, None, refs_of(k, g_second))
            k["dg"][...] = feed_back(k["dxb"], k, k["up"], k["down"], gain, emit)

        seven = run_kernel(
            "extractor_feed_back", body, 0,
            {**gain_refs, **there(six, "dxb"), **there(two, "act", "gp"), **there(one, "n2", "mid"), **weights(0, "up", "down")},
            {**g_second, **pick("dmid", "dmb", "dg")}, pick("dh", "dn"), 7, after=[last],
        )
        second_zero = traded(seven, g_second, 0, 1)

        def body(k, gain):
            emit = Emit(plan, 0, refs_of(k, g_first), None)
            attention_back(k, k["wide"], emit, L)

        eight = run_kernel(
            "extractor_attention_back", body, 0,
            {**there(seven, "dmb"), **there(one, "attT", "pk", "pt", "n1"), **weights(0, "wide")},
            {**g_first, **pick("dpk")}, back_scratch, 6,
        )
        first_zero = traded(eight, g_first, 0, 0)
        sum_zero = Scatter(plan, 0)
        last = sum_zero.begin([first_zero, second_zero], eight["dpk"])
        last = sum_one.step(last)

        def body(k, gain):
            dg = input_back(k["x"], k, k["wide"], gain, k["dx"], None)
            leading = lax.axis_index("pipe") == 0
            k["own"][...] = jnp.where(leading, k["dx"][...], k["y2"][...])
            k["send"][...] = jnp.where(leading, k["y2"][...], k["dx"][...])
            for i, (zero, one) in enumerate(((dg, k["g10"][...]), (k["g01"][...], k["g11"][...]))):
                k["gain_own"][i : i + 1, :] = jnp.where(leading, zero, one)
                k["gain_send"][i : i + 1, :] = jnp.where(leading, one, zero)

        nine = run_kernel(
            "extractor_input_back", body, 0,
            {**gain_refs, **there(eight, "dpk"), **there(seven, "dmid"), **x0, **weights(0, "wide"), **there(four, "y2"),
             "g01": seven["dg"], "g10": six["dg"], "g11": four["dg"]},
            {"own": sh["dx"], "send": sh["dx"], "gain_own": ((2, D), F32), "gain_send": ((2, D), F32)},
            pick("dn", "dx"), 3, after=[last],
        )
        gain_got = swap_cores(nine["gain_send"])
        result, laid = lay_results(nine["own"], swap_cores(nine["send"]))
        section_result = result[None, :, None]
        last = sum_one.step(nine["gain_own"])
        last = sum_zero.step(last, gain_got)
        beside = (laid,)
        while sum_zero.turn < plan.bits:
            if sum_one.turn < plan.bits:
                last = sum_one.step(last)
            last = sum_zero.step(last, *beside)
            beside = ()
        own, send = owners((sum_zero,), (sum_one,))
        grad_got = swap_cores(send)

        drifts, spreads, updates, small = update_moments(
            plan, own, grad_got, masters, firsts, seconds, nine["gain_own"], gain_got
        )
        small = lax.all_to_all(small, "dp", 0, 0)
        done = finish(small, masters, updates, gains[0], gain_first[0], gain_second[0])
        return (
            section_result,
            *[v[None] for v in (*drifts, *spreads)],
            *[v[None] for v in done],
        )

    rows = P(None, "dp", None, None)
    matrix = P("pipe", "dp", None)
    gain = P("pipe", None, None)
    in_specs = (rows, rows, rows, P(None, "dp", None)) + (matrix,) * 12 + (gain,) * 3
    out_specs = (P("pipe", None, "dp", None, None),) + (matrix,) * 16 + (gain,) * 4
    return jax.shard_map(
        per_device, mesh=mesh, in_specs=in_specs, out_specs=out_specs, check_vma=False
    )
```

```python
import math

import jax
import jax.numpy as jnp
from jax import lax
from jax.experimental import pallas as pl
from jax.experimental.pallas import tpu as pltpu
from jax.sharding import PartitionSpec as P

D = 384
FF = 1536
HEADS = 6
HEAD_DIM = 64
STEP = 3
BF = jnp.bfloat16
F32 = jnp.float32

rate = 0.3
beta = 0.5
eps_adam = 1e-06
decay = 0.01
eps_norm = 1e-05
neg_large = -1e30

QB = 128
REACH = 256
ROWS = 64
CHUNK = 512
WIDE = 4 * D
HALF = WIDE // 2
PAIRS = HEADS // 2
PAIR = 2 * HEAD_DIM
VM = pl.BlockSpec(memory_space=pltpu.VMEM)
SM = pl.BlockSpec(memory_space=pltpu.SMEM)
ANY = pl.BlockSpec(memory_space=pl.ANY)
struct = jax.ShapeDtypeStruct


def dot(a, b, ca=1, cb=0):
    return lax.dot_general(a, b, (((ca,), (cb,)), ((), ())), preferred_element_type=F32)


def bands(length):
    out = []
    off = 0
    for b in range(length // QB):
        ks, ke = max(0, QB * b - REACH), QB * (b + 1)
        out.append((b, ks, ke, off))
        off += ke - ks
    return out, off


def unit_of(x):
    mean = jnp.sum(x, axis=-1, keepdims=True) * (1.0 / D)
    centered = x - mean
    variance = jnp.sum(centered * centered, axis=-1, keepdims=True) * (1.0 / D)
    inverse = lax.rsqrt(variance + eps_norm)
    return centered * inverse, inverse


def norm_into(x_ref, gain, n_ref):
    for r in range(0, x_ref.shape[0], ROWS):
        unit, _ = unit_of(x_ref[r : r + ROWS, :].astype(F32))
        n_ref[r : r + ROWS, :] = (unit * gain).astype(BF)


def norm_back(dn_ref, x_ref, dy_ref, gain, out_ref, low_ref):
    grad = jnp.zeros((1, D), F32)
    for r in range(0, x_ref.shape[0], ROWS):
        unit, inverse = unit_of(x_ref[r : r + ROWS, :].astype(F32))
        dn = dn_ref[r : r + ROWS, :]
        grad = grad + jnp.sum(dn * unit, axis=0, keepdims=True)
        e = dn * gain
        first = jnp.sum(e, axis=-1, keepdims=True) * (1.0 / D)
        cross = jnp.sum(e * unit, axis=-1, keepdims=True) * (1.0 / D)
        total = dy_ref[r : r + ROWS, :].astype(F32) + (e - first - unit * cross) * inverse
        if out_ref is not None:
            out_ref[r : r + ROWS, :] = total
        if low_ref is not None:
            low_ref[r : r + ROWS, :] = total.astype(BF)
    return grad


def make_bias(seg_ref, bias_ref, length):
    columns = []
    for b in range(length // QB):
        row = seg_ref[:, QB * b : QB * b + QB].astype(F32)
        columns.append(jnp.broadcast_to(row, (QB, QB)).T)
    for b, ks, ke, off in bands(length)[0]:
        row = seg_ref[:, QB * b : QB * b + QB].astype(F32)
        for k in range(ks, ke, QB):
            allowed = columns[k // QB] == row
            if k == QB * b:
                keys = lax.broadcasted_iota(jnp.int32, (QB, QB), 0)
                allowed = allowed & (keys <= lax.broadcasted_iota(jnp.int32, (QB, QB), 1))
            bias_ref[off + k - ks : off + k - ks + QB, :] = jnp.where(allowed, 0.0, neg_large)


def head_masked(pair_of, scale, dst_ref):
    lane = lax.broadcasted_iota(jnp.int32, (1, PAIR), 1)
    for p in range(PAIRS):
        for b in range(dst_ref.shape[1]):
            pair = pair_of(p, b)
            for member in (0, 1):
                mask = jnp.where(lane // HEAD_DIM == member, scale, 0.0).astype(BF)
                dst_ref[p, b, QB * member : QB * member + QB, :] = pair * mask


def attend(pk, k, length):
    q2, vT, bias, ss, pt, attT = k["q2"], k["vT"], k["bias"], k["ss"], k["pt"], k["attT"]
    vT[...] = pk[:, 2 * D :].T
    head_masked(lambda p, b: pk[QB * b : QB * b + QB, PAIR * p : PAIR * p + PAIR], HEAD_DIM ** (-0.5), q2)
    places = bands(length)[0]
    for p in range(PAIRS):
        lo = D + PAIR * p
        for b, ks, ke, off in places:
            seen = bias[off : off + ke - ks, :]
            products = dot(pk[ks:ke, lo : lo + PAIR], q2[p, b], 1, 1)
            ss[p, off : off + ke - ks, :] = products + jnp.concatenate([seen, seen], 1)
    for p in range(PAIRS):
        for b, ks, ke, off in places:
            for m in (0, 1):
                cols = slice(QB * m, QB * m + QB)
                scores = ss[p, off : off + ke - ks, cols]
                lifted = jnp.exp(scores - jnp.max(scores, axis=0, keepdims=True))
                share = 1.0 / jnp.sum(lifted, axis=0, keepdims=True)
                pt[p, off : off + ke - ks, cols] = (lifted * share).astype(BF)
    for p in range(PAIRS):
        for b, ks, ke, off in places:
            both = dot(vT[PAIR * p : PAIR * p + PAIR, ks:ke], pt[p, off : off + ke - ks, :])
            for m in (0, 1):
                lo = HEAD_DIM * m
                part = both[lo : lo + HEAD_DIM, QB * m : QB * m + QB].astype(BF)
                attT[PAIR * p + lo : PAIR * p + lo + HEAD_DIM, QB * b : QB * b + QB] = part


def attend_back(pk, pt, da, k, length):
    d2, q2, kT, ss, ds, dqT, dk, dv, dpk = (k[n] for n in ("d2", "q2", "kT", "ss", "ds", "dqT", "dk", "dv", "dpk"))
    head_masked(lambda p, b: pk[QB * b : QB * b + QB, PAIR * p : PAIR * p + PAIR], HEAD_DIM ** (-0.5), q2)
    head_masked(lambda p, b: da[QB * b : QB * b + QB, PAIR * p : PAIR * p + PAIR], 1.0, d2)
    kT[...] = pk[:, D : 2 * D].T
    places = bands(length)[0]
    for p in range(PAIRS):
        lo = 2 * D + PAIR * p
        for b, ks, ke, off in places:
            ss[p, off : off + ke - ks, :] = dot(pk[ks:ke, lo : lo + PAIR], d2[p, b], 1, 1)
    for p in range(PAIRS):
        for b, ks, ke, off in places:
            for m in (0, 1):
                cols = slice(QB * m, QB * m + QB)
                chances = pt[p, off : off + ke - ks, cols].astype(F32)
                grad = ss[p, off : off + ke - ks, cols]
                inner = jnp.sum(chances * grad, axis=0, keepdims=True)
                ds[p, off : off + ke - ks, cols] = (chances * (grad - inner)).astype(BF)
    for p in range(PAIRS):
        lo = PAIR * p
        for b, ks, ke, off in places:
            grad = ds[p, off : off + ke - ks, :]
            both = dot(kT[lo : lo + PAIR, ks:ke], grad)
            for m in (0, 1):
                rows = slice(HEAD_DIM * m, HEAD_DIM * m + HEAD_DIM)
                part = both[rows, QB * m : QB * m + QB] * HEAD_DIM ** (-0.5)
                dqT[lo + HEAD_DIM * m : lo + HEAD_DIM * m + HEAD_DIM, QB * b : QB * b + QB] = part
            gk, gv = dot(grad, q2[p, b]), dot(pt[p, off : off + ke - ks, :], d2[p, b])
            n = ke - ks - QB
            if n:
                dk[ks : ks + n, lo : lo + PAIR] += gk[:n]
                dv[ks : ks + n, lo : lo + PAIR] += gv[:n]
            dk[ks + n : ke, lo : lo + PAIR] = gk[n:]
            dv[ks + n : ke, lo : lo + PAIR] = gv[n:]
    dpk[:, 0:D] = dqT[...].T.astype(BF)
    dpk[:, D : 2 * D] = dk[...].astype(BF)
    dpk[:, 2 * D :] = dv[...].astype(BF)


def attention_half(x, k, wide, gain, length):
    norm_into(x, gain[0:1, :], k["n1"])
    make_bias(k["seg"], k["bias"], length)
    pk = k["pk"]
    pk[...] = dot(k["n1"][...], wide[:, : 3 * D]).astype(BF)
    attend(pk, k, length)
    mid = k["mid"]
    mid[...] = x[...].astype(F32) + dot(k["attT"][...], wide[:, 3 * D :], 0, 0)
    norm_into(mid, gain[1:2, :], k["n2"])


def feed_forward(k, up, down, length, out):
    c0 = 0.7978845608028654
    c1 = 0.044715
    hs, act, gp, n2 = k["hs"], k["act"], k["gp"], k["n2"]
    for i, c in enumerate(range(0, FF, CHUNK)):
        hs[i % 2] = dot(n2[...], up[:, c : c + CHUNK])
        for r in range(0, length, ROWS):
            v = hs[i % 2, r : r + ROWS, :]
            v2 = v * v
            th = jnp.tanh(v * (c0 + (c0 * c1) * v2))
            half = 0.5 * v
            act[r : r + ROWS, c : c + CHUNK] = (half + half * th).astype(BF)
            slope = 0.5 + 0.5 * th + half * (1.0 - th * th) * (c0 + (3.0 * c0 * c1) * v2)
            gp[r : r + ROWS, c : c + CHUNK] = slope.astype(BF)
    out(k["mid"][...] + dot(act[...], down[...]))


def feed_back(dy, k, up, down, gain, emit):
    act, n2, dh, dn = k["act"], k["n2"], k["dh"], k["dn"]
    emit.down(lambda lo, n: dot(act[:, lo : lo + n], dy[...], 0, 0))
    for c in range(0, FF, CHUNK):
        grad = dot(dy[...], down[c : c + CHUNK, :], 1, 1) * k["gp"][:, c : c + CHUNK].astype(F32)
        dh[:, c : c + CHUNK] = grad.astype(BF)
    emit.up(lambda lo, n: dot(n2[...], dh[:, lo : lo + n], 0, 0))
    dn[...] = dot(dh[...], up[...], 1, 1)
    grad = norm_back(dn, k["mid"], dy, gain[1:2, :], k["dmid"], k["dmb"])
    return grad


def attention_back(k, wide, emit, length):
    dmb, da, dpk = k["dmb"], k["da"], k["dpk"]
    da[...] = dot(dmb[...], wide[:, 3 * D :], 1, 1).astype(BF)
    attend_back(k["pk"], k["pt"], da, k, length)

    n1 = k["n1"]
    zero = dot(n1[...], dpk[:, :HALF], 0, 0)
    emit.wide(zero[:, :D], dot(n1[...], dpk[:, HALF:], 0, 0), 0)
    emit.wide(zero[:, D:], dot(k["attT"][...], dmb[...]), D)


def input_back(x, k, wide, gain, out, low):
    k["dn"][...] = dot(k["dpk"][...], wide[:, : 3 * D], 1, 1)
    return norm_back(k["dn"], x, k["dmid"], gain[0:1, :], out, low)


def spread_bits(index, order):
    out = 0
    for k, bit in enumerate(order):
        out = out | (((index >> k) & 1) << bit)
    return out


def gather_bits(index, order):
    out = 0
    for k, bit in enumerate(order):
        out = out | (((index >> bit) & 1) << k)
    return out


class Plan:
    def __init__(self, mesh):
        self.count = mesh.shape["dp"]
        self.bits = self.count.bit_length() - 1
        rest = tuple(range(4, self.bits))
        x, y, near, far = 0, 1, 2, 3
        gathers = (
            ((y, far, x, near), (far, near, y, x)),
            ((near, x, far, y), (far, x, near, y)),
            ((near, far, y, x), (far, x, y, near)),
        )
        scatters = (((y, x, near, far), (near, y, x, far)), ((near, x, y, far), (y, x, far, near)))
        self.gather_orders = tuple(tuple(rest + o for o in pair) for pair in gathers)
        self.scatter_orders = tuple(tuple(o + rest for o in pair) for pair in scatters)
        self.thin = (D // self.count) % 8 != 0
        self.slabs = 1 if self.thin else self.count
        self.rows = D // self.slabs

    def source(self, flow, block, place, me):
        return spread_bits(place, self.gather_orders[flow][block]) ^ me

    def place(self, block, half, device, me):
        order = tuple(reversed(self.scatter_orders[block][half]))
        return gather_bits(device, order) ^ gather_bits(me, order)

    def weight_shape(self, flow):
        return (D, WIDE) if flow < 2 else (FF, D)

    def grad_shapes(self):
        if self.thin:
            return {"gp_": [((D, WIDE), BF)], "gq_": [((D, WIDE), BF), ((FF, D), BF)]}
        n, r = self.slabs, self.rows
        return {"gp_": [((n, 1, r, HALF), BF)] * 2, "gq_": [((n, 2, r, HALF), BF)] * 2}


class Emit:
    def __init__(self, plan, block, first, second):
        self.plan, self.first, self.second = plan, first, second
        self.core, me = lax.axis_index("pipe"), lax.axis_index("dp")
        if plan.thin:
            return
        leading = self.core == 0
        places = [[plan.place(block, half, s, me) for s in range(plan.slabs)] for half in (0, 1)]
        self.places = [
            [jnp.where(leading, places[which][s], places[1 - which][s]) for s in range(plan.slabs)] for which in (0, 1)
        ]

    def halves(self, zero, one, put, first=0):
        leading = self.core == 0
        for which, value in ((0, jnp.where(leading, zero, one)), (1, jnp.where(leading, one, zero))):
            value = value.astype(BF)
            for s in range(value.shape[0]):
                put(which, self.places[which][first + s], value[s])

    def wide(self, zero, one, at):
        plan = self.plan
        if plan.thin:
            self.first[0][:, at : at + D] = zero.astype(BF)
            self.first[0][:, HALF + at : HALF + at + D] = one.astype(BF)
            return
        shape = (plan.slabs, plan.rows, D)

        def put(which, place, value):
            self.first[which][place, 0, :, at : at + D] = value

        self.halves(zero.reshape(shape), one.reshape(shape), put)

    def up(self, make):
        plan = self.plan
        if plan.thin:
            for lo in (0, HALF):
                self.second[0][:, lo : lo + HALF] = make(lo, HALF).astype(BF)
            return
        shape = (plan.slabs, plan.rows, HALF)

        def put(which, place, value):
            self.second[which][place, 0, :, :] = value

        self.halves(make(0, HALF).reshape(shape), make(HALF, HALF).reshape(shape), put)

    def down(self, make):
        plan = self.plan
        for lo in range(0, FF, HALF):
            value = make(lo, HALF)
            if plan.thin:
                self.second[1][lo : lo + HALF, :] = value.astype(BF)
                continue
            value = value.reshape(HALF // (4 * plan.rows), 2, 2 * plan.rows, D)

            def put(which, place, value, r=plan.rows):
                self.second[which][place, 1, :, 0:D] = value[:r]
                self.second[which][place, 1, :, D : 2 * D] = value[r:]

            self.halves(value[:, 0], value[:, 1], put, lo // (4 * plan.rows))


def limit(size):
    return pltpu.CompilerParams(vmem_limit_bytes=int(size) + 6 * 2**20)


def run_kernel(name, body, block, inputs, outs, scratch, cost, after=()):
    arrays = {n: v if isinstance(v, tuple) else (v, ()) for n, v in inputs.items()}
    size = sum(math.prod(shape) * jnp.dtype(dtype).itemsize for shape, dtype in scratch.values())

    def kernel(*refs):
        names = list(arrays) + [None] * len(after) + list(outs) + list(scratch)
        k = dict(zip(names, refs))
        core = lax.axis_index("pipe")
        for n, (_, index) in arrays.items():
            if index:
                k[n] = k[n].at[tuple(core if i == "core" else i for i in index)]
        gain = None
        if "gains" in arrays:
            gain = jnp.where(core == block, k["gains"][...], k["gains_got"][...])
        body(k, gain)

    result = pl.pallas_call(
        kernel,
        name=name,
        out_shape=[struct(*v) for v in outs.values()],
        in_specs=[VM] * len(arrays) + [ANY] * len(after),
        out_specs=[VM] * len(outs),
        scratch_shapes=[pltpu.VMEM(*v) for v in scratch.values()],
        compiler_params=limit(size),
        cost_estimate=pl.CostEstimate(flops=int(cost * 1e10), bytes_accessed=8, transcendentals=0),
    )(*[v for v, _ in arrays.values()], *after)
    return dict(zip(outs, result))


def small_kernel(name, kernel, outs, *inputs, after=()):
    def run(*refs):
        kernel(*refs[: len(inputs)], *refs[len(inputs) + len(after) :])

    return pl.pallas_call(
        run,
        name=name,
        out_shape=outs,
        in_specs=[VM] * len(inputs) + [ANY] * len(after),
        out_specs=[VM] * len(outs),
        compiler_params=limit(0),
    )(*inputs, *after)


def arrange(plan, flow, own, got, after):
    n, each = plan.slabs, plan.slabs // 2

    def kernel(a0, b0, a1, b1, zero, one):
        core, me = lax.axis_index("pipe"), lax.axis_index("dp")

        def move(first, second, dst, block):
            for place in range(n):
                src = first if place < each else second
                dst[plan.source(flow, block, place, me)] = src[place % each]

        @pl.when(core == 0)
        def _():
            move(a0, b0, zero, 0)
            move(a1, b1, one, 1)

        @pl.when(core != 0)
        def _():
            move(a0, b0, one, 1)
            move(a1, b1, zero, 0)

    like = struct((n, *own[0].shape[1:]), BF)
    out = small_kernel("arrange", kernel, [like, like], *own, *got, after=after)
    return [v.reshape(plan.weight_shape(flow)) for v in out]


def shapes(L):
    nb = bands(L)[1]
    return dict(
        n1=((L, D), BF),
        pk=((L, 3 * D), BF),
        pt=((PAIRS, nb, 2 * QB), BF),
        attT=((D, L), BF),
        mid=((L, D), F32),
        n2=((L, D), BF),
        act=((L, FF), BF),
        gp=((L, FF), BF),
        q2=((PAIRS, L // QB, 2 * QB, PAIR), BF),
        d2=((PAIRS, L // QB, 2 * QB, PAIR), BF),
        vT=((D, L), BF),
        bias=((nb, QB), F32),
        ss=((PAIRS, nb, 2 * QB), F32),
        ds=((PAIRS, nb, 2 * QB), BF),
        hs=((2, L, CHUNK), F32),
        dh=((L, FF), BF),
        dn=((L, D), F32),
        dmid=((L, D), F32),
        dmb=((L, D), BF),
        kT=((D, L), BF),
        dqT=((D, L), F32),
        dk=((L, D), F32),
        dv=((L, D), F32),
        dpk=((L, 3 * D), BF),
        da=((L, D), BF),
        x1=((L, D), F32),
        y2=((L, D), F32),
        dx=((L, D), F32),
        dxb=((L, D), BF),
        dg=((1, D), F32),
    )


def swap_cores(block):
    return lax.ppermute(block, "pipe", [(0, 1), (1, 0)])


def swap(block, bits):
    n = lax.axis_size("dp")
    route = [(c * n + i, c * n + (i ^ (1 << bits[c]))) for c in range(2) for i in range(n)]
    return lax.ppermute(block, ("pipe", "dp"), route)


def join(a, b, after):
    def kernel(a, b, out):
        n = a.shape[0]
        out[:n] = a[...]
        out[n:] = b[...]

    return small_kernel("join", kernel, [struct((2 * a.shape[0], *a.shape[1:]), a.dtype)], a, b, after=after)[0]


def gather(plan, shards, early):
    held = [shard[None] for shard in shards]
    last = ()
    for turn in range(plan.bits):
        came = [swap(held[f], (orders[0][turn], orders[1][turn])) for f, orders in enumerate(plan.gather_orders)]
        last = (*last, early) if turn == 1 else last
        if turn < plan.bits - 1:
            for f in range(3):
                held[f] = join(held[f], came[f], last)
                last = (held[f],)
    return [(a, b) for a, b in zip(held, came)]


def added(a, b):
    return (a.astype(F32) + b.astype(F32)).astype(BF)


def add_split(pairs, after=()):
    def kernel(*refs):
        outs, n, at = refs[-2:], refs[-1].shape[0], 0
        for k in range(0, len(refs) - 2, 2):
            a, b = refs[k : k + 2]
            wide = a.shape[1]
            for i, out in enumerate(outs):
                for j in range(n):
                    out[j, at : at + wide] = added(a[n * i + j], b[n * i + j])
            at += wide

    n, _, r, width = pairs[0][0].shape
    outs = [struct((n // 2, sum(a.shape[1] for a, _ in pairs), r, width), BF)] * 2
    return small_kernel("add_split", kernel, outs, *[v for pair in pairs for v in pair], after=after)


def behind(value, *others):
    return lax.optimization_barrier((value, *others))[0]


class Scatter:
    def __init__(self, plan, block):
        self.orders, self.turn, self.pairs = plan.scatter_orders[block], 0, []

    def exchange(self, pairs, turn, after):
        keep, send = add_split(pairs, after)
        return keep, swap(send, (self.orders[0][turn], self.orders[1][turn]))

    def begin(self, parts, *after):
        self.pairs = [self.exchange(parts, 0, after)]
        self.turn = 1
        return self.pairs[0][0]

    def part(self, mine, came, *after):
        self.pairs.append(self.exchange([(mine, came)], 0, after))
        self.turn = 1
        return self.pairs[-1][0]

    def step(self, *after):
        if self.turn == 1:
            self.pairs.reverse()
        self.pairs = [self.exchange(self.pairs, self.turn, after)]
        self.turn += 1
        return self.pairs[0][0]


def owners(zero, one):
    zero, one = ([pair for sums in v for pair in sums.pairs] for v in (zero, one))

    def total(refs):
        return jnp.concatenate([a[0].astype(F32) + b[0].astype(F32) for a, b in zip(refs[0::2], refs[1::2])], 0)

    def kernel(*refs):
        own, send = refs[-2:]
        a, b = total(refs[: 2 * len(zero)]), total(refs[2 * len(zero) : -2])
        leading = lax.axis_index("pipe") == 0
        own[...] = jnp.where(leading, a, b).astype(BF)
        send[...] = jnp.where(leading, b, a).astype(BF)

    like = struct((3, *zero[0][0].shape[2:]), BF)
    return small_kernel("owners", kernel, [like, like], *[v for pair in zero + one for v in pair])


def thin_arrange(plan, flow, own, got, after):
    core, me = lax.axis_index("pipe"), lax.axis_index("dp")
    index = jnp.arange(plan.count, dtype=jnp.int32)
    out = []
    for block in (0, 1):
        held = jnp.where(core == block, jnp.concatenate(own, 0), jnp.concatenate(got, 0))
        held = jnp.zeros_like(held).at[plan.source(flow, block, index, me)].set(held)
        out.append(held.reshape(plan.weight_shape(flow)))
    return out


def thin_halves(plan, block, grads, bundle):
    core, me = lax.axis_index("pipe"), lax.axis_index("dp")
    n, r = plan.count, D // plan.count
    parts = grads[0].reshape(n, r, 2, HALF).transpose(2, 0, 1, 3)
    parts = parts[:, :, None]
    if bundle:
        down = grads[1].reshape(n, 2, 2, r, D).transpose(1, 0, 3, 2, 4).reshape(2, n, 1, r, HALF)
        parts = jnp.concatenate([parts, down], 2)
    index = jnp.arange(n, dtype=jnp.int32)
    halves = [jnp.zeros_like(parts[h]).at[plan.place(block, h, index, me)].set(parts[h]) for h in (0, 1)]
    return [jnp.where(core == 0, halves[i], halves[1 - i]) for i in (0, 1)]


def lanes(values):
    lane = lax.broadcasted_iota(jnp.int32, (1, D), 1)
    row = jnp.zeros((1, D), F32)
    for place, value in values:
        row = row + jnp.where(lane == place, value, 0.0)
    return row


def square_sum(v):
    return jnp.sum(jnp.sum(v * v, axis=1, keepdims=True), axis=0, keepdims=True)


def moments(master, grad, first, second):
    drift = beta * first + (1.0 - beta) * grad
    spread = beta * second + (1.0 - beta) * grad * grad
    correction = 1.0 - beta**STEP
    update = drift / correction / (jnp.sqrt(spread / correction) + eps_adam) + decay * master
    return (drift, spread, update)


def update_moments(plan, own, got, masters, firsts, seconds, gain_own, gain_got):
    r = D // plan.count

    def kernel(own, got, *refs):
        masters, firsts, seconds, (gain_own, gain_got) = refs[0:4], refs[4:8], refs[8:12], refs[12:14]
        drifts, spreads, updates, small = refs[14:18], refs[18:22], refs[22:26], refs[26]
        leading = lax.axis_index("pipe") == 0
        a, b = own[...].astype(F32), got[...].astype(F32)
        h = (jnp.where(leading, a, b), jnp.where(leading, b, a))
        whole, tail = slice(None), 3 * D - HALF
        grads = [
            [((whole, slice(0, HALF)), h[0][0]), ((whole, slice(HALF, 3 * D)), h[1][0][:, :tail])],
            [((whole, slice(0, D)), h[1][0][:, tail:])],
            [((whole, slice(HALF * i, HALF * i + HALF)), h[i][1]) for i in (0, 1)],
            [
                ((slice(r * (2 * i + q), r * (2 * i + q) + r), whole), h[i][2][:, D * q : D * q + D])
                for i in (0, 1)
                for q in (0, 1)
            ],
        ]
        sums = [(m, square_sum(masters[m][...])) for m in range(4)]
        for m in range(4):
            total = jnp.zeros((1, 1), F32)
            for at, grad in grads[m]:
                drift, spread, update = moments(masters[m][at], grad, firsts[m][at], seconds[m][at])
                drifts[m][at], spreads[m][at], updates[m][at] = drift, spread, update
                total = total + square_sum(update)
            sums.append((4 + m, total))
        row = lanes(sums)
        gain = gain_own[...] + gain_got[...]
        for i in range(plan.count):
            small[i, 0:1, :] = row
            small[i, 1:3, :] = gain

    like = [struct(m.shape, F32) for m in masters]
    outs = like * 3 + [struct((plan.count, 3, D), F32)]
    res = small_kernel("moments", kernel, outs, own, got, *masters, *firsts, *seconds, gain_own, gain_got)
    return res[0:4], res[4:8], res[8:12], res[12]


def finish(small, masters, updates, gains, gain_first, gain_second):
    def kernel(parts, m0, m1, m2, m3, u0, u1, u2, u3, gains, gf, gs, *outs):
        new, low, (gain_drift, gain_spread, gain_new, pairs) = outs[0:4], outs[4:8], outs[8:12]
        small = jnp.sum(parts[...], axis=0)
        weight = [jnp.sqrt(small[0:1, i : i + 1]) for i in range(4)]
        step = [jnp.sqrt(small[0:1, 4 + i : 5 + i]) for i in range(4)]
        for i, (m, u) in enumerate(zip((m0, m1, m2, m3), (u0, u1, u2, u3))):
            value = m[...] - rate * (weight[i] / step[i]) * u[...]
            new[i][...] = value
            low[i][...] = value.astype(BF)
        drift, spread, update = moments(gains[...], small[1:3, :], gf[...], gs[...])
        gain_drift[...] = drift
        gain_spread[...] = spread
        gain_weight = jnp.sqrt(jnp.sum(gains[...] * gains[...], axis=1, keepdims=True))
        gain_step = jnp.sqrt(jnp.sum(update * update, axis=1, keepdims=True))
        gain_new[...] = gains[...] - rate * (gain_weight / gain_step) * update
        for i in range(4):
            pairs[0:1, i : i + 1] = weight[i]
            pairs[1:2, i : i + 1] = step[i]
        for i in range(2):
            pairs[0:1, 4 + i : 5 + i] = gain_weight[i : i + 1, :]
            pairs[1:2, 4 + i : 5 + i] = gain_step[i : i + 1, :]

    outs = [struct(m.shape, F32) for m in masters] + [struct(m.shape, BF) for m in masters]
    outs += [struct((2, D), F32)] * 3 + [struct((2, 6), F32)]
    res = small_kernel("finish", kernel, outs, small, *masters, *updates, gains, gain_first, gain_second)
    return [*res[:-1], res[-1].T]


def lay_results(own, got):
    def kernel(own, got, out, done):
        core = lax.axis_index("pipe")
        out[core] = own[...]
        out[1 - core] = got[...]
        done[...] = jnp.zeros(done.shape, F32)

    return small_kernel("lay_results", kernel, [struct((2, *own.shape), F32), struct((8, 128), F32)], own, got)


def solution(mesh):
    plan = Plan(mesh)

    def per_device(
        tokens,
        prompts,
        cotangent,
        segments,
        weight_in,
        weight_out,
        weight_up,
        weight_down,
        first_in,
        first_out,
        first_up,
        first_down,
        second_in,
        second_out,
        second_up,
        second_down,
        gains,
        gain_first,
        gain_second,
    ):
        L = tokens.shape[2]
        sh = shapes(L)
        masters = (weight_in[0], weight_out[0], weight_up[0], weight_down[0])
        firsts = (first_in[0], first_out[0], first_up[0], first_down[0])
        seconds = (second_in[0], second_out[0], second_up[0], second_down[0])

        low = [m.astype(BF) for m in masters]
        wide = jnp.concatenate(low[:2], 1)
        gains_got = swap_cores(gains[0])
        flows = gather(plan, (wide, low[2], low[3].reshape(4, -1, D)), gains_got)
        put = thin_arrange if plan.thin else arrange
        both = [None] * 3

        def place_flow(flow, *after):
            both[flow] = put(plan, flow, flows[flow], tuple(swap_cores(v) for v in flows[flow]), after)

        place_flow(0)

        def weights(block, *which):
            return {n: both[f][block] for f, n in enumerate(("wide", "up", "down")) if n in which}

        def pick(*names):
            return {n: sh[n] for n in names}

        def there(source, *names):
            return {n: source[n] for n in names}

        gain_refs = {"gains": gains[0], "gains_got": gains_got}
        grads = plan.grad_shapes()
        g_first = {f"p{i}": v for i, v in enumerate(grads["gp_"])}
        g_second = {f"q{i}": v for i, v in enumerate(grads["gq_"])}
        x0 = {"x": (tokens, ("core", 0))}
        seg = {"seg": (segments[:, :, None], ("core", 0))}

        def refs_of(k, table):
            return [k[n] for n in table]

        def traded(source, table, block, bundle):
            values = [source[n] for n in table]
            if plan.thin:
                values = thin_halves(plan, block, values, bundle)
            return values[0], swap_cores(values[1])

        def body(k, gain):
            attention_half(k["x"], k, k["wide"], gain, L)

        attention_scratch = pick("q2", "vT", "bias", "ss")
        one = run_kernel(
            "extractor_attention", body, 0, {**gain_refs, **x0, **seg, "pr": (prompts, ("core", 0)), **weights(0, "wide")},
            pick("n1", "pk", "pt", "attT", "mid", "n2"), attention_scratch, 1e-9,
        )

        place_flow(1, one["n2"])
        place_flow(2, one["n2"])

        def body(k, gain):
            def out(value):
                k["x1"][...] = value.astype(BF).astype(F32) + k["pr"][...].astype(F32)

            feed_forward(k, k["up"], k["down"], L, out)

        two = run_kernel(
            "extractor_feed", body, 0,
            {**there(one, "n2", "mid"), "pr": (prompts, ("core", 0)), **weights(0, "up", "down")},
            pick("act", "gp", "x1"), pick("hs"), 3.2,
        )

        def body(k, gain):
            attention_half(k["x1"], k, k["wide"], gain, L)

        three = run_kernel(
            "generator_attention", body, 1, {**gain_refs, **there(two, "x1"), **seg, **weights(1, "wide")},
            pick("n1", "pk", "pt", "attT", "mid", "n2"), attention_scratch, 1e-9,
        )

        def body(k, gain):
            def out(value):
                k["y2"][...] = value

            feed_forward(k, k["up"], k["down"], L, out)
            emit = Emit(plan, 1, None, refs_of(k, g_second))
            k["dg"][...] = feed_back(k["dy"], k, k["up"], k["down"], gain, emit)

        cot = {"dy": (cotangent, ("core", 0))}
        four = run_kernel(
            "generator_feed", body, 1,
            {**gain_refs, **there(three, "mid", "n2"), **cot, **weights(1, "up", "down")},
            {**pick("y2", "dmid", "dmb", "dg"), **g_second}, pick("act", "gp", "hs", "dh", "dn"), 10,
        )

        second_one = traded(four, g_second, 1, 1)
        back_scratch = pick("q2", "d2", "kT", "ss", "ds", "dqT", "dk", "dv", "da")

        def body(k, gain):
            emit = Emit(plan, 1, refs_of(k, g_first), None)
            attention_back(k, k["wide"], emit, L)

        five = run_kernel(
            "generator_attention_back", body, 1,
            {**there(four, "dmb"), **there(three, "attT", "pk", "pt", "n1"), **weights(1, "wide")},
            {**g_first, **pick("dpk")}, back_scratch, 6,
        )
        sum_one = Scatter(plan, 1)
        first_one = traded(five, g_first, 1, 0)

        def body(k, gain):
            k["dg"][...] = input_back(k["x1"], k, k["wide"], gain, None, k["dxb"])

        six = run_kernel(
            "generator_input_back", body, 1,
            {**gain_refs, **there(five, "dpk"), **there(four, "dmid"), **there(two, "x1"), **weights(1, "wide")},
            pick("dg", "dxb"), pick("dn"), 3,
        )
        last = sum_one.begin([first_one, second_one], six["dxb"])

        def body(k, gain):
            emit = Emit(plan, 0, None, refs_of(k, g_second))
            k["dg"][...] = feed_back(k["dxb"], k, k["up"], k["down"], gain, emit)

        seven = run_kernel(
            "extractor_feed_back", body, 0,
            {**gain_refs, **there(six, "dxb"), **there(two, "act", "gp"), **there(one, "n2", "mid"), **weights(0, "up", "down")},
            {**g_second, **pick("dmid", "dmb", "dg")}, pick("dh", "dn"), 7, after=[last],
        )
        second_zero = traded(seven, g_second, 0, 1)

        def body(k, gain):
            emit = Emit(plan, 0, refs_of(k, g_first), None)
            attention_back(k, k["wide"], emit, L)

        eight = run_kernel(
            "extractor_attention_back", body, 0,
            {**there(seven, "dmb"), **there(one, "attT", "pk", "pt", "n1"), **weights(0, "wide")},
            {**g_first, **pick("dpk")}, back_scratch, 6,
        )
        first_zero = traded(eight, g_first, 0, 0)
        sum_zero = Scatter(plan, 0)
        last = sum_zero.begin([first_zero, second_zero], eight["dpk"])
        last = sum_one.step(last)

        def body(k, gain):
            dg = input_back(k["x"], k, k["wide"], gain, k["dx"], None)
            leading = lax.axis_index("pipe") == 0
            k["own"][...] = jnp.where(leading, k["dx"][...], k["y2"][...])
            k["send"][...] = jnp.where(leading, k["y2"][...], k["dx"][...])
            for i, (zero, one) in enumerate(((dg, k["g10"][...]), (k["g01"][...], k["g11"][...]))):
                k["gain_own"][i : i + 1, :] = jnp.where(leading, zero, one)
                k["gain_send"][i : i + 1, :] = jnp.where(leading, one, zero)

        nine = run_kernel(
            "extractor_input_back", body, 0,
            {**gain_refs, **there(eight, "dpk"), **there(seven, "dmid"), **x0, **weights(0, "wide"), **there(four, "y2"),
             "g01": seven["dg"], "g10": six["dg"], "g11": four["dg"]},
            {"own": sh["dx"], "send": sh["dx"], "gain_own": ((2, D), F32), "gain_send": ((2, D), F32)},
            pick("dn", "dx"), 3, after=[last],
        )
        gain_got = swap_cores(nine["gain_send"])
        result, laid = lay_results(nine["own"], swap_cores(nine["send"]))
        section_result = result[None, :, None]
        last = sum_zero.step(nine["gain_own"], gain_got)
        last = sum_one.step(last)
        last = sum_zero.step(last, laid)
        while min(sum_one.turn, sum_zero.turn) < plan.bits:
            for sums in (sum_one, sum_zero):
                if sums.turn < plan.bits:
                    last = sums.step(last)
        own, send = owners((sum_zero,), (sum_one,))
        grad_got = swap_cores(send)

        drifts, spreads, updates, small = update_moments(
            plan, own, grad_got, masters, firsts, seconds, nine["gain_own"], gain_got
        )
        small = lax.all_to_all(small, "dp", 0, 0)
        done = finish(small, masters, updates, gains[0], gain_first[0], gain_second[0])
        return (
            section_result,
            *[v[None] for v in (*drifts, *spreads)],
            *[v[None] for v in done],
        )

    rows = P(None, "dp", None, None)
    matrix = P("pipe", "dp", None)
    gain = P("pipe", None, None)
    in_specs = (rows, rows, rows, P(None, "dp", None)) + (matrix,) * 12 + (gain,) * 3
    out_specs = (P("pipe", None, "dp", None, None),) + (matrix,) * 16 + (gain,) * 4
    return jax.shard_map(
        per_device, mesh=mesh, in_specs=in_specs, out_specs=out_specs, check_vma=False
    )
```

```python
import math

import jax
import jax.numpy as jnp
from jax import lax
from jax.experimental import pallas as pl
from jax.experimental.pallas import tpu as pltpu
from jax.sharding import PartitionSpec as P

D = 384
FF = 1536
HEADS = 6
HEAD_DIM = 64
STEP = 3
BF = jnp.bfloat16
F32 = jnp.float32

rate = 0.3
beta = 0.5
eps_adam = 1e-06
decay = 0.01
eps_norm = 1e-05
neg_large = -1e30

QB = 128
REACH = 256
ROWS = 64
CHUNK = 512
WIDE = 4 * D
HALF = WIDE // 2
PAIRS = HEADS // 2
PAIR = 2 * HEAD_DIM
VM = pl.BlockSpec(memory_space=pltpu.VMEM)
SM = pl.BlockSpec(memory_space=pltpu.SMEM)
ANY = pl.BlockSpec(memory_space=pl.ANY)
struct = jax.ShapeDtypeStruct


def dot(a, b, ca=1, cb=0):
    return lax.dot_general(a, b, (((ca,), (cb,)), ((), ())), preferred_element_type=F32)


def bands(length):
    out = []
    off = 0
    for b in range(length // QB):
        ks, ke = max(0, QB * b - REACH), QB * (b + 1)
        out.append((b, ks, ke, off))
        off += ke - ks
    return out, off


def unit_of(x):
    mean = jnp.sum(x, axis=-1, keepdims=True) * (1.0 / D)
    centered = x - mean
    variance = jnp.sum(centered * centered, axis=-1, keepdims=True) * (1.0 / D)
    inverse = lax.rsqrt(variance + eps_norm)
    return centered * inverse, inverse


def norm_into(x_ref, gain, n_ref):
    for r in range(0, x_ref.shape[0], ROWS):
        unit, _ = unit_of(x_ref[r : r + ROWS, :].astype(F32))
        n_ref[r : r + ROWS, :] = (unit * gain).astype(BF)


def norm_back(dn_ref, x_ref, dy_ref, gain, out_ref, low_ref):
    grad = jnp.zeros((1, D), F32)
    for r in range(0, x_ref.shape[0], ROWS):
        unit, inverse = unit_of(x_ref[r : r + ROWS, :].astype(F32))
        dn = dn_ref[r : r + ROWS, :]
        grad = grad + jnp.sum(dn * unit, axis=0, keepdims=True)
        e = dn * gain
        first = jnp.sum(e, axis=-1, keepdims=True) * (1.0 / D)
        cross = jnp.sum(e * unit, axis=-1, keepdims=True) * (1.0 / D)
        total = dy_ref[r : r + ROWS, :].astype(F32) + (e - first - unit * cross) * inverse
        if out_ref is not None:
            out_ref[r : r + ROWS, :] = total
        if low_ref is not None:
            low_ref[r : r + ROWS, :] = total.astype(BF)
    return grad


def make_bias(seg_ref, bias_ref, length):
    columns = []
    for b in range(length // QB):
        row = seg_ref[:, QB * b : QB * b + QB].astype(F32)
        columns.append(jnp.broadcast_to(row, (QB, QB)).T)
    for b, ks, ke, off in bands(length)[0]:
        row = seg_ref[:, QB * b : QB * b + QB].astype(F32)
        for k in range(ks, ke, QB):
            allowed = columns[k // QB] == row
            if k == QB * b:
                keys = lax.broadcasted_iota(jnp.int32, (QB, QB), 0)
                allowed = allowed & (keys <= lax.broadcasted_iota(jnp.int32, (QB, QB), 1))
            bias_ref[off + k - ks : off + k - ks + QB, :] = jnp.where(allowed, 0.0, neg_large)


def head_masked(pair_of, scale, dst_ref):
    lane = lax.broadcasted_iota(jnp.int32, (1, PAIR), 1)
    for p in range(PAIRS):
        for b in range(dst_ref.shape[1]):
            pair = pair_of(p, b)
            for member in (0, 1):
                mask = jnp.where(lane // HEAD_DIM == member, scale, 0.0).astype(BF)
                dst_ref[p, b, QB * member : QB * member + QB, :] = pair * mask


def attend(pk, k, length):
    q2, vT, bias, ss, pt, attT = k["q2"], k["vT"], k["bias"], k["ss"], k["pt"], k["attT"]
    vT[...] = pk[:, 2 * D :].T
    head_masked(lambda p, b: pk[QB * b : QB * b + QB, PAIR * p : PAIR * p + PAIR], HEAD_DIM ** (-0.5), q2)
    places = bands(length)[0]
    for p in range(PAIRS):
        lo = D + PAIR * p
        for b, ks, ke, off in places:
            seen = bias[off : off + ke - ks, :]
            products = dot(pk[ks:ke, lo : lo + PAIR], q2[p, b], 1, 1)
            ss[p, off : off + ke - ks, :] = products + jnp.concatenate([seen, seen], 1)
    for p in range(PAIRS):
        for b, ks, ke, off in places:
            for m in (0, 1):
                cols = slice(QB * m, QB * m + QB)
                scores = ss[p, off : off + ke - ks, cols]
                lifted = jnp.exp(scores - jnp.max(scores, axis=0, keepdims=True))
                share = 1.0 / jnp.sum(lifted, axis=0, keepdims=True)
                pt[p, off : off + ke - ks, cols] = (lifted * share).astype(BF)
    for p in range(PAIRS):
        for b, ks, ke, off in places:
            both = dot(vT[PAIR * p : PAIR * p + PAIR, ks:ke], pt[p, off : off + ke - ks, :])
            for m in (0, 1):
                lo = HEAD_DIM * m
                part = both[lo : lo + HEAD_DIM, QB * m : QB * m + QB].astype(BF)
                attT[PAIR * p + lo : PAIR * p + lo + HEAD_DIM, QB * b : QB * b + QB] = part


def attend_back(pk, pt, da, k, length):
    d2, q2, kT, ss, ds, dqT, dk, dv, dpk = (k[n] for n in ("d2", "q2", "kT", "ss", "ds", "dqT", "dk", "dv", "dpk"))
    head_masked(lambda p, b: pk[QB * b : QB * b + QB, PAIR * p : PAIR * p + PAIR], HEAD_DIM ** (-0.5), q2)
    head_masked(lambda p, b: da[QB * b : QB * b + QB, PAIR * p : PAIR * p + PAIR], 1.0, d2)
    kT[...] = pk[:, D : 2 * D].T
    places = bands(length)[0]
    for p in range(PAIRS):
        lo = 2 * D + PAIR * p
        for b, ks, ke, off in places:
            ss[p, off : off + ke - ks, :] = dot(pk[ks:ke, lo : lo + PAIR], d2[p, b], 1, 1)
    for p in range(PAIRS):
        for b, ks, ke, off in places:
            for m in (0, 1):
                cols = slice(QB * m, QB * m + QB)
                chances = pt[p, off : off + ke - ks, cols].astype(F32)
                grad = ss[p, off : off + ke - ks, cols]
                inner = jnp.sum(chances * grad, axis=0, keepdims=True)
                ds[p, off : off + ke - ks, cols] = (chances * (grad - inner)).astype(BF)
    for p in range(PAIRS):
        lo = PAIR * p
        for b, ks, ke, off in places:
            grad = ds[p, off : off + ke - ks, :]
            both = dot(kT[lo : lo + PAIR, ks:ke], grad)
            for m in (0, 1):
                rows = slice(HEAD_DIM * m, HEAD_DIM * m + HEAD_DIM)
                part = both[rows, QB * m : QB * m + QB] * HEAD_DIM ** (-0.5)
                dqT[lo + HEAD_DIM * m : lo + HEAD_DIM * m + HEAD_DIM, QB * b : QB * b + QB] = part
            gk, gv = dot(grad, q2[p, b]), dot(pt[p, off : off + ke - ks, :], d2[p, b])
            n = ke - ks - QB
            if n:
                dk[ks : ks + n, lo : lo + PAIR] += gk[:n]
                dv[ks : ks + n, lo : lo + PAIR] += gv[:n]
            dk[ks + n : ke, lo : lo + PAIR] = gk[n:]
            dv[ks + n : ke, lo : lo + PAIR] = gv[n:]
    dpk[:, 0:D] = dqT[...].T.astype(BF)
    dpk[:, D : 2 * D] = dk[...].astype(BF)
    dpk[:, 2 * D :] = dv[...].astype(BF)


def attention_half(x, k, wide, gain, length):
    norm_into(x, gain[0:1, :], k["n1"])
    make_bias(k["seg"], k["bias"], length)
    pk = k["pk"]
    pk[...] = dot(k["n1"][...], wide[:, : 3 * D]).astype(BF)
    attend(pk, k, length)
    mid = k["mid"]
    mid[...] = x[...].astype(F32) + dot(k["attT"][...], wide[:, 3 * D :], 0, 0)
    norm_into(mid, gain[1:2, :], k["n2"])


def feed_forward(k, up, down, length, out):
    c0 = 0.7978845608028654
    c1 = 0.044715
    hs, act, gp, n2 = k["hs"], k["act"], k["gp"], k["n2"]
    for i, c in enumerate(range(0, FF, CHUNK)):
        hs[i % 2] = dot(n2[...], up[:, c : c + CHUNK])
        for r in range(0, length, ROWS):
            v = hs[i % 2, r : r + ROWS, :]
            v2 = v * v
            th = jnp.tanh(v * (c0 + (c0 * c1) * v2))
            half = 0.5 * v
            act[r : r + ROWS, c : c + CHUNK] = (half + half * th).astype(BF)
            slope = 0.5 + 0.5 * th + half * (1.0 - th * th) * (c0 + (3.0 * c0 * c1) * v2)
            gp[r : r + ROWS, c : c + CHUNK] = slope.astype(BF)
    out(k["mid"][...] + dot(act[...], down[...]))


def feed_back(dy, k, up, down, gain, emit):
    act, n2, dh, dn = k["act"], k["n2"], k["dh"], k["dn"]
    emit.down(lambda lo, n: dot(act[:, lo : lo + n], dy[...], 0, 0))
    for c in range(0, FF, CHUNK):
        grad = dot(dy[...], down[c : c + CHUNK, :], 1, 1) * k["gp"][:, c : c + CHUNK].astype(F32)
        dh[:, c : c + CHUNK] = grad.astype(BF)
    emit.up(lambda lo, n: dot(n2[...], dh[:, lo : lo + n], 0, 0))
    dn[...] = dot(dh[...], up[...], 1, 1)
    grad = norm_back(dn, k["mid"], dy, gain[1:2, :], k["dmid"], k["dmb"])
    return grad


def attention_back(k, wide, emit, length):
    dmb, da, dpk = k["dmb"], k["da"], k["dpk"]
    da[...] = dot(dmb[...], wide[:, 3 * D :], 1, 1).astype(BF)
    attend_back(k["pk"], k["pt"], da, k, length)

    n1 = k["n1"]
    zero = dot(n1[...], dpk[:, :HALF], 0, 0)
    emit.wide(zero[:, :D], dot(n1[...], dpk[:, HALF:], 0, 0), 0)
    emit.wide(zero[:, D:], dot(k["attT"][...], dmb[...]), D)


def input_back(x, k, wide, gain, out, low):
    k["dn"][...] = dot(k["dpk"][...], wide[:, : 3 * D], 1, 1)
    return norm_back(k["dn"], x, k["dmid"], gain[0:1, :], out, low)


def spread_bits(index, order):
    out = 0
    for k, bit in enumerate(order):
        out = out | (((index >> k) & 1) << bit)
    return out


def gather_bits(index, order):
    out = 0
    for k, bit in enumerate(order):
        out = out | (((index >> bit) & 1) << k)
    return out


class Plan:
    def __init__(self, mesh):
        self.count = mesh.shape["dp"]
        self.bits = self.count.bit_length() - 1
        rest = tuple(range(4, self.bits))
        x, y, near, far = 0, 1, 2, 3
        gathers = (
            ((y, far, x, near), (far, near, y, x)),
            ((near, x, far, y), (far, x, near, y)),
            ((near, far, y, x), (far, x, y, near)),
        )
        scatters = (((y, x, near, far), (near, y, x, far)), ((near, x, far, y), (y, x, far, near)))
        self.gather_orders = tuple(tuple(rest + o for o in pair) for pair in gathers)
        self.scatter_orders = tuple(tuple(o + rest for o in pair) for pair in scatters)
        self.thin = (D // self.count) % 8 != 0
        self.slabs = 1 if self.thin else self.count
        self.rows = D // self.slabs

    def source(self, flow, block, place, me):
        return spread_bits(place, self.gather_orders[flow][block]) ^ me

    def place(self, block, half, device, me):
        order = tuple(reversed(self.scatter_orders[block][half]))
        return gather_bits(device, order) ^ gather_bits(me, order)

    def weight_shape(self, flow):
        return (D, WIDE) if flow < 2 else (FF, D)

    def grad_shapes(self):
        if self.thin:
            return {"gp_": [((D, WIDE), BF)], "gq_": [((D, WIDE), BF), ((FF, D), BF)]}
        n, r = self.slabs, self.rows
        return {"gp_": [((n, 1, r, HALF), BF)] * 2, "gq_": [((n, 2, r, HALF), BF)] * 2}


class Emit:
    def __init__(self, plan, block, first, second):
        self.plan, self.first, self.second = plan, first, second
        self.core, me = lax.axis_index("pipe"), lax.axis_index("dp")
        if plan.thin:
            return
        leading = self.core == 0
        places = [[plan.place(block, half, s, me) for s in range(plan.slabs)] for half in (0, 1)]
        self.places = [
            [jnp.where(leading, places[which][s], places[1 - which][s]) for s in range(plan.slabs)] for which in (0, 1)
        ]

    def halves(self, zero, one, put, first=0):
        leading = self.core == 0
        for which, value in ((0, jnp.where(leading, zero, one)), (1, jnp.where(leading, one, zero))):
            value = value.astype(BF)
            for s in range(value.shape[0]):
                put(which, self.places[which][first + s], value[s])

    def wide(self, zero, one, at):
        plan = self.plan
        if plan.thin:
            self.first[0][:, at : at + D] = zero.astype(BF)
            self.first[0][:, HALF + at : HALF + at + D] = one.astype(BF)
            return
        shape = (plan.slabs, plan.rows, D)

        def put(which, place, value):
            self.first[which][place, 0, :, at : at + D] = value

        self.halves(zero.reshape(shape), one.reshape(shape), put)

    def up(self, make):
        plan = self.plan
        if plan.thin:
            for lo in (0, HALF):
                self.second[0][:, lo : lo + HALF] = make(lo, HALF).astype(BF)
            return
        shape = (plan.slabs, plan.rows, HALF)

        def put(which, place, value):
            self.second[which][place, 0, :, :] = value

        self.halves(make(0, HALF).reshape(shape), make(HALF, HALF).reshape(shape), put)

    def down(self, make):
        plan = self.plan
        for lo in range(0, FF, HALF):
            value = make(lo, HALF)
            if plan.thin:
                self.second[1][lo : lo + HALF, :] = value.astype(BF)
                continue
            value = value.reshape(HALF // (4 * plan.rows), 2, 2 * plan.rows, D)

            def put(which, place, value, r=plan.rows):
                self.second[which][place, 1, :, 0:D] = value[:r]
                self.second[which][place, 1, :, D : 2 * D] = value[r:]

            self.halves(value[:, 0], value[:, 1], put, lo // (4 * plan.rows))


def limit(size):
    return pltpu.CompilerParams(vmem_limit_bytes=int(size) + 6 * 2**20)


def run_kernel(name, body, block, inputs, outs, scratch, cost, after=()):
    arrays = {n: v if isinstance(v, tuple) else (v, ()) for n, v in inputs.items()}
    size = sum(math.prod(shape) * jnp.dtype(dtype).itemsize for shape, dtype in scratch.values())

    def kernel(*refs):
        names = list(arrays) + [None] * len(after) + list(outs) + list(scratch)
        k = dict(zip(names, refs))
        core = lax.axis_index("pipe")
        for n, (_, index) in arrays.items():
            if index:
                k[n] = k[n].at[tuple(core if i == "core" else i for i in index)]
        gain = None
        if "gains" in arrays:
            gain = jnp.where(core == block, k["gains"][...], k["gains_got"][...])
        body(k, gain)

    result = pl.pallas_call(
        kernel,
        name=name,
        out_shape=[struct(*v) for v in outs.values()],
        in_specs=[VM] * len(arrays) + [ANY] * len(after),
        out_specs=[VM] * len(outs),
        scratch_shapes=[pltpu.VMEM(*v) for v in scratch.values()],
        compiler_params=limit(size),
        cost_estimate=pl.CostEstimate(flops=int(cost * 1e10), bytes_accessed=8, transcendentals=0),
    )(*[v for v, _ in arrays.values()], *after)
    return dict(zip(outs, result))


def small_kernel(name, kernel, outs, *inputs, after=()):
    def run(*refs):
        kernel(*refs[: len(inputs)], *refs[len(inputs) + len(after) :])

    return pl.pallas_call(
        run,
        name=name,
        out_shape=outs,
        in_specs=[VM] * len(inputs) + [ANY] * len(after),
        out_specs=[VM] * len(outs),
        compiler_params=limit(0),
    )(*inputs, *after)


def arrange(plan, flow, own, got, after):
    n, each = plan.slabs, plan.slabs // 2

    def kernel(a0, b0, a1, b1, zero, one):
        core, me = lax.axis_index("pipe"), lax.axis_index("dp")

        def move(first, second, dst, block):
            for place in range(n):
                src = first if place < each else second
                dst[plan.source(flow, block, place, me)] = src[place % each]

        @pl.when(core == 0)
        def _():
            move(a0, b0, zero, 0)
            move(a1, b1, one, 1)

        @pl.when(core != 0)
        def _():
            move(a0, b0, one, 1)
            move(a1, b1, zero, 0)

    like = struct((n, *own[0].shape[1:]), BF)
    out = small_kernel("arrange", kernel, [like, like], *own, *got, after=after)
    return [v.reshape(plan.weight_shape(flow)) for v in out]


def shapes(L):
    nb = bands(L)[1]
    return dict(
        n1=((L, D), BF),
        pk=((L, 3 * D), BF),
        pt=((PAIRS, nb, 2 * QB), BF),
        attT=((D, L), BF),
        mid=((L, D), F32),
        n2=((L, D), BF),
        act=((L, FF), BF),
        gp=((L, FF), BF),
        q2=((PAIRS, L // QB, 2 * QB, PAIR), BF),
        d2=((PAIRS, L // QB, 2 * QB, PAIR), BF),
        vT=((D, L), BF),
        bias=((nb, QB), F32),
        ss=((PAIRS, nb, 2 * QB), F32),
        ds=((PAIRS, nb, 2 * QB), BF),
        hs=((2, L, CHUNK), F32),
        dh=((L, FF), BF),
        dn=((L, D), F32),
        dmid=((L, D), F32),
        dmb=((L, D), BF),
        kT=((D, L), BF),
        dqT=((D, L), F32),
        dk=((L, D), F32),
        dv=((L, D), F32),
        dpk=((L, 3 * D), BF),
        da=((L, D), BF),
        x1=((L, D), F32),
        y2=((L, D), F32),
        dx=((L, D), F32),
        dxb=((L, D), BF),
        dg=((1, D), F32),
    )


def swap_cores(block):
    return lax.ppermute(block, "pipe", [(0, 1), (1, 0)])


def swap(block, bits):
    n = lax.axis_size("dp")
    route = [(c * n + i, c * n + (i ^ (1 << bits[c]))) for c in range(2) for i in range(n)]
    return lax.ppermute(block, ("pipe", "dp"), route)


def join(a, b, after):
    def kernel(a, b, out):
        n = a.shape[0]
        out[:n] = a[...]
        out[n:] = b[...]

    return small_kernel("join", kernel, [struct((2 * a.shape[0], *a.shape[1:]), a.dtype)], a, b, after=after)[0]


def gather(plan, shards, early):
    held = [shard[None] for shard in shards]
    last = ()
    for turn in range(plan.bits):
        came = [swap(held[f], (orders[0][turn], orders[1][turn])) for f, orders in enumerate(plan.gather_orders)]
        last = (*last, early) if turn == 1 else last
        if turn < plan.bits - 1:
            for f in range(3):
                held[f] = join(held[f], came[f], last)
                last = (held[f],)
    return [(a, b) for a, b in zip(held, came)]


def added(a, b):
    return (a.astype(F32) + b.astype(F32)).astype(BF)


def add_split(pairs, after=()):
    def kernel(*refs):
        outs, n, at = refs[-2:], refs[-1].shape[0], 0
        for k in range(0, len(refs) - 2, 2):
            a, b = refs[k : k + 2]
            wide = a.shape[1]
            for i, out in enumerate(outs):
                for j in range(n):
                    out[j, at : at + wide] = added(a[n * i + j], b[n * i + j])
            at += wide

    n, _, r, width = pairs[0][0].shape
    outs = [struct((n // 2, sum(a.shape[1] for a, _ in pairs), r, width), BF)] * 2
    return small_kernel("add_split", kernel, outs, *[v for pair in pairs for v in pair], after=after)


def behind(value, *others):
    return lax.optimization_barrier((value, *others))[0]


class Scatter:
    def __init__(self, plan, block):
        self.orders, self.turn, self.pairs = plan.scatter_orders[block], 0, []

    def exchange(self, pairs, turn, after):
        keep, send = add_split(pairs, after)
        return keep, swap(send, (self.orders[0][turn], self.orders[1][turn]))

    def begin(self, parts, *after):
        self.pairs = [self.exchange(parts, 0, after)]
        self.turn = 1
        return self.pairs[0][0]

    def part(self, mine, came, *after):
        self.pairs.append(self.exchange([(mine, came)], 0, after))
        self.turn = 1
        return self.pairs[-1][0]

    def step(self, *after):
        if self.turn == 1:
            self.pairs.reverse()
        self.pairs = [self.exchange(self.pairs, self.turn, after)]
        self.turn += 1
        return self.pairs[0][0]


def owners(zero, one):
    zero, one = ([pair for sums in v for pair in sums.pairs] for v in (zero, one))

    def total(refs):
        return jnp.concatenate([a[0].astype(F32) + b[0].astype(F32) for a, b in zip(refs[0::2], refs[1::2])], 0)

    def kernel(*refs):
        own, send = refs[-2:]
        a, b = total(refs[: 2 * len(zero)]), total(refs[2 * len(zero) : -2])
        leading = lax.axis_index("pipe") == 0
        own[...] = jnp.where(leading, a, b).astype(BF)
        send[...] = jnp.where(leading, b, a).astype(BF)

    like = struct((3, *zero[0][0].shape[2:]), BF)
    return small_kernel("owners", kernel, [like, like], *[v for pair in zero + one for v in pair])


def thin_arrange(plan, flow, own, got, after):
    core, me = lax.axis_index("pipe"), lax.axis_index("dp")
    index = jnp.arange(plan.count, dtype=jnp.int32)
    out = []
    for block in (0, 1):
        held = jnp.where(core == block, jnp.concatenate(own, 0), jnp.concatenate(got, 0))
        held = jnp.zeros_like(held).at[plan.source(flow, block, index, me)].set(held)
        out.append(held.reshape(plan.weight_shape(flow)))
    return out


def thin_halves(plan, block, grads, bundle):
    core, me = lax.axis_index("pipe"), lax.axis_index("dp")
    n, r = plan.count, D // plan.count
    parts = grads[0].reshape(n, r, 2, HALF).transpose(2, 0, 1, 3)
    parts = parts[:, :, None]
    if bundle:
        down = grads[1].reshape(n, 2, 2, r, D).transpose(1, 0, 3, 2, 4).reshape(2, n, 1, r, HALF)
        parts = jnp.concatenate([parts, down], 2)
    index = jnp.arange(n, dtype=jnp.int32)
    halves = [jnp.zeros_like(parts[h]).at[plan.place(block, h, index, me)].set(parts[h]) for h in (0, 1)]
    return [jnp.where(core == 0, halves[i], halves[1 - i]) for i in (0, 1)]


def lanes(values):
    lane = lax.broadcasted_iota(jnp.int32, (1, D), 1)
    row = jnp.zeros((1, D), F32)
    for place, value in values:
        row = row + jnp.where(lane == place, value, 0.0)
    return row


def square_sum(v):
    return jnp.sum(jnp.sum(v * v, axis=1, keepdims=True), axis=0, keepdims=True)


def moments(master, grad, first, second):
    drift = beta * first + (1.0 - beta) * grad
    spread = beta * second + (1.0 - beta) * grad * grad
    correction = 1.0 - beta**STEP
    update = drift / correction / (jnp.sqrt(spread / correction) + eps_adam) + decay * master
    return (drift, spread, update)


def update_moments(plan, own, got, masters, firsts, seconds, gain_own, gain_got):
    r = D // plan.count

    def kernel(own, got, *refs):
        masters, firsts, seconds, (gain_own, gain_got) = refs[0:4], refs[4:8], refs[8:12], refs[12:14]
        drifts, spreads, updates, small = refs[14:18], refs[18:22], refs[22:26], refs[26]
        leading = lax.axis_index("pipe") == 0
        a, b = own[...].astype(F32), got[...].astype(F32)
        h = (jnp.where(leading, a, b), jnp.where(leading, b, a))
        whole, tail = slice(None), 3 * D - HALF
        grads = [
            [((whole, slice(0, HALF)), h[0][0]), ((whole, slice(HALF, 3 * D)), h[1][0][:, :tail])],
            [((whole, slice(0, D)), h[1][0][:, tail:])],
            [((whole, slice(HALF * i, HALF * i + HALF)), h[i][1]) for i in (0, 1)],
            [
                ((slice(r * (2 * i + q), r * (2 * i + q) + r), whole), h[i][2][:, D * q : D * q + D])
                for i in (0, 1)
                for q in (0, 1)
            ],
        ]
        sums = [(m, square_sum(masters[m][...])) for m in range(4)]
        for m in range(4):
            total = jnp.zeros((1, 1), F32)
            for at, grad in grads[m]:
                drift, spread, update = moments(masters[m][at], grad, firsts[m][at], seconds[m][at])
                drifts[m][at], spreads[m][at], updates[m][at] = drift, spread, update
                total = total + square_sum(update)
            sums.append((4 + m, total))
        row = lanes(sums)
        gain = gain_own[...] + gain_got[...]
        for i in range(plan.count):
            small[i, 0:1, :] = row
            small[i, 1:3, :] = gain

    like = [struct(m.shape, F32) for m in masters]
    outs = like * 3 + [struct((plan.count, 3, D), F32)]
    res = small_kernel("moments", kernel, outs, own, got, *masters, *firsts, *seconds, gain_own, gain_got)
    return res[0:4], res[4:8], res[8:12], res[12]


def finish(small, masters, updates, gains, gain_first, gain_second):
    def kernel(parts, m0, m1, m2, m3, u0, u1, u2, u3, gains, gf, gs, *outs):
        new, low, (gain_drift, gain_spread, gain_new, pairs) = outs[0:4], outs[4:8], outs[8:12]
        small = jnp.sum(parts[...], axis=0)
        weight = [jnp.sqrt(small[0:1, i : i + 1]) for i in range(4)]
        step = [jnp.sqrt(small[0:1, 4 + i : 5 + i]) for i in range(4)]
        for i, (m, u) in enumerate(zip((m0, m1, m2, m3), (u0, u1, u2, u3))):
            value = m[...] - rate * (weight[i] / step[i]) * u[...]
            new[i][...] = value
            low[i][...] = value.astype(BF)
        drift, spread, update = moments(gains[...], small[1:3, :], gf[...], gs[...])
        gain_drift[...] = drift
        gain_spread[...] = spread
        gain_weight = jnp.sqrt(jnp.sum(gains[...] * gains[...], axis=1, keepdims=True))
        gain_step = jnp.sqrt(jnp.sum(update * update, axis=1, keepdims=True))
        gain_new[...] = gains[...] - rate * (gain_weight / gain_step) * update
        for i in range(4):
            pairs[0:1, i : i + 1] = weight[i]
            pairs[1:2, i : i + 1] = step[i]
        for i in range(2):
            pairs[0:1, 4 + i : 5 + i] = gain_weight[i : i + 1, :]
            pairs[1:2, 4 + i : 5 + i] = gain_step[i : i + 1, :]

    outs = [struct(m.shape, F32) for m in masters] + [struct(m.shape, BF) for m in masters]
    outs += [struct((2, D), F32)] * 3 + [struct((2, 6), F32)]
    res = small_kernel("finish", kernel, outs, small, *masters, *updates, gains, gain_first, gain_second)
    return [*res[:-1], res[-1].T]


def lay_results(own, got):
    def kernel(own, got, out, done):
        core = lax.axis_index("pipe")
        out[core] = own[...]
        out[1 - core] = got[...]
        done[...] = jnp.zeros(done.shape, F32)

    return small_kernel("lay_results", kernel, [struct((2, *own.shape), F32), struct((8, 128), F32)], own, got)


def solution(mesh):
    plan = Plan(mesh)

    def per_device(
        tokens,
        prompts,
        cotangent,
        segments,
        weight_in,
        weight_out,
        weight_up,
        weight_down,
        first_in,
        first_out,
        first_up,
        first_down,
        second_in,
        second_out,
        second_up,
        second_down,
        gains,
        gain_first,
        gain_second,
    ):
        L = tokens.shape[2]
        sh = shapes(L)
        masters = (weight_in[0], weight_out[0], weight_up[0], weight_down[0])
        firsts = (first_in[0], first_out[0], first_up[0], first_down[0])
        seconds = (second_in[0], second_out[0], second_up[0], second_down[0])

        low = [m.astype(BF) for m in masters]
        wide = jnp.concatenate(low[:2], 1)
        gains_got = swap_cores(gains[0])
        flows = gather(plan, (wide, low[2], low[3].reshape(4, -1, D)), gains_got)
        put = thin_arrange if plan.thin else arrange
        both = [None] * 3

        def place_flow(flow, *after):
            both[flow] = put(plan, flow, flows[flow], tuple(swap_cores(v) for v in flows[flow]), after)

        place_flow(0)

        def weights(block, *which):
            return {n: both[f][block] for f, n in enumerate(("wide", "up", "down")) if n in which}

        def pick(*names):
            return {n: sh[n] for n in names}

        def there(source, *names):
            return {n: source[n] for n in names}

        gain_refs = {"gains": gains[0], "gains_got": gains_got}
        grads = plan.grad_shapes()
        g_first = {f"p{i}": v for i, v in enumerate(grads["gp_"])}
        g_second = {f"q{i}": v for i, v in enumerate(grads["gq_"])}
        x0 = {"x": (tokens, ("core", 0))}
        seg = {"seg": (segments[:, :, None], ("core", 0))}

        def refs_of(k, table):
            return [k[n] for n in table]

        def traded(source, table, block, bundle):
            values = [source[n] for n in table]
            if plan.thin:
                values = thin_halves(plan, block, values, bundle)
            return values[0], swap_cores(values[1])

        def body(k, gain):
            attention_half(k["x"], k, k["wide"], gain, L)

        attention_scratch = pick("q2", "vT", "bias", "ss")
        one = run_kernel(
            "extractor_attention", body, 0, {**gain_refs, **x0, **seg, "pr": (prompts, ("core", 0)), **weights(0, "wide")},
            pick("n1", "pk", "pt", "attT", "mid", "n2"), attention_scratch, 1e-9,
        )

        place_flow(1, one["n2"])
        place_flow(2, one["n2"])

        def body(k, gain):
            def out(value):
                k["x1"][...] = value.astype(BF).astype(F32) + k["pr"][...].astype(F32)

            feed_forward(k, k["up"], k["down"], L, out)

        two = run_kernel(
            "extractor_feed", body, 0,
            {**there(one, "n2", "mid"), "pr": (prompts, ("core", 0)), **weights(0, "up", "down")},
            pick("act", "gp", "x1"), pick("hs"), 3.2,
        )

        def body(k, gain):
            attention_half(k["x1"], k, k["wide"], gain, L)

        three = run_kernel(
            "generator_attention", body, 1, {**gain_refs, **there(two, "x1"), **seg, **weights(1, "wide")},
            pick("n1", "pk", "pt", "attT", "mid", "n2"), attention_scratch, 1e-9,
        )

        def body(k, gain):
            def out(value):
                k["y2"][...] = value

            feed_forward(k, k["up"], k["down"], L, out)
            emit = Emit(plan, 1, None, refs_of(k, g_second))
            k["dg"][...] = feed_back(k["dy"], k, k["up"], k["down"], gain, emit)

        cot = {"dy": (cotangent, ("core", 0))}
        four = run_kernel(
            "generator_feed", body, 1,
            {**gain_refs, **there(three, "mid", "n2"), **cot, **weights(1, "up", "down")},
            {**pick("y2", "dmid", "dmb", "dg"), **g_second}, pick("act", "gp", "hs", "dh", "dn"), 10,
        )

        second_one = traded(four, g_second, 1, 1)
        back_scratch = pick("q2", "d2", "kT", "ss", "ds", "dqT", "dk", "dv", "da")

        def body(k, gain):
            emit = Emit(plan, 1, refs_of(k, g_first), None)
            attention_back(k, k["wide"], emit, L)

        five = run_kernel(
            "generator_attention_back", body, 1,
            {**there(four, "dmb"), **there(three, "attT", "pk", "pt", "n1"), **weights(1, "wide")},
            {**g_first, **pick("dpk")}, back_scratch, 6,
        )
        sum_one = Scatter(plan, 1)
        first_one = traded(five, g_first, 1, 0)

        def body(k, gain):
            k["dg"][...] = input_back(k["x1"], k, k["wide"], gain, None, k["dxb"])

        six = run_kernel(
            "generator_input_back", body, 1,
            {**gain_refs, **there(five, "dpk"), **there(four, "dmid"), **there(two, "x1"), **weights(1, "wide")},
            pick("dg", "dxb"), pick("dn"), 3,
        )
        last = sum_one.begin([first_one, second_one], six["dxb"])

        def body(k, gain):
            emit = Emit(plan, 0, None, refs_of(k, g_second))
            k["dg"][...] = feed_back(k["dxb"], k, k["up"], k["down"], gain, emit)

        seven = run_kernel(
            "extractor_feed_back", body, 0,
            {**gain_refs, **there(six, "dxb"), **there(two, "act", "gp"), **there(one, "n2", "mid"), **weights(0, "up", "down")},
            {**g_second, **pick("dmid", "dmb", "dg")}, pick("dh", "dn"), 7, after=[last],
        )
        second_zero = traded(seven, g_second, 0, 1)

        def body(k, gain):
            emit = Emit(plan, 0, refs_of(k, g_first), None)
            attention_back(k, k["wide"], emit, L)

        eight = run_kernel(
            "extractor_attention_back", body, 0,
            {**there(seven, "dmb"), **there(one, "attT", "pk", "pt", "n1"), **weights(0, "wide")},
            {**g_first, **pick("dpk")}, back_scratch, 6,
        )
        first_zero = traded(eight, g_first, 0, 0)
        sum_zero = Scatter(plan, 0)
        last = sum_zero.begin([first_zero, second_zero], eight["dpk"])
        last = sum_one.step(last)

        def body(k, gain):
            dg = input_back(k["x"], k, k["wide"], gain, k["dx"], None)
            leading = lax.axis_index("pipe") == 0
            k["own"][...] = jnp.where(leading, k["dx"][...], k["y2"][...])
            k["send"][...] = jnp.where(leading, k["y2"][...], k["dx"][...])
            for i, (zero, one) in enumerate(((dg, k["g10"][...]), (k["g01"][...], k["g11"][...]))):
                k["gain_own"][i : i + 1, :] = jnp.where(leading, zero, one)
                k["gain_send"][i : i + 1, :] = jnp.where(leading, one, zero)

        nine = run_kernel(
            "extractor_input_back", body, 0,
            {**gain_refs, **there(eight, "dpk"), **there(seven, "dmid"), **x0, **weights(0, "wide"), **there(four, "y2"),
             "g01": seven["dg"], "g10": six["dg"], "g11": four["dg"]},
            {"own": sh["dx"], "send": sh["dx"], "gain_own": ((2, D), F32), "gain_send": ((2, D), F32)},
            pick("dn", "dx"), 3, after=[last],
        )
        gain_got = swap_cores(nine["gain_send"])
        result, laid = lay_results(nine["own"], swap_cores(nine["send"]))
        section_result = result[None, :, None]
        last = sum_zero.step(nine["gain_own"], gain_got)
        last = sum_one.step(last)
        last = sum_zero.step(last, laid)
        while min(sum_one.turn, sum_zero.turn) < plan.bits:
            for sums in (sum_one, sum_zero):
                if sums.turn < plan.bits:
                    last = sums.step(last)
        own, send = owners((sum_zero,), (sum_one,))
        grad_got = swap_cores(send)

        drifts, spreads, updates, small = update_moments(
            plan, own, grad_got, masters, firsts, seconds, nine["gain_own"], gain_got
        )
        small = lax.all_to_all(small, "dp", 0, 0)
        done = finish(small, masters, updates, gains[0], gain_first[0], gain_second[0])
        return (
            section_result,
            *[v[None] for v in (*drifts, *spreads)],
            *[v[None] for v in done],
        )

    rows = P(None, "dp", None, None)
    matrix = P("pipe", "dp", None)
    gain = P("pipe", None, None)
    in_specs = (rows, rows, rows, P(None, "dp", None)) + (matrix,) * 12 + (gain,) * 3
    out_specs = (P("pipe", None, "dp", None, None),) + (matrix,) * 16 + (gain,) * 4
    return jax.shard_map(
        per_device, mesh=mesh, in_specs=in_specs, out_specs=out_specs, check_vma=False
    )
```
